32 devices in a mesh: groups: 2 (over y), ctx: 4 (over z), exp: 2 (over x), tp: 2 (over core).
Axes of the slice: x: 2, y: 2, z: 4, core: 2. Of those that a mesh axis runs over, the one named last changes fastest.
Arguments:
- resid: bfloat16 [512, 4096], P(('groups', 'ctx')), parts along dimension 0, may hold values from -40 to 40
- conv_out: bfloat16 [512, 4096], P(('groups', 'ctx'), ('exp', 'tp')), parts along dimension 0, may hold values from -6 to 6
- gate_z: bfloat16 [512, 4096], P(('groups', 'ctx'), ('exp', 'tp')), parts along dimension 0, may hold values from -6 to 6
- dt_raw: float32 [512, 4096], P(('groups', 'ctx'), ('exp', 'tp')), parts along dimension 0, may hold values from -14 to 2
- b_proj: float32 [512, 16], P(('groups', 'ctx')), parts along dimension 0, may hold values from -6 to 6
- c_proj: float32 [512, 16], P(('groups', 'ctx')), parts along dimension 0, may hold values from -6 to 6
- a_log: float32 [16, 4096], P(None, ('exp', 'tp')), may hold values from -0.7 to 0.7
- d_skip: float32 [4096], P(('exp', 'tp')), may hold values from 0.5 to 1.5
- out_weight: bfloat16 [4096, 4096], P(('exp', 'tp'), 'ctx'), may hold values from -0.09375 to 0.09375
- norm_gain: float32 [4096], replicated, may hold values from 0.1 to 1.9
- route_ids: int32 [512, 2], P(('groups', 'ctx')), parts along dimension 0, may hold values from 0 to 3, as said below
- route_weight: float32 [512, 2], P(('groups', 'ctx')), parts along dimension 0, may hold values from 0.2 to 1
- w_gate: bfloat16 [4096, 32768], P('tp', ('ctx', 'exp')), may hold values from -0.09375 to 0.09375
- w_up: bfloat16 [4096, 32768], P('tp', ('ctx', 'exp')), may hold values from -0.09375 to 0.09375
- w_down: bfloat16 [32768, 4096], P(('ctx', 'exp'), 'tp'), may hold values from -0.0625 to 0.0625
Outputs:
- layer_out: bfloat16 [512, 4096], P(('groups', 'ctx'), ('tp', 'exp')), parts along dimension 0
The draws below stay inside these ranges and needn't reach their ends.
There are 2 independent parts, one for each index of `groups`. The reference program is written for one: setup_inputs(seed, part) draws one part's arguments, and reference() takes and returns one part's arrays. A program takes and returns all parts, laid end to end along the dimension named above; an argument that names none is the same for every part. Nothing has to cross between parts.
Inputs may be any that keep to these rules, and one draw needn't show every extreme that they name: `route_ids`: each row names two different experts. Among the 64 rows of one block (rows b * 64 to (b + 1) * 64 - 1), no expert is named by more than 40 rows, and one expert, the same in every block of a part, is named by exactly 40 rows of every block.
All inputs are finite; a program needn't handle non-finite values.
Results may differ from the reference program's by a relative error of at most 0.01.
Values may be sent and summed in bfloat16 or wider, within the bound.
No kernel may reach another device: no remote copies, remote signals or barrier semaphores. Data moves between devices by JAX's collectives and lax.ppermute only.
A program may use at most 128 MiB of HBM per device.

```python
import math
import jax
import jax.numpy as jnp
from jax import lax

D = 4096
STATE = 16
INNER = 4096
FF = 8192
EXPERTS = 4
TOK = 64
CAP = 40
PROMPT_WORDS = 256
N_CTX = 4
N_EXP = 2


def draw_resid(key, part):
    key = jax.random.fold_in(key, 7)
    sampler_seeds = jax.random.split(key, 3)
    starting_index = jax.random.normal(sampler_seeds[0], (PROMPT_WORDS, D), jnp.float32)
    row_scale = jnp.exp(jax.random.uniform(sampler_seeds[1], (PROMPT_WORDS, 1), jnp.float32, math.log(0.3), math.log(3.0)))
    col_scale = jnp.exp(jax.random.uniform(sampler_seeds[2], (1, D), jnp.float32, math.log(0.3), math.log(3.0)))
    return jnp.clip(starting_index * row_scale * col_scale, -40.0, 40.0).astype(jnp.bfloat16)


def draw_dt_raw(key, part):
    key = jax.random.fold_in(key, 5)
    sampler_seeds = jax.random.split(key, 5)
    slow_share = 0.5
    slow = jax.random.uniform(sampler_seeds[0], (1, INNER), jnp.float32) < slow_share
    starting_index = jnp.where(slow, 0.8 / PROMPT_WORDS, 0.06)
    feature_lane = jnp.exp(jax.random.uniform(sampler_seeds[1], (1, INNER), jnp.float32, -0.7, 0.7))
    tile_extent = jnp.exp(jax.random.uniform(sampler_seeds[2], (PROMPT_WORDS // TOK, 1, INNER), jnp.float32, -0.4, 0.4))
    tile_extent = jnp.broadcast_to(tile_extent, (PROMPT_WORDS // TOK, TOK, INNER)).reshape(PROMPT_WORDS, INNER)
    approximate_guess = jnp.exp(jax.random.uniform(sampler_seeds[3], (PROMPT_WORDS, INNER), jnp.float32, -0.4, 0.4))
    transfer_cursor = jax.random.randint(sampler_seeds[4], (3,), 0, PROMPT_WORDS)
    transfer_batch = jnp.any(jnp.arange(PROMPT_WORDS)[:, None] == transfer_cursor[None, :], axis=1).astype(jnp.float32)[:, None]
    stride_amount = starting_index * feature_lane * tile_extent * approximate_guess + 0.5 * transfer_batch
    return jnp.log(jnp.expm1(stride_amount))


def draw_route_ids(key, part):
    key = jax.random.fold_in(key, 11)
    hot_key, block_key = jax.random.split(key)
    hot = jax.random.randint(hot_key, (), 0, EXPERTS)
    spare = 2 * CAP - TOK
    others = EXPERTS - 1

    def one_block(block_seed):
        sampler_seeds = jax.random.split(block_seed, 5)
        order = jax.random.permutation(sampler_seeds[0], TOK)
        remaining = jnp.int32(CAP)
        running = jnp.int32(0)
        bounds = []
        for index in range(others):
            lowest = jnp.maximum(0, remaining - spare * (others - 1 - index))
            highest = jnp.minimum(spare, remaining)
            amount = jax.random.randint(jax.random.fold_in(sampler_seeds[1], index), (), lowest, highest + 1)
            running = running + amount
            bounds.append(running)
            remaining = remaining - amount
        slot_index = jnp.arange(CAP)
        which = jnp.zeros((CAP,), jnp.int32)
        for bound in bounds[:-1]:
            which = which + (slot_index >= bound).astype(jnp.int32)
        which = jax.random.permutation(sampler_seeds[2], which)
        second = (hot + 1 + which) % EXPERTS
        flip = jax.random.randint(sampler_seeds[3], (CAP,), 0, 2)
        hot_first = jnp.where(flip == 1, hot, second)
        hot_second = jnp.where(flip == 1, second, hot)
        begin_other = jax.random.randint(sampler_seeds[4], (TOK - CAP,), 0, others)
        cold_first = (hot + 1 + begin_other) % EXPERTS
        cold_second = (hot + 1 + (begin_other + 1) % others) % EXPERTS
        ranked = jnp.stack([jnp.concatenate([hot_first, cold_first]), jnp.concatenate([hot_second, cold_second])], axis=1)
        inverse = jnp.argsort(order, stable=True)
        return ranked[inverse]
    blocks = jax.vmap(one_block)(jax.random.split(block_key, PROMPT_WORDS // TOK))
    return blocks.reshape(PROMPT_WORDS, 2).astype(jnp.int32)


def levels(stream_key, dims, pieces, smallest, top_value):
    def one(axis_at, parts):
        heights = jax.random.uniform(jax.random.fold_in(jax.random.fold_in(stream_key, 6), axis_at), (parts,), jnp.float32, smallest / len(pieces), top_value / len(pieces))
        return jnp.repeat(jnp.exp(heights), dims[axis_at] // parts).reshape((-1,) + (1,) * (len(dims) - axis_at - 1))

    loudness = one(*pieces[0])
    for cut in pieces[1:]:
        loudness = loudness * one(*cut)
    return loudness


def bell_draw(own_key, extent, deviation, most, cuts=(), kind=jnp.bfloat16):
    result = deviation * jax.random.normal(own_key, extent, jnp.float32)
    if cuts:
        result = result * levels(own_key, extent, cuts, -0.22, 0.18)
    return jnp.clip(result, -most, most).astype(kind)


def setup_inputs(seed: int = 0, part: int = 0) -> dict:
    seeds = jax.random.split(jax.random.key(seed), 16)
    part_splits = jax.random.split(jax.random.fold_in(seeds[15], part), 16)
    return {
        "resid": draw_resid(jax.random.fold_in(jax.random.fold_in(seeds[15], part), 71), part),
        "conv_out": bell_draw(part_splits[1], (PROMPT_WORDS, INNER), 1.0, 6.0, ((0, 4), (1, 4))),
        "gate_z": bell_draw(part_splits[2], (PROMPT_WORDS, INNER), 1.0, 6.0, ((0, 4), (1, 4))),
        "dt_raw": draw_dt_raw(jax.random.fold_in(jax.random.fold_in(seeds[15], part), 71), part),
        "b_proj": bell_draw(part_splits[4], (PROMPT_WORDS, STATE), 1.0, 6.0, ((0, 4),), jnp.float32),
        "c_proj": bell_draw(part_splits[5], (PROMPT_WORDS, STATE), 1.0, 6.0, ((0, 4),), jnp.float32),
        "a_log": jnp.clip(jax.random.uniform(seeds[6], (STATE, INNER), jnp.float32, -0.7, 0.7) * levels(seeds[6], (STATE, INNER), ((1, 4),), -0.4, 0.0), -0.7, 0.7),
        "d_skip": jnp.clip(0.5 + 1.0 * jax.random.uniform(seeds[7], (INNER,), jnp.float32) ** levels(seeds[7], (INNER,), ((0, 4),), -0.2, 0.2), 0.5, 1.5),
        "out_weight": bell_draw(seeds[8], (INNER, D), INNER ** -0.5, 0.09375, ((0, 4), (1, 4))),
        "norm_gain": jnp.clip(1.0 + 0.18 * jax.random.normal(seeds[9], (D,), jnp.float32), 0.1, 1.9),
        "route_ids": draw_route_ids(jax.random.fold_in(jax.random.fold_in(seeds[15], part), 71), part),
        "route_weight": jnp.clip(0.2 + 0.8 * jax.random.uniform(part_splits[11], (PROMPT_WORDS, 2), jnp.float32) ** levels(part_splits[11], (PROMPT_WORDS, 2), ((0, 4),), -0.2, 0.2), 0.2, 1.0),
        "w_gate": bell_draw(seeds[12], (D, EXPERTS * FF), D ** -0.5, 0.09375, ((0, 2), (1, 8))),
        "w_up": bell_draw(seeds[13], (D, EXPERTS * FF), D ** -0.5, 0.09375, ((0, 2), (1, 8))),
        "w_down": bell_draw(seeds[14], (EXPERTS * FF, D), FF ** -0.5, 0.0625, ((0, 8), (1, 2))),
    }


def mamba_gated(conv_out, gate_z, dt_raw, b_proj, c_proj, a_log, d_skip):
    stride_amount = jax.nn.softplus(dt_raw)
    rate = -jnp.exp(a_log)
    inputs = conv_out.astype(jnp.float32)

    def advance(carry_state, column):
        step_now, b_now, c_now, in_now = column
        carry_state = jnp.exp(step_now[None, :] * rate) * carry_state + step_now[None, :] * b_now[:, None] * in_now[None, :]
        return (carry_state, lax.optimization_barrier(jnp.sum(c_now[:, None] * carry_state, axis=0)))
    start_state = jnp.zeros(a_log.shape, jnp.float32)
    _, scanned = lax.scan(advance, start_state, (stride_amount, b_proj, c_proj, inputs))
    mixed = scanned + d_skip[None, :] * inputs
    return (mixed * jax.nn.silu(gate_z.astype(jnp.float32))).astype(jnp.bfloat16)

def reference(resid, conv_out, gate_z, dt_raw, b_proj, c_proj, a_log, d_skip, out_weight, norm_gain, route_ids, route_weight, w_gate, w_up, w_down):
    gated_out = mamba_gated(conv_out, gate_z, dt_raw, b_proj, c_proj, a_log, d_skip)
    mamba_out = jnp.dot(gated_out, out_weight, preferred_element_type=jnp.float32)
    stream = (resid.astype(jnp.float32) + mamba_out).astype(jnp.bfloat16)
    stream_wide = stream.astype(jnp.float32)
    square_mean = lax.optimization_barrier(jnp.mean(stream_wide * stream_wide, axis=1, keepdims=True))
    normed = (stream_wide * lax.rsqrt(square_mean + 1e-06) * norm_gain[None, :]).astype(jnp.bfloat16)
    block_count = N_CTX // EXPERTS * N_EXP
    block_width = FF // block_count
    capacity = N_CTX * CAP
    flat_ids = route_ids.reshape(-1)
    flat_weight = route_weight.reshape(-1)
    owner_rows = (jnp.arange(2 * PROMPT_WORDS, dtype=jnp.int32) // 2).astype(jnp.int32)

    def one_expert(moe_total, expert):
        chosen = flat_ids == expert
        chosen_count = jnp.sum(chosen.astype(jnp.int32))
        picked = jnp.nonzero(chosen, size=capacity, fill_value=0)[0].astype(jnp.int32)
        filled = jnp.arange(capacity, dtype=jnp.int32) < chosen_count
        token_rows = owner_rows[picked]
        features = normed[token_rows]
        gate_cols = lax.dynamic_slice_in_dim(w_gate, (expert * FF).astype(jnp.int32), FF, 1)
        up_cols = lax.dynamic_slice_in_dim(w_up, (expert * FF).astype(jnp.int32), FF, 1)
        down_rows = lax.dynamic_slice_in_dim(w_down, (expert * FF).astype(jnp.int32), FF, 0)
        gate_value = jnp.dot(features, gate_cols, preferred_element_type=jnp.float32)
        up_value = jnp.dot(features, up_cols, preferred_element_type=jnp.float32)
        hidden = (jax.nn.silu(gate_value) * up_value).astype(jnp.bfloat16)

        def add_block(partial_value, block_index):
            begin_unit = (block_index * block_width).astype(jnp.int32)
            hidden_block = lax.dynamic_slice_in_dim(hidden, begin_unit, block_width, 1)
            weight_block = lax.dynamic_slice_in_dim(down_rows, begin_unit, block_width, 0)
            rounded = jnp.dot(hidden_block, weight_block, preferred_element_type=jnp.float32).astype(jnp.bfloat16)
            rounded = lax.optimization_barrier(rounded)
            return (partial_value + rounded.astype(jnp.float32), None)
        zero_out = jnp.zeros((capacity, resid.shape[1]), jnp.float32)
        expert_out, _ = lax.scan(add_block, zero_out, jnp.arange(block_count, dtype=jnp.int32))
        pair_scale = jnp.where(filled, flat_weight[picked], jnp.zeros((capacity,), jnp.float32))
        return (moe_total.at[token_rows].add(pair_scale[:, None] * expert_out), None)
    moe_out, _ = lax.scan(one_expert, jnp.zeros(resid.shape, jnp.float32), jnp.arange(EXPERTS, dtype=jnp.int32))
    return (stream_wide + moe_out).astype(jnp.bfloat16)
```

```python
import jax
import jax.numpy as jnp
from jax import lax
from jax.experimental import pallas as pl
from jax.experimental.pallas import tpu as pltpu
from jax.sharding import PartitionSpec as P

EXPERTS = 4
CAP = 40


def shifted(x, axis, by):
    peers = lax.axis_size(axis)
    pairs = [(i, i + by) for i in range(peers) if 0 <= i + by < peers]
    return lax.ppermute(x, axis, pairs)


def body(
    resid,
    conv_out,
    gate_z,
    dt_raw,
    b_proj,
    c_proj,
    a_log,
    d_skip,
    out_weight,
    norm_gain,
    route_ids,
    route_weight,
    w_gate,
    w_up,
    w_down,
):
    tokens = resid.shape[0]
    model_width = resid.shape[1]
    ctx_count = lax.axis_size("ctx")
    exp_count = lax.axis_size("exp")
    tp_count = lax.axis_size("tp")
    half_width = model_width // tp_count
    piece_width = half_width // exp_count
    tp_index = lax.axis_index("tp")
    exp_index = lax.axis_index("exp")
    stride_amount = jax.nn.softplus(dt_raw)
    rate = -jnp.exp(a_log)
    inputs = conv_out.astype(jnp.float32)

    def advance(carry_state, column):
        step_now, b_now, c_now, in_now = column
        carry_state = (
            jnp.exp(step_now[None, :] * rate) * carry_state
            + step_now[None, :] * b_now[:, None] * in_now[None, :]
        )
        return (carry_state, jnp.sum(c_now[:, None] * carry_state, axis=0))

    last_state, scanned_local = lax.scan(
        advance,
        jnp.zeros(rate.shape, jnp.float32),
        (stride_amount, b_proj, c_proj, inputs),
        unroll=8,
    )
    cum_step = jnp.cumsum(stride_amount, axis=0)
    last_decay = jnp.exp(cum_step[-1][None, :] * rate)

    def relay_turn(turn_index, carry_state):
        return shifted(last_decay * carry_state + last_state, "ctx", 1)

    entering = lax.fori_loop(0, ctx_count - 1, relay_turn, jnp.zeros_like(last_state))
    carried = jnp.exp(cum_step[:, None, :] * rate[None, :, :])
    scanned = scanned_local + jnp.sum(c_proj[:, :, None] * carried * entering[None, :, :], axis=1)
    gated_out = (
        (scanned + d_skip[None, :] * inputs) * jax.nn.silu(gate_z.astype(jnp.float32))
    ).astype(jnp.bfloat16)
    partial_value = jnp.dot(
        gated_out,
        lax.all_gather(out_weight, "ctx", axis=1, tiled=True),
        preferred_element_type=jnp.float32,
    )
    mamba_out = lax.psum(partial_value, ("exp", "tp"))
    stream = (resid.astype(jnp.float32) + mamba_out).astype(jnp.bfloat16)
    stream_wide = stream.astype(jnp.float32)
    square_mean = jnp.mean(stream_wide * stream_wide, axis=1, keepdims=True)
    normed = (stream_wide * lax.rsqrt(square_mean + 1e-06) * norm_gain[None, :]).astype(
        jnp.bfloat16
    )
    half_feats = lax.dynamic_slice_in_dim(normed, tp_index * half_width, half_width, 1)
    slot_total = EXPERTS * CAP
    flat_ids = route_ids.reshape(-1)
    pair_count = flat_ids.shape[0]
    onehot = (flat_ids[:, None] == jnp.arange(EXPERTS, dtype=jnp.int32)[None, :]).astype(
        jnp.float32
    )
    pair_index = jnp.arange(pair_count, dtype=jnp.int32)
    earlier_mask = (pair_index[:, None] > pair_index[None, :]).astype(jnp.float32)
    before = jnp.dot(earlier_mask, onehot, precision=lax.Precision.HIGHEST)
    position = jnp.sum(before * onehot, axis=1).astype(jnp.int32)
    target = (flat_ids * CAP + position).reshape(tokens, 2)
    matches = jnp.arange(slot_total, dtype=jnp.int32)[None, :, None] == target[:, None, :]
    placement = jnp.any(matches, axis=2).astype(jnp.bfloat16)
    combine_weights = jnp.sum(jnp.where(matches, route_weight[:, None, :], 0.0), axis=2)
    members = ctx_count // EXPERTS
    outgoing = lax.dot_general(
        placement, half_feats, (((0,), (0,)), ((), ())), preferred_element_type=jnp.float32
    )
    outgoing = jnp.repeat(
        outgoing.astype(jnp.bfloat16).reshape(EXPERTS, CAP, half_width), members, axis=0
    )
    arrived = lax.all_to_all(outgoing, "ctx", split_axis=0, concat_axis=0, tiled=True)
    sources = arrived.shape[0]
    item_count = arrived.shape[1]
    flat_rows = arrived.reshape(sources * item_count, half_width)
    gate_value = jnp.dot(flat_rows, w_gate, preferred_element_type=jnp.float32)
    up_value = jnp.dot(flat_rows, w_up, preferred_element_type=jnp.float32)
    gate_value, up_value = (
        lax.psum(gate_value.astype(jnp.bfloat16), "tp").astype(jnp.float32),
        lax.psum(up_value.astype(jnp.bfloat16), "tp").astype(jnp.float32),
    )
    hidden = (jax.nn.silu(gate_value) * up_value).astype(jnp.bfloat16)
    answer = jnp.dot(hidden, w_down, preferred_element_type=jnp.float32).astype(jnp.bfloat16)
    answer = answer.reshape(sources, item_count, half_width)
    returned = lax.all_to_all(answer, "ctx", split_axis=0, concat_axis=0, tiled=True)
    reply_width = returned.shape[2]
    merged = jnp.sum(
        returned.astype(jnp.float32).reshape(EXPERTS, members, CAP, reply_width), axis=1
    )
    merged = merged.reshape(slot_total, reply_width)
    moe_rows = jnp.dot(combine_weights, merged, precision=lax.Precision.HIGHEST)
    moe_piece = lax.psum_scatter(
        moe_rows.astype(jnp.bfloat16), "exp", scatter_dimension=1, tiled=True
    ).astype(jnp.float32)
    own_stream = lax.dynamic_slice_in_dim(
        stream_wide, tp_index * half_width + exp_index * piece_width, piece_width, 1
    )
    return (own_stream + moe_piece).astype(jnp.bfloat16)


LOG2E = 1.4426950408889634
AXES = ("ctx", "exp", "tp")
f32 = jnp.float32
bf16 = jnp.bfloat16


def lanes_to_rows(store_ref, value):
    rows, width = value.shape
    count = width // 128
    for k in range(count):
        store_ref[pl.ds(k, rows, stride=count), :] = value[:, k * 128 : (k + 1) * 128]


def scan_kernel(
    b_ref, c_ref, dt_ref, conv_ref, z_ref, alog_ref, skip_ref,
    base_ref, cum_ref, silu_ref, rate_ref, pack_ref, step_s, in_s, z_s, alog_s,
):
    tokens, width = dt_ref.shape
    states = alog_ref.shape[0]
    g = width // 128
    lanes_to_rows(step_s, jax.nn.softplus(dt_ref[...]))
    lanes_to_rows(in_s, conv_ref[...].astype(f32))
    lanes_to_rows(z_s, z_ref[...].astype(f32))
    lanes_to_rows(alog_s, alog_ref[...])
    rate_ref[...] = -jnp.exp(alog_s[...]) * LOG2E
    skip = skip_ref[...]

    def advance(t, carry):
        state, cum = carry
        rows = pl.ds(pl.multiple_of(t * g, g), g)
        step = step_s[rows, :]
        inp = in_s[rows, :]
        drive = step * inp
        out = skip * inp
        after = []
        for n in range(states):
            now = jnp.exp2(step * rate_ref[n * g : (n + 1) * g, :]) * state[n] + b_ref[t, n] * drive
            out = out + c_ref[t, n] * now
            after.append(now)
        cum = cum + step
        base_ref[rows, :] = out
        cum_ref[rows, :] = cum
        return (tuple(after), cum)

    zero = jnp.zeros((g, 128), f32)
    state, cum = lax.fori_loop(0, tokens, advance, ((zero,) * states, zero), unroll=2)
    z = z_s[...]
    silu_ref[...] = z / (1.0 + jnp.exp(-z))
    pack_ref[...] = jnp.concatenate(list(state) + [cum, zero], axis=0).astype(bf16)


def correct_kernel(c_ref, one_ref, two_ref, three_ref, base_ref, cum_ref, silu_ref, rate_ref, out_ref, gated_s):
    tokens, width = out_ref.shape
    g = width // 128
    states = rate_ref.shape[0] // g
    top = states * g

    def halves(ref):
        both = ref[...].astype(f32)
        return both[:top].reshape(states, g, 128), both[top : top + g]

    rate = rate_ref[...].reshape(states, g, 128)
    s1, c1 = halves(one_ref)
    s2, c2 = halves(two_ref)
    s3, _ = halves(three_ref)
    entering = s1 + jnp.exp2(c1[None] * rate) * (s2 + jnp.exp2(c2[None] * rate) * s3)

    def one(t, _):
        rows = pl.ds(pl.multiple_of(t * g, g), g)
        cum = cum_ref[rows, :]
        out = base_ref[rows, :]
        for n in range(states):
            out = out + c_ref[t, n] * (jnp.exp2(cum * rate_ref[n * g : (n + 1) * g, :]) * entering[n])
        gated_s[rows, :] = out * silu_ref[rows, :]
        return 0

    lax.fori_loop(0, tokens, one, 0, unroll=2)
    for k in range(g):
        out_ref[:, k * 128 : (k + 1) * 128] = gated_s[pl.ds(k, tokens, stride=g), :].astype(bf16)


def place_pair(scratch, odd, first, second):
    rows = first.shape[0]
    scratch[pl.ds(pl.multiple_of(odd * rows, rows), rows), :] = first
    scratch[pl.ds(pl.multiple_of((1 - odd) * rows, rows), rows), :] = second


def project_kernel(first_ref, second_ref, own_w_ref, peer_w_ref, out_ref, rows_s):
    @pl.when(pl.program_id(0) == 0)
    def _():
        place_pair(rows_s, lax.axis_index("ctx") % 2, first_ref[...], second_ref[...])

    half = own_w_ref.shape[0]
    out_ref[...] = (
        jnp.dot(rows_s[:, :half], own_w_ref[...], preferred_element_type=f32)
        + jnp.dot(rows_s[:, half:], peer_w_ref[...], preferred_element_type=f32)
    ).astype(bf16)


def select_kernel(
    own_ref, peer_ref, first_ref, second_ref, gain_ref, choose_ref,
    stream_first_ref, stream_second_ref, d0_ref, d1_ref, d2_ref, d3_ref, rows_s,
):
    odd = lax.axis_index("ctx") % 2
    block = stream_first_ref.shape[0]
    width = own_ref.shape[1]
    place_pair(rows_s, odd, first_ref[...], second_ref[...])
    stream = (
        rows_s[:, :width].astype(f32) + (own_ref[...].astype(f32) + peer_ref[...].astype(f32))
    ).astype(bf16)
    rows_s[:, :width] = stream
    stream_first_ref[...] = rows_s[pl.ds(pl.multiple_of(odd * block, block), block), :width]
    stream_second_ref[...] = rows_s[pl.ds(pl.multiple_of((1 - odd) * block, block), block), :width]
    wide = stream.astype(f32)
    squares = jnp.sum(wide * wide, axis=1, keepdims=True)
    high = squares.astype(bf16)
    low = (squares - high.astype(f32)).astype(bf16)
    lane = lax.broadcasted_iota(jnp.int32, (2 * block, 128), 1)
    stats = jnp.where(lane == 0, high.astype(f32), jnp.where(lane == 1, low.astype(f32), 0.0)).astype(bf16)
    feats = (wide * gain_ref[...]).astype(bf16)
    count = d0_ref.shape[0]
    for p, ref in enumerate((d0_ref, d1_ref, d2_ref, d3_ref)):
        pick = choose_ref[p * count : (p + 1) * count, :]
        ref[:, :width] = jnp.dot(pick, feats, preferred_element_type=f32).astype(bf16)
        ref[:, width:] = jnp.dot(pick, stats, preferred_element_type=f32).astype(bf16)


def gate_up_kernel(
    a0_ref, a1_ref, a2_ref, a3_ref, b0_ref, b1_ref, b2_ref, b3_ref, wg_ref, wu_ref,
    gate_ref, up_ref, squares_ref, feats_s,
):
    @pl.when(pl.program_id(0) == 0)
    def _():
        expert = lax.axis_index("ctx")
        tp = lax.axis_index("tp")
        here = expert // 2 == tp
        count = a0_ref.shape[0]
        width = a0_ref.shape[1] - 128

        def put(group, near_ref, far_ref):
            rows = pl.ds(pl.multiple_of((tp ^ group) * count, count), count)
            for side, ref in ((expert % 2, near_ref), (1 - expert % 2, far_ref)):
                feats_s[rows, pl.ds(pl.multiple_of(side * width, width), width)] = ref[:, :width]
            squares_ref[rows, :] = near_ref[:, width:].astype(f32) + far_ref[:, width:].astype(f32)

        @pl.when(here)
        def _():
            put(0, a0_ref, a1_ref)
            put(1, b0_ref, b1_ref)

        @pl.when(jnp.logical_not(here))
        def _():
            put(0, a2_ref, a3_ref)
            put(1, b2_ref, b3_ref)

    feats = feats_s[...]
    gate_ref[...] = jnp.dot(feats, wg_ref[...], preferred_element_type=f32).astype(bf16)
    up_ref[...] = jnp.dot(feats, wu_ref[...], preferred_element_type=f32).astype(bf16)


def hidden_of(gate0, gate1, up0, up1, sq0, sq1, features):
    squares = sq0[...] + sq1[...]
    scale = lax.rsqrt((squares[:, 0:1] + squares[:, 1:2]) * (1.0 / features) + 1e-06)
    gate = (gate0[...].astype(f32) + gate1[...].astype(f32)) * scale
    up = (up0[...].astype(f32) + up1[...].astype(f32)) * scale
    return (gate / (1.0 + jnp.exp(-gate)) * up).astype(bf16)


def down_first_kernel(features, gate0, gate1, up0, up1, sq0, sq1, w_ref, out_ref, hidden_s):
    @pl.when(pl.program_id(0) == 0)
    def _():
        hidden_s[...] = hidden_of(gate0, gate1, up0, up1, sq0, sq1, features)

    out_ref[...] = jnp.dot(hidden_s[...], w_ref[...], preferred_element_type=f32)


def down_second_kernel(features, gate0, gate1, up0, up1, sq0, sq1, w_ref, acc_ref, out_ref, hidden_s):
    @pl.when(pl.program_id(0) == 0)
    def _():
        hidden_s[...] = hidden_of(gate0, gate1, up0, up1, sq0, sq1, features)

    out_ref[...] = (acc_ref[...] + jnp.dot(hidden_s[...], w_ref[...], preferred_element_type=f32)).astype(bf16)


def reply_kernel(own_ref, peer_ref, r0_ref, r1_ref, r2_ref, r3_ref, sum_s):
    expert = lax.axis_index("ctx")
    sum_s[...] = own_ref[...].astype(f32) + peer_ref[...].astype(f32)
    count = r0_ref.shape[0]
    for p, ref in enumerate((r0_ref, r1_ref, r2_ref, r3_ref)):
        ref[...] = sum_s[pl.ds(pl.multiple_of((expert ^ p) * count, 8), count), :].astype(bf16)


def finish_kernel(stream_ref, high_ref, low_ref, r0_ref, r1_ref, r2_ref, r3_ref, out_ref):
    total = stream_ref[...].astype(f32)
    for p, ref in enumerate((r0_ref, r1_ref, r2_ref, r3_ref)):
        rows = ref[...]
        total = total + jnp.dot(high_ref[p], rows, preferred_element_type=f32)
        total = total + jnp.dot(low_ref[p], rows, preferred_element_type=f32)
    out_ref[...] = total.astype(bf16)


VMEM_LIMIT = 40 * 1024 * 1024


def params(**kw):
    return pltpu.CompilerParams(vmem_limit_bytes=VMEM_LIMIT, **kw)


VM = pl.BlockSpec(memory_space=pltpu.VMEM)
SM = pl.BlockSpec(memory_space=pltpu.SMEM)


def call(kernel, out, ins, scratch=(), args=()):
    return pl.pallas_call(
        kernel, out_shape=out, in_specs=ins, out_specs=jax.tree.map(lambda _: VM, out), scratch_shapes=list(scratch),
        compiler_params=params(),
    )(*args)


def shape(rows, cols, kind):
    return jax.ShapeDtypeStruct((rows, cols), kind)


def fast_body(
    resid, conv_out, gate_z, dt_raw, b_proj, c_proj, a_log, d_skip, out_weight, norm_gain,
    route_ids, route_weight, w_gate, w_up, w_down,
):
    tokens, model_width = resid.shape
    ctx_count, exp_count, tp_count = (lax.axis_size(a) for a in AXES)
    ctx, exp, tp = (lax.axis_index(a) for a in AXES)
    channels = conv_out.shape[1]
    states = a_log.shape[0]
    block_cols = out_weight.shape[1]
    half_width = model_width // tp_count
    piece_width = half_width // exp_count
    g = channels // 128

    def number(c, x, t):
        return (c * exp_count + x) * tp_count + t

    def owner(c):
        return c // (ctx_count // tp_count)

    chips = [(c, x) for c in range(ctx_count) for x in range(exp_count)]

    def permute(x, pairs):
        return lax.ppermute(x, AXES, pairs)

    def to_owner(x, p):
        return permute(x, [(number(c ^ p, e, owner(c)), number(c, e, owner(c))) for c, e in chips])

    def from_owner(x, p):
        return permute(x, [(number(c, e, owner(c)), number(c ^ p, e, owner(c))) for c, e in chips])

    def swap_tp(x):
        return lax.ppermute(x, "tp", [(i, tp_count - 1 - i) for i in range(tp_count)])

    with jax.named_scope("scan"):
        flat = shape(tokens * g, 128, f32)
        rates = shape(states * g, 128, f32)
        packed = shape((states + 2) * g, 128, bf16)
        base, cum, silu_z, rate, pack = call(
            scan_kernel, (flat, flat, flat, rates, packed), [SM, SM] + [VM] * 5,
            [pltpu.VMEM((tokens * g, 128), f32)] * 3 + [pltpu.VMEM((states * g, 128), f32)],
            (b_proj, c_proj, dt_raw, conv_out, gate_z, a_log, d_skip.reshape(g, 128)),
        )
    with jax.named_scope("relay"):
        entered = [
            permute(
                pack,
                [(number(c, x, t), number(c + s, x, t)) for c, x in chips for t in range(tp_count) if c + s < ctx_count],
            )
            for s in range(1, ctx_count)
        ]
    with jax.named_scope("routing"):
        flat_ids = route_ids.reshape(-1)
        pairs = flat_ids.shape[0]
        onehot = (flat_ids[:, None] == jnp.arange(EXPERTS, dtype=jnp.int32)[None, :]).astype(f32)
        index = jnp.arange(pairs, dtype=jnp.int32)
        earlier = (index[:, None] > index[None, :]).astype(f32)
        before = jnp.dot(earlier, onehot, preferred_element_type=f32)
        position = jnp.sum(before * onehot, axis=1).astype(jnp.int32)
        target = (flat_ids * CAP + position).reshape(tokens, 2)
        slots = jnp.arange(EXPERTS * CAP, dtype=jnp.int32)
        hits = slots[None, :, None] == target[:, None, :]
        weights = jnp.sum(jnp.where(hits, route_weight[:, None, :], 0.0), axis=2).reshape(tokens, EXPERTS, CAP)
        weights = jnp.stack(
            [lax.dynamic_index_in_dim(weights, ctx ^ p, 1, keepdims=False) for p in range(EXPERTS)]
        )
        weights_high = weights.astype(bf16)
        weights_low = (weights - weights_high.astype(f32)).astype(bf16)
        target_lanes = jnp.pad(target.astype(bf16), ((0, 0), (0, 126)))
    with jax.named_scope("residual"):
        cols = [
            jnp.concatenate([lax.dynamic_slice_in_dim(resid, (ctx ^ p) * block_cols, block_cols, 1), target_lanes], axis=1)
            for p in range(ctx_count)
        ]
        cols = [cols[0]] + [to_owner(cols[p], p) for p in range(1, ctx_count)]
        gain = lax.dynamic_slice_in_dim(norm_gain, ctx * block_cols, block_cols, 0)[None, :]
        peer_weight = swap_tp(out_weight)
    with jax.named_scope("choices"):
        odd = ctx % 2
        choose = []
        for first, second in ((cols[0], cols[1]), (cols[2], cols[3])):
            ids = [v[:, block_cols : block_cols + 2].astype(f32).T for v in (first, second)]
            ids = jnp.stack([jnp.where(odd == 0, ids[0], ids[1]), jnp.where(odd == 0, ids[1], ids[0])])
            want = (
                (ctx ^ jnp.arange(EXPERTS, dtype=jnp.int32))[:, None] * CAP + jnp.arange(CAP, dtype=jnp.int32)[None, :]
            ).astype(f32)
            hit = jnp.any(want[:, None, :, None, None] == ids.transpose(0, 2, 1)[None, :, None, :, :], axis=4)
            both = hit[:, :, :, None, :] & (jnp.arange(2)[:, None] == jnp.arange(2)[None, :])[None, :, None, :, None]
            choose.append(both.reshape(EXPERTS * 2 * CAP, 2 * tokens).astype(bf16))
    with jax.named_scope("correct"):
        gated = call(
            correct_kernel, shape(tokens, channels, bf16), [SM] + [VM] * 7, [pltpu.VMEM((tokens * g, 128), f32)],
            (c_proj, *entered, base, cum, silu_z, rate),
        )
    with jax.named_scope("gather_gated"):
        gated = jnp.concatenate([gated, swap_tp(gated)], axis=1)
        blocks = [gated] + [to_owner(gated, p) for p in range(1, ctx_count)]

    def project(first, second):
        n_block = 256 if block_cols % 256 == 0 else block_cols
        rows = 2 * tokens
        depth = out_weight.shape[0]
        whole = pl.BlockSpec((tokens, 2 * depth), lambda n: (0, 0))
        part = pl.BlockSpec((depth, n_block), lambda n: (0, n))
        return pl.pallas_call(
            project_kernel,
            out_shape=shape(rows, block_cols, bf16),
            grid=(block_cols // n_block,),
            in_specs=[whole, whole, part, part],
            out_specs=pl.BlockSpec((rows, n_block), lambda n: (0, n)),
            scratch_shapes=[pltpu.VMEM((rows, 2 * depth), bf16)],
            compiler_params=params(),
        )(first, second, out_weight, peer_weight)

    stream_blocks = []
    sent = []
    for group in range(2):
        with jax.named_scope("project"):
            own = project(blocks[2 * group], blocks[2 * group + 1])
        with jax.named_scope("sum_exp"):
            peer = permute(own, [(number(c, x, owner(c)), number(c, 1 - x, owner(c))) for c, x in chips])
        with jax.named_scope("select"):
            block = shape(tokens, block_cols, bf16)
            routed = shape(2 * CAP, block_cols + 128, bf16)
            first, second, *out = call(
                select_kernel, (block, block) + (routed,) * 4, [VM] * 6,
                [pltpu.VMEM((2 * tokens, block_cols + 128), bf16)],
                (own, peer, cols[2 * group], cols[2 * group + 1], gain, choose[group]),
            )
            stream_blocks += [first, second]
        with jax.named_scope("dispatch"):
            sent.append([out[0]] + [from_owner(out[p], p) for p in range(1, ctx_count)])
    with jax.named_scope("stream_home"):
        own_stream = stream_blocks[0]
        home = [
            permute(
                stream_blocks[p],
                [(number(c, c % exp_count, owner(c)), number(c ^ p, c % exp_count, owner(c))) for c in range(ctx_count)],
            )
            for p in range(1, ctx_count)
        ]
        apart = ctx ^ (tp * exp_count + exp)
        for p in range(1, ctx_count):
            own_stream = jnp.where(apart == p, home[p - 1], own_stream)

    slots_total = EXPERTS * CAP
    hidden_width = w_gate.shape[1]
    part_width = hidden_width // 2

    def gate_up(part):
        n_block = 256
        steps = part_width // n_block
        begin = part * steps
        routed = pl.BlockSpec((2 * CAP, block_cols + 128), lambda n: (0, 0))
        weight = pl.BlockSpec((half_width, n_block), lambda n: (0, begin + n))
        out = pl.BlockSpec((slots_total, n_block), lambda n: (0, n))
        return pl.pallas_call(
            gate_up_kernel,
            out_shape=(
                shape(slots_total, part_width, bf16), shape(slots_total, part_width, bf16), shape(slots_total, 128, f32),
            ),
            grid=(steps,),
            in_specs=[routed] * 8 + [weight, weight],
            out_specs=(out, out, pl.BlockSpec((slots_total, 128), lambda n: (0, 0))),
            scratch_shapes=[pltpu.VMEM((slots_total, half_width), bf16)],
            compiler_params=params(),
        )(*sent[0], *sent[1], w_gate, w_up)

    with jax.named_scope("gate_up"):
        parts = []
        for part in range(2):
            gate, up, squares = gate_up(part)
            if part == 0:
                squares_own, squares_peer = squares, swap_tp(squares)
            parts.append((gate, swap_tp(gate), up, swap_tp(up), squares_own, squares_peer))

    def down(part, kernel, kind, base_block, count, acc=None):
        n_block = 256
        whole = pl.BlockSpec((slots_total, part_width), lambda n, s: (0, 0))
        small = pl.BlockSpec((slots_total, 128), lambda n, s: (0, 0))
        ins = [whole] * 4 + [small] * 2 + [pl.BlockSpec((part_width, n_block), lambda n, s: (part, s[0] + n))]
        args = [*parts[part], w_down]
        if acc is not None:
            ins.append(pl.BlockSpec((slots_total, n_block), lambda n, s: (0, s[0] + n)))
            args.append(acc)

        def body_kernel(start_ref, *refs):
            kernel(model_width, *refs)

        return pl.pallas_call(
            body_kernel,
            out_shape=shape(slots_total, count * n_block, kind),
            grid_spec=pltpu.PrefetchScalarGridSpec(
                num_scalar_prefetch=1,
                grid=(count,),
                in_specs=ins,
                out_specs=pl.BlockSpec((slots_total, n_block), lambda n, s: (0, n)),
                scratch_shapes=[pltpu.VMEM((slots_total, part_width), bf16)],
            ),
            compiler_params=params(),
        )(base_block, *args)

    with jax.named_scope("down"):
        blocks_per_piece = piece_width // 256
        zero = jnp.zeros((1,), jnp.int32)
        acc = down(0, down_first_kernel, f32, zero, half_width // 256)
        theirs = down(1, down_second_kernel, bf16, zero + (1 - exp) * blocks_per_piece, blocks_per_piece, acc)
        mine = down(1, down_second_kernel, bf16, zero + exp * blocks_per_piece, blocks_per_piece, acc)
    with jax.named_scope("reply"):
        peer = lax.ppermute(theirs, "exp", [(0, 1), (1, 0)])
        reply = shape(CAP, piece_width, bf16)
        replies = call(
            reply_kernel, (reply,) * 4, [VM] * 2, [pltpu.VMEM((slots_total, piece_width), f32)], (mine, peer)
        )
        replies = [replies[0]] + [
            permute(replies[p], [(number(c, x, t), number(c ^ p, x, t)) for c, x in chips for t in range(tp_count)])
            for p in range(1, ctx_count)
        ]
    with jax.named_scope("finish"):
        return call(
            finish_kernel, shape(tokens, piece_width, bf16), [VM] * 7, (),
            (own_stream, weights_high, weights_low, *replies),
        )


def solution(mesh):
    in_specs = (
        P(("groups", "ctx"), None),
        P(("groups", "ctx"), ("exp", "tp")),
        P(("groups", "ctx"), ("exp", "tp")),
        P(("groups", "ctx"), ("exp", "tp")),
        P(("groups", "ctx"), None),
        P(("groups", "ctx"), None),
        P(None, ("exp", "tp")),
        P(("exp", "tp")),
        P(("exp", "tp"), "ctx"),
        P(),
        P(("groups", "ctx"), None),
        P(("groups", "ctx"), None),
        P("tp", ("ctx", "exp")),
        P("tp", ("ctx", "exp")),
        P(("ctx", "exp"), "tp"),
    )
    out_specs = P(("groups", "ctx"), ("tp", "exp"))
    sizes = dict(mesh.shape)
    small = (sizes["ctx"], sizes["exp"], sizes["tp"]) == (EXPERTS, 2, 2)
    chosen = fast_body if small else body
    return jax.shard_map(chosen, mesh=mesh, in_specs=in_specs, out_specs=out_specs, check_vma=False)
```

```python
import functools

import jax
import jax.numpy as jnp
from jax import lax
from jax.experimental import pallas as pl
from jax.experimental.pallas import tpu as pltpu
from jax.sharding import PartitionSpec as P

EXPERTS = 4
CAP = 40


def shifted(x, axis, by):
    peers = lax.axis_size(axis)
    pairs = [(i, i + by) for i in range(peers) if 0 <= i + by < peers]
    return lax.ppermute(x, axis, pairs)


def body(
    resid,
    conv_out,
    gate_z,
    dt_raw,
    b_proj,
    c_proj,
    a_log,
    d_skip,
    out_weight,
    norm_gain,
    route_ids,
    route_weight,
    w_gate,
    w_up,
    w_down,
):
    tokens = resid.shape[0]
    model_width = resid.shape[1]
    ctx_count = lax.axis_size("ctx")
    exp_count = lax.axis_size("exp")
    tp_count = lax.axis_size("tp")
    half_width = model_width // tp_count
    piece_width = half_width // exp_count
    tp_index = lax.axis_index("tp")
    exp_index = lax.axis_index("exp")
    stride_amount = jax.nn.softplus(dt_raw)
    rate = -jnp.exp(a_log)
    inputs = conv_out.astype(jnp.float32)

    def advance(carry_state, column):
        step_now, b_now, c_now, in_now = column
        carry_state = (
            jnp.exp(step_now[None, :] * rate) * carry_state
            + step_now[None, :] * b_now[:, None] * in_now[None, :]
        )
        return (carry_state, jnp.sum(c_now[:, None] * carry_state, axis=0))

    last_state, scanned_local = lax.scan(
        advance,
        jnp.zeros(rate.shape, jnp.float32),
        (stride_amount, b_proj, c_proj, inputs),
        unroll=8,
    )
    cum_step = jnp.cumsum(stride_amount, axis=0)
    last_decay = jnp.exp(cum_step[-1][None, :] * rate)

    def relay_turn(turn_index, carry_state):
        return shifted(last_decay * carry_state + last_state, "ctx", 1)

    entering = lax.fori_loop(0, ctx_count - 1, relay_turn, jnp.zeros_like(last_state))
    carried = jnp.exp(cum_step[:, None, :] * rate[None, :, :])
    scanned = scanned_local + jnp.sum(c_proj[:, :, None] * carried * entering[None, :, :], axis=1)
    gated_out = (
        (scanned + d_skip[None, :] * inputs) * jax.nn.silu(gate_z.astype(jnp.float32))
    ).astype(jnp.bfloat16)
    partial_value = jnp.dot(
        gated_out,
        lax.all_gather(out_weight, "ctx", axis=1, tiled=True),
        preferred_element_type=jnp.float32,
    )
    mamba_out = lax.psum(partial_value, ("exp", "tp"))
    stream = (resid.astype(jnp.float32) + mamba_out).astype(jnp.bfloat16)
    stream_wide = stream.astype(jnp.float32)
    square_mean = jnp.mean(stream_wide * stream_wide, axis=1, keepdims=True)
    normed = (stream_wide * lax.rsqrt(square_mean + 1e-06) * norm_gain[None, :]).astype(
        jnp.bfloat16
    )
    half_feats = lax.dynamic_slice_in_dim(normed, tp_index * half_width, half_width, 1)
    slot_total = EXPERTS * CAP
    flat_ids = route_ids.reshape(-1)
    pair_count = flat_ids.shape[0]
    onehot = (flat_ids[:, None] == jnp.arange(EXPERTS, dtype=jnp.int32)[None, :]).astype(
        jnp.float32
    )
    pair_index = jnp.arange(pair_count, dtype=jnp.int32)
    earlier_mask = (pair_index[:, None] > pair_index[None, :]).astype(jnp.float32)
    before = jnp.dot(earlier_mask, onehot, precision=lax.Precision.HIGHEST)
    position = jnp.sum(before * onehot, axis=1).astype(jnp.int32)
    target = (flat_ids * CAP + position).reshape(tokens, 2)
    matches = jnp.arange(slot_total, dtype=jnp.int32)[None, :, None] == target[:, None, :]
    placement = jnp.any(matches, axis=2).astype(jnp.bfloat16)
    combine_weights = jnp.sum(jnp.where(matches, route_weight[:, None, :], 0.0), axis=2)
    members = ctx_count // EXPERTS
    outgoing = lax.dot_general(
        placement, half_feats, (((0,), (0,)), ((), ())), preferred_element_type=jnp.float32
    )
    outgoing = jnp.repeat(
        outgoing.astype(jnp.bfloat16).reshape(EXPERTS, CAP, half_width), members, axis=0
    )
    arrived = lax.all_to_all(outgoing, "ctx", split_axis=0, concat_axis=0, tiled=True)
    sources = arrived.shape[0]
    item_count = arrived.shape[1]
    flat_rows = arrived.reshape(sources * item_count, half_width)
    gate_value = jnp.dot(flat_rows, w_gate, preferred_element_type=jnp.float32)
    up_value = jnp.dot(flat_rows, w_up, preferred_element_type=jnp.float32)
    gate_value, up_value = (
        lax.psum(gate_value.astype(jnp.bfloat16), "tp").astype(jnp.float32),
        lax.psum(up_value.astype(jnp.bfloat16), "tp").astype(jnp.float32),
    )
    hidden = (jax.nn.silu(gate_value) * up_value).astype(jnp.bfloat16)
    answer = jnp.dot(hidden, w_down, preferred_element_type=jnp.float32).astype(jnp.bfloat16)
    answer = answer.reshape(sources, item_count, half_width)
    returned = lax.all_to_all(answer, "ctx", split_axis=0, concat_axis=0, tiled=True)
    reply_width = returned.shape[2]
    merged = jnp.sum(
        returned.astype(jnp.float32).reshape(EXPERTS, members, CAP, reply_width), axis=1
    )
    merged = merged.reshape(slot_total, reply_width)
    moe_rows = jnp.dot(combine_weights, merged, precision=lax.Precision.HIGHEST)
    moe_piece = lax.psum_scatter(
        moe_rows.astype(jnp.bfloat16), "exp", scatter_dimension=1, tiled=True
    ).astype(jnp.float32)
    own_stream = lax.dynamic_slice_in_dim(
        stream_wide, tp_index * half_width + exp_index * piece_width, piece_width, 1
    )
    return (own_stream + moe_piece).astype(jnp.bfloat16)


LOG2E = 1.4426950408889634
AXES = ("ctx", "exp", "tp")
f32 = jnp.float32
bf16 = jnp.bfloat16


def lanes_to_rows(store_ref, value):
    rows, width = value.shape
    count = width // 128
    for k in range(count):
        store_ref[pl.ds(k, rows, stride=count), :] = value[:, k * 128 : (k + 1) * 128]


def scan_kernel(
    b_ref, c_ref, dt_ref, conv_ref, z_ref, alog_ref, skip_ref,
    base_ref, cum_ref, silu_ref, rate_ref, pack_ref, step_s, in_s, z_s, alog_s,
):
    tokens, width = dt_ref.shape
    states = alog_ref.shape[0]
    g = width // 128
    lanes_to_rows(step_s, jax.nn.softplus(dt_ref[...]))
    lanes_to_rows(in_s, conv_ref[...].astype(f32))
    lanes_to_rows(z_s, z_ref[...].astype(f32))
    lanes_to_rows(alog_s, alog_ref[...])
    rate_ref[...] = -jnp.exp(alog_s[...]) * LOG2E
    skip = skip_ref[...]

    def advance(t, carry):
        state, cum = carry
        rows = pl.ds(pl.multiple_of(t * g, g), g)
        step = step_s[rows, :]
        inp = in_s[rows, :]
        drive = step * inp
        out = skip * inp
        after = []
        for n in range(states):
            now = jnp.exp2(step * rate_ref[n * g : (n + 1) * g, :]) * state[n] + b_ref[n, t] * drive
            out = out + c_ref[n, t] * now
            after.append(now)
        cum = cum + step
        base_ref[rows, :] = out
        cum_ref[rows, :] = cum
        return (tuple(after), cum)

    zero = jnp.zeros((g, 128), f32)
    state, cum = lax.fori_loop(0, tokens, advance, ((zero,) * states, zero), unroll=2)
    z = z_s[...]
    silu_ref[...] = z / (1.0 + jnp.exp(-z))
    pack_ref[...] = jnp.concatenate(list(state) + [cum, zero], axis=0).astype(bf16)


def correct_kernel(c_ref, one_ref, two_ref, three_ref, base_ref, cum_ref, silu_ref, rate_ref, out_ref, gated_s):
    tokens, width = out_ref.shape
    g = width // 128
    states = rate_ref.shape[0] // g
    top = states * g

    def halves(ref):
        both = ref[...].astype(f32)
        return both[:top].reshape(states, g, 128), both[top : top + g]

    rate = rate_ref[...].reshape(states, g, 128)
    ctx = lax.axis_index("ctx")
    s1, c1 = halves(one_ref)
    s2, c2 = halves(two_ref)
    s3, c3 = halves(three_ref)
    near, near_sum = jnp.where(ctx == 2, s3, s1), jnp.where(ctx == 2, c3, c1)
    far = jnp.where(ctx == 3, s3, 0.0)
    middle = s2 + jnp.exp2(c2[None] * rate) * far
    entering = near + jnp.exp2(near_sum[None] * rate) * jnp.where(ctx >= 2, middle, 0.0)
    entering = jnp.where(ctx == 0, 0.0, entering)

    def one(t, _):
        rows = pl.ds(pl.multiple_of(t * g, g), g)
        cum = cum_ref[rows, :]
        out = base_ref[rows, :]
        for n in range(states):
            out = out + c_ref[n, t] * (jnp.exp2(cum * rate_ref[n * g : (n + 1) * g, :]) * entering[n])
        gated_s[rows, :] = out * silu_ref[rows, :]
        return 0

    lax.fori_loop(0, tokens, one, 0, unroll=2)
    for k in range(g):
        out_ref[:, k * 128 : (k + 1) * 128] = gated_s[pl.ds(k, tokens, stride=g), :].astype(bf16)


def place_pair(scratch, odd, first, second):
    rows = first.shape[0]
    scratch[pl.ds(pl.multiple_of(odd * rows, rows), rows), :] = first
    scratch[pl.ds(pl.multiple_of((1 - odd) * rows, rows), rows), :] = second


def route_kernel(ids_ref, lanes_ref, cols_ref):
    count = cols_ref.shape[0]
    ids = ids_ref[...].astype(f32)
    first, second = ids[0:1, :], ids[1:2, :]
    expert = lax.broadcasted_iota(jnp.int32, (8, 128), 0).astype(f32)
    member = (jnp.where(expert == first, 1.0, 0.0) + jnp.where(expert == second, 1.0, 0.0)).astype(bf16)
    before = lax.broadcasted_iota(jnp.int32, (128, 128), 0)
    token = lax.broadcasted_iota(jnp.int32, (128, 128), 1)
    token = jnp.where(token >= count, token - count, token)
    earlier = jnp.where((before < token) & (before < count), 1.0, 0.0).astype(bf16)
    rank = jnp.dot(member, earlier, preferred_element_type=f32)
    slot = [
        which * CAP + jnp.sum(jnp.where(expert == which, rank, 0.0), axis=0, keepdims=True) for which in (first, second)
    ]
    row = lax.broadcasted_iota(jnp.int32, (128, 128), 0)
    both = jnp.where(row == 0, slot[0], jnp.where(row == 1, slot[1], 0.0))
    lanes_ref[...] = both[:8]
    cols_ref[...] = both.T[:count].astype(bf16)


def pack_kernel(own_ref, peer_ref, resid_ref, slots_ref, m0_ref, m1_ref, m2_ref, m3_ref):
    ctx, exp = lax.axis_index("ctx"), lax.axis_index("exp")
    width = own_ref.shape[1]
    part = m0_ref.shape[1] - 2 * width - 128
    for p, ref in enumerate((m0_ref, m1_ref, m2_ref, m3_ref)):
        ref[:, :width] = own_ref[...]
        ref[:, width : 2 * width] = peer_ref[...]
        begin = pl.multiple_of((ctx ^ p) * 2 * part + exp * part, 128)
        ref[:, 2 * width : 2 * width + part] = resid_ref[:, pl.ds(begin, part)]
        ref[:, 2 * width + part :] = slots_ref[...]


def hold_kernel(own_ref, peer_ref, out_ref, sems):
    half = own_ref.shape[0]
    copies = [
        pltpu.make_async_copy(ref, out_ref.at[pl.ds(k * half, half)], sems.at[k]) for k, ref in enumerate((own_ref, peer_ref))
    ]
    for copy in copies:
        copy.start()
    for copy in copies:
        copy.wait()


def place_pair(scratch, odd, first, second):
    rows = first.shape[0]
    scratch[pl.ds(pl.multiple_of(odd * rows, rows), rows), :] = first
    scratch[pl.ds(pl.multiple_of((1 - odd) * rows, rows), rows), :] = second


def project_kernel(first_ref, second_ref, w_ref, out_ref, slots_ref, rows_s):
    place_pair(rows_s, lax.axis_index("ctx") % 2, first_ref[...], second_ref[...])
    exp = lax.axis_index("exp")
    depth = w_ref.shape[0]
    part = out_ref.shape[1] // 2
    resid = rows_s[:, depth : depth + part].astype(f32)
    feats = rows_s[:, :depth]
    for side in range(2):
        value = jnp.dot(feats, w_ref[:, side * part : (side + 1) * part], preferred_element_type=f32)
        out_ref[:, side * part : (side + 1) * part] = (value + jnp.where(exp == side, resid, 0.0)).astype(bf16)
    slots_ref[...] = rows_s[:, depth + part :]


def select_kernel(
    own_ref, peer_ref, slots_ref, gain_ref, stream_first_ref, stream_second_ref, d0_ref, d1_ref, d2_ref, d3_ref, rows_s
):
    ctx = lax.axis_index("ctx")
    odd = ctx % 2
    block = stream_first_ref.shape[0]
    width = own_ref.shape[1]
    rows_s[...] = (own_ref[...].astype(f32) + peer_ref[...].astype(f32)).astype(bf16)
    stream_first_ref[...] = rows_s[pl.ds(pl.multiple_of(odd * block, block), block), :]
    stream_second_ref[...] = rows_s[pl.ds(pl.multiple_of((1 - odd) * block, block), block), :]
    wide = rows_s[...].astype(f32)
    squares = jnp.sum(wide * wide, axis=1, keepdims=True)
    high = squares.astype(bf16).astype(f32)
    lane = lax.broadcasted_iota(jnp.int32, (2 * block, 128), 1)
    stats = jnp.where(lane == 0, high, jnp.where(lane == 1, squares - high, 0.0)).astype(bf16)
    feats = (wide * gain_ref[...]).astype(bf16)
    slots = slots_ref[...].astype(f32).T
    count = d0_ref.shape[0]
    row = lax.broadcasted_iota(jnp.int32, (count, 2 * block), 0)
    lane = lax.broadcasted_iota(jnp.int32, (count, 2 * block), 1)
    late = row >= CAP
    mine = late == (lane >= block)
    want = jnp.where(late, row - CAP, row).astype(f32)
    for p, ref in enumerate((d0_ref, d1_ref, d2_ref, d3_ref)):
        base = ((ctx ^ p) * CAP).astype(f32)
        hit = mine & ((slots[0:1, :] == want + base) | (slots[1:2, :] == want + base))
        pick = jnp.where(hit, 1.0, 0.0).astype(bf16)
        ref[:, :width] = jnp.dot(pick, feats, preferred_element_type=f32).astype(bf16)
        ref[:, width:] = jnp.dot(pick, stats, preferred_element_type=f32).astype(bf16)


def gate_up_copies(wg_ref, wu_ref, held_ref, sems, begin):
    depth = wg_ref.shape[0]
    width = held_ref.shape[1]
    return [
        pltpu.make_async_copy(
            ref.at[:, pl.ds(begin, width)], held_ref.at[pl.ds(k * depth, depth)], sems.at[k]
        )
        for k, ref in enumerate((wg_ref, wu_ref))
    ]


def hold_first_kernel(wg_ref, wu_ref, held_ref, sems):
    copies = gate_up_copies(wg_ref, wu_ref, held_ref, sems, 0)
    for copy in copies:
        copy.start()
    for copy in copies:
        copy.wait()


def gate_up(feats, held_ref, out_ref):
    depth = feats.shape[1]
    width = held_ref.shape[1]
    block = min(512, width)
    for k in range(2):
        for n in range(0, width, block):
            out_ref[:, k * width + n : k * width + n + block] = jnp.dot(
                feats, held_ref[k * depth : (k + 1) * depth, n : n + block], preferred_element_type=f32
            ).astype(bf16)


def first_half_kernel(
    a0_ref, a1_ref, a2_ref, a3_ref, b0_ref, b1_ref, b2_ref, b3_ref, held_ref, wg_ref, wu_ref,
    out_ref, squares_ref, feats_ref, next_ref, sems,
):
    copies = gate_up_copies(wg_ref, wu_ref, next_ref, sems, held_ref.shape[1])
    for copy in copies:
        copy.start()
    expert = lax.axis_index("ctx")
    tp = lax.axis_index("tp")
    here = expert // 2 == tp
    count = a0_ref.shape[0]
    width = a0_ref.shape[1] - 128

    def put(group, near_ref, far_ref):
        rows = pl.ds(pl.multiple_of((tp ^ group) * count, count), count)
        for side, ref in ((expert % 2, near_ref), (1 - expert % 2, far_ref)):
            feats_ref[rows, pl.ds(pl.multiple_of(side * width, width), width)] = ref[:, :width]
        squares_ref[rows, :] = near_ref[:, width:].astype(f32) + far_ref[:, width:].astype(f32)

    @pl.when(here)
    def _():
        put(0, a0_ref, a1_ref)
        put(1, b0_ref, b1_ref)

    @pl.when(jnp.logical_not(here))
    def _():
        put(0, a2_ref, a3_ref)
        put(1, b2_ref, b3_ref)

    gate_up(feats_ref[...], held_ref, out_ref)
    for copy in copies:
        copy.wait()


def second_half_kernel(feats_ref, held_ref, wd_ref, out_ref, next_ref, sem):
    copy = pltpu.make_async_copy(wd_ref, next_ref, sem)
    copy.start()
    gate_up(feats_ref[...], held_ref, out_ref)
    copy.wait()


def hidden_of(own_ref, peer_ref, sq0, sq1, features):
    squares = sq0[...] + sq1[...]
    scale = lax.rsqrt((squares[:, 0:1] + squares[:, 1:2]) * (1.0 / features) + 1e-06)
    width = own_ref.shape[1] // 2
    gate = (own_ref[:, :width].astype(f32) + peer_ref[:, :width].astype(f32)) * scale
    up = (own_ref[:, width:].astype(f32) + peer_ref[:, width:].astype(f32)) * scale
    return (gate / (1.0 + jnp.exp(-gate)) * up).astype(bf16)


def down_first_kernel(features, own_ref, peer_ref, sq0, sq1, held_ref, out_ref):
    hidden = hidden_of(own_ref, peer_ref, sq0, sq1, features)
    depth = hidden.shape[1]
    block = min(512, out_ref.shape[1])
    for n in range(0, out_ref.shape[1], block):
        out_ref[:, n : n + block] = jnp.dot(hidden, held_ref[:depth, n : n + block], preferred_element_type=f32)


def down_piece(hidden, held_ref, acc_ref, near_ref, far_ref, sum_s, piece):
    depth = hidden.shape[1]
    count, width = near_ref.shape
    cols = pl.ds(pl.multiple_of(piece * width, width), width)
    sum_s[...] = acc_ref[:, cols] + jnp.dot(hidden, held_ref[depth:, cols], preferred_element_type=f32)
    pair = lax.axis_index("ctx") // 2
    near_ref[...] = sum_s[pl.ds(pl.multiple_of(pair * count, count), count), :].astype(bf16)
    far_ref[...] = sum_s[pl.ds(pl.multiple_of((1 - pair) * count, count), count), :].astype(bf16)


def down_theirs_kernel(
    features, own_ref, peer_ref, sq0, sq1, held_ref, acc_ref, near_ref, far_ref, hidden_ref, sum_s
):
    hidden_ref[...] = hidden_of(own_ref, peer_ref, sq0, sq1, features)
    down_piece(hidden_ref[...], held_ref, acc_ref, near_ref, far_ref, sum_s, 1 - lax.axis_index("exp"))


def down_mine_kernel(hidden_ref, held_ref, acc_ref, near_ref, far_ref, sum_s):
    down_piece(hidden_ref[...], held_ref, acc_ref, near_ref, far_ref, sum_s, lax.axis_index("exp"))


def reply_kernel(own_ref, peer_ref, first_ref, second_ref, sum_s):
    odd = lax.axis_index("ctx") % 2
    sum_s[...] = own_ref[...].astype(f32) + peer_ref[...].astype(f32)
    count = first_ref.shape[0]
    for place, ref in ((odd, first_ref), (1 - odd, second_ref)):
        ref[...] = sum_s[pl.ds(pl.multiple_of(place * count, 8), count), :].astype(bf16)


def finish_kernel(
    s0_ref, s1_ref, s2_ref, s3_ref, slots_ref, weights_ref, r0_ref, r1_ref, r2_ref, r3_ref, out_ref
):
    ctx = lax.axis_index("ctx")
    apart = ctx ^ (lax.axis_index("tp") * lax.axis_size("exp") + lax.axis_index("exp"))
    tokens = out_ref.shape[0]
    stream = s0_ref[...]
    for p, ref in ((1, s1_ref), (2, s2_ref), (3, s3_ref)):
        stream = jnp.where(apart == p, ref[...], stream)
    total = stream.astype(f32)
    over_rows = (((0,), (0,)), ((), ()))
    want = lax.broadcasted_iota(jnp.int32, (r0_ref.shape[0], tokens), 0).astype(f32)
    for p, ref in enumerate((r0_ref, r1_ref, r2_ref, r3_ref)):
        base = ((ctx ^ p) * CAP).astype(f32)
        weight = jnp.zeros(want.shape, f32)
        for k in range(2):
            weight = weight + jnp.where(slots_ref[k : k + 1, :tokens] == want + base, weights_ref[k : k + 1, :], 0.0)
        high = weight.astype(bf16)
        low = (weight - high.astype(f32)).astype(bf16)
        rows = ref[...]
        total = total + lax.dot_general(high, rows, over_rows, preferred_element_type=f32)
        total = total + lax.dot_general(low, rows, over_rows, preferred_element_type=f32)
    out_ref[...] = total.astype(bf16)


VM = pl.BlockSpec(memory_space=pltpu.VMEM)
SM = pl.BlockSpec(memory_space=pltpu.SMEM)
HB = pl.BlockSpec(memory_space=pltpu.HBM)
AN = pl.BlockSpec(memory_space=pl.ANY)


def call(kernel, out, ins, scratch=(), args=(), limit=8, us=1.0):
    return pl.pallas_call(
        kernel, out_shape=out, in_specs=ins, out_specs=jax.tree.map(lambda _: VM, out), scratch_shapes=list(scratch),
        compiler_params=pltpu.CompilerParams(vmem_limit_bytes=limit * 1024 * 1024),
        cost_estimate=pl.CostEstimate(flops=0, transcendentals=0, bytes_accessed=int(us * 3.0e6)),
    )(*args)


def shape(rows, cols, kind):
    return jax.ShapeDtypeStruct((rows, cols), kind)


def in_hbm(x):
    return pltpu.with_memory_space_constraint(x, pltpu.HBM)


def in_vmem(x):
    return pltpu.with_memory_space_constraint(x, pltpu.VMEM)


def fast_body(
    resid, conv_out, gate_z, dt_raw, b_proj, c_proj, a_log, d_skip, out_weight, norm_gain,
    route_ids, route_weight, w_gate, w_up, w_down,
):
    tokens, model_width = resid.shape
    ctx_count, exp_count, tp_count = (lax.axis_size(a) for a in AXES)
    ctx = lax.axis_index("ctx")
    channels = conv_out.shape[1]
    states = a_log.shape[0]
    block_cols = out_weight.shape[1]
    half_width = model_width // tp_count
    piece_width = half_width // exp_count
    g = channels // 128

    def number(c, x, t):
        return (c * exp_count + x) * tp_count + t

    def owner(c):
        return c // (ctx_count // tp_count)

    chips = [(c, x) for c in range(ctx_count) for x in range(exp_count)]
    away = range(1, ctx_count)

    def permute(x, pairs):
        return lax.ppermute(x, AXES, pairs)

    def to_owner(x, p):
        return permute(x, [(number(c ^ p, e, owner(c)), number(c, e, owner(c))) for c, e in chips])

    def from_owner(x, p):
        return permute(x, [(number(c, e, owner(c)), number(c ^ p, e, owner(c))) for c, e in chips])

    def swap_tp(x):
        return lax.ppermute(x, "tp", [(i, tp_count - 1 - i) for i in range(tp_count)])

    peer_weight = swap_tp(out_weight)
    with jax.named_scope("scan"):
        flat = shape(tokens * g, 128, f32)
        b_rows, c_rows = b_proj.T, c_proj.T
        base, cum, silu_z, rate, pack = call(
            scan_kernel,
            (flat, flat, flat, shape(states * g, 128, f32), shape((states + 2) * g, 128, bf16)),
            [SM, SM] + [VM] * 5,
            [pltpu.VMEM((tokens * g, 128), f32)] * 3 + [pltpu.VMEM((states * g, 128), f32)],
            tuple(in_hbm(v) for v in (b_rows, c_rows, dt_raw, conv_out, gate_z, a_log, d_skip.reshape(g, 128))), us=3.0,
        )
    with jax.named_scope("relay"):
        entered = [
            permute(pack, [(number(c, x, t), number(c ^ p, x, t)) for c, x in chips for t in range(tp_count)])
            for p in away
        ]
    with jax.named_scope("correct"):
        gated = call(
            correct_kernel, shape(tokens, channels, bf16), [SM] + [VM] * 7, [pltpu.VMEM((tokens * g, 128), f32)],
            (in_hbm(c_rows), *entered, base, cum, silu_z, rate), us=2.0,
        )
    gated, route_ids, norm_gain = lax.optimization_barrier((gated, route_ids, norm_gain))
    with jax.named_scope("gather_gated"):
        peer_gated = swap_tp(gated)
    with jax.named_scope("route"):
        ids = route_ids.T
        slot_lanes, slot_cols = call(
            route_kernel, (shape(8, 128, f32), shape(tokens, 128, bf16)), [VM], (), (jnp.concatenate([ids, ids], axis=1),)
        )
    with jax.named_scope("gather_gated"):
        message = shape(tokens, 2 * channels + block_cols // 2 + 128, bf16)
        messages = call(
            pack_kernel, (message,) * 4, [VM] * 4, (), (gated, peer_gated, in_hbm(resid), slot_cols)
        )
        blocks = [messages[0]] + [to_owner(messages[p], p) for p in away]

    def hold_out(after):
        own_rows, peer_rows, _ = lax.optimization_barrier((out_weight, peer_weight, after))
        with jax.named_scope("hold_out_weight"):
            return call(
                hold_kernel, pltpu.VMEM((2 * own_rows.shape[0], block_cols), bf16), [HB, AN], [pltpu.SemaphoreType.DMA((2,))],
                (in_hbm(own_rows), peer_rows), us=1.6,
            )

    held_out = hold_out(messages[0])
    gain = lax.dynamic_slice_in_dim(norm_gain, ctx * block_cols, block_cols, 0)[None, :]

    streams = []
    sent = []
    for group in range(2):
        with jax.named_scope("project"):
            own, slots = call(
                project_kernel, (shape(2 * tokens, block_cols, bf16), shape(2 * tokens, 128, bf16)), [VM] * 3,
                [pltpu.VMEM((2 * tokens, message.shape[1]), bf16)],
                (blocks[2 * group], blocks[2 * group + 1], in_vmem(held_out)),
            )
        if group == 0:
            held_out = hold_out(own)
        with jax.named_scope("sum_exp"):
            peer = permute(own, [(number(c, x, owner(c)), number(c, 1 - x, owner(c))) for c, x in chips])
        with jax.named_scope("select"):
            block = shape(tokens, block_cols, bf16)
            routed = shape(2 * CAP, block_cols + 128, bf16)
            first, second, *out = call(
                select_kernel, (block, block) + (routed,) * 4, [VM] * 4, [pltpu.VMEM((2 * tokens, block_cols), bf16)],
                (own, peer, slots, gain),
            )
            streams += [first, second]
            if group == 0:
                *out, blocks[2], blocks[3] = lax.optimization_barrier((*out, blocks[2], blocks[3]))
        with jax.named_scope("dispatch"):
            sent.append([out[0]] + [from_owner(out[p], p) for p in away])

    slots_total = EXPERTS * CAP
    part_width = w_gate.shape[1] // 2
    wg, wu, wd = (in_hbm(v) for v in (w_gate, w_up, w_down))
    dma = pltpu.SemaphoreType.DMA
    with jax.named_scope("hold_weights"):
        held_kind = pltpu.VMEM((2 * half_width, part_width), bf16)
        held = call(hold_first_kernel, held_kind, [HB, HB], [dma((2,))], (wg, wu), us=5.8)
    with jax.named_scope("gate_up"):
        both = shape(slots_total, 2 * part_width, bf16)
        first, squares, feats, held = call(
            first_half_kernel,
            (both, shape(slots_total, 128, f32), shape(slots_total, half_width, bf16), held_kind),
            [VM] * 9 + [HB] * 2, [dma((2,))],
            (*sent[0], *sent[1], in_vmem(held), wg, wu), us=5.8,
        )
        peer_squares = swap_tp(squares)
        peer_first = swap_tp(first)
        second, held = call(
            second_half_kernel, (both, pltpu.VMEM(w_down.shape, bf16)), [VM, VM, HB], [dma], (feats, in_vmem(held), wd), us=5.8
        )
        peer_second = swap_tp(second)
    with jax.named_scope("down"):
        held = in_vmem(held)
        acc = call(
            functools.partial(down_first_kernel, model_width), shape(slots_total, half_width, f32), [VM] * 5, (),
            (first, peer_first, squares, peer_squares, held), us=2.0,
        )
        piece = shape(slots_total // 2, piece_width, bf16)
        total = pltpu.VMEM((slots_total, piece_width), f32)
        theirs_near, theirs_far, hidden = call(
            functools.partial(down_theirs_kernel, model_width), (piece, piece, shape(slots_total, part_width, bf16)),
            [VM] * 6, [total], (second, peer_second, squares, peer_squares, held, acc), us=1.4,
        )
    with jax.named_scope("sum_experts"):
        swap = [(0, 1), (1, 0)]
        peer_far = lax.ppermute(theirs_far, "exp", swap)
        theirs_near, _ = lax.optimization_barrier((theirs_near, theirs_far))
        peer_near = lax.ppermute(theirs_near, "exp", swap)
        mine_near, mine_far = call(down_mine_kernel, (piece, piece), [VM] * 3, [total], (hidden, held, acc))
    with jax.named_scope("stream_home"):
        *streams, mine_far = lax.optimization_barrier((*streams, mine_far))
        home = [
            permute(
                streams[p],
                [(number(c, c % exp_count, owner(c)), number(c ^ p, c % exp_count, owner(c))) for c in range(ctx_count)],
            )
            for p in away
        ]

    def reply(own, peer):
        small = shape(CAP, piece_width, bf16)
        return call(
            reply_kernel, (small, small), [VM] * 2, [pltpu.VMEM((slots_total // 2, piece_width), f32)], (own, peer)
        )

    def send(x, p):
        return permute(x, [(number(c, x_at, t), number(c ^ p, x_at, t)) for c, x_at in chips for t in range(tp_count)])

    with jax.named_scope("reply"):
        r2, r3 = reply(mine_far, peer_far)
        far = [send(r2, 2), send(r3, 3)]
        mine_near, peer_near, _ = lax.optimization_barrier((mine_near, peer_near, r2))
        r0, r1 = reply(mine_near, peer_near)
        replies = [r0, send(r1, 1), *far]
    with jax.named_scope("finish"):
        return call(
            finish_kernel, shape(tokens, piece_width, bf16), [VM] * 10, (),
            (streams[0], *home, slot_lanes, route_weight.T, *replies),
        )


def solution(mesh):
    in_specs = (
        P(("groups", "ctx"), None),
        P(("groups", "ctx"), ("exp", "tp")),
        P(("groups", "ctx"), ("exp", "tp")),
        P(("groups", "ctx"), ("exp", "tp")),
        P(("groups", "ctx"), None),
        P(("groups", "ctx"), None),
        P(None, ("exp", "tp")),
        P(("exp", "tp")),
        P(("exp", "tp"), "ctx"),
        P(),
        P(("groups", "ctx"), None),
        P(("groups", "ctx"), None),
        P("tp", ("ctx", "exp")),
        P("tp", ("ctx", "exp")),
        P(("ctx", "exp"), "tp"),
    )
    out_specs = P(("groups", "ctx"), ("tp", "exp"))
    sizes = dict(mesh.shape)
    small = (sizes["ctx"], sizes["exp"], sizes["tp"]) == (EXPERTS, 2, 2)
    chosen = fast_body if small else body
    return jax.shard_map(chosen, mesh=mesh, in_specs=in_specs, out_specs=out_specs, check_vma=False)
```

```python
import functools

import jax
import jax.numpy as jnp
from jax import lax
from jax.experimental import pallas as pl
from jax.experimental.pallas import tpu as pltpu
from jax.sharding import PartitionSpec as P

EXPERTS = 4
CAP = 40


def shifted(x, axis, by):
    peers = lax.axis_size(axis)
    pairs = [(i, i + by) for i in range(peers) if 0 <= i + by < peers]
    return lax.ppermute(x, axis, pairs)


def body(
    resid,
    conv_out,
    gate_z,
    dt_raw,
    b_proj,
    c_proj,
    a_log,
    d_skip,
    out_weight,
    norm_gain,
    route_ids,
    route_weight,
    w_gate,
    w_up,
    w_down,
):
    tokens = resid.shape[0]
    model_width = resid.shape[1]
    ctx_count = lax.axis_size("ctx")
    exp_count = lax.axis_size("exp")
    tp_count = lax.axis_size("tp")
    half_width = model_width // tp_count
    piece_width = half_width // exp_count
    tp_index = lax.axis_index("tp")
    exp_index = lax.axis_index("exp")
    stride_amount = jax.nn.softplus(dt_raw)
    rate = -jnp.exp(a_log)
    inputs = conv_out.astype(jnp.float32)

    def advance(carry_state, column):
        step_now, b_now, c_now, in_now = column
        carry_state = (
            jnp.exp(step_now[None, :] * rate) * carry_state
            + step_now[None, :] * b_now[:, None] * in_now[None, :]
        )
        return (carry_state, jnp.sum(c_now[:, None] * carry_state, axis=0))

    last_state, scanned_local = lax.scan(
        advance,
        jnp.zeros(rate.shape, jnp.float32),
        (stride_amount, b_proj, c_proj, inputs),
        unroll=8,
    )
    cum_step = jnp.cumsum(stride_amount, axis=0)
    last_decay = jnp.exp(cum_step[-1][None, :] * rate)

    def relay_turn(turn_index, carry_state):
        return shifted(last_decay * carry_state + last_state, "ctx", 1)

    entering = lax.fori_loop(0, ctx_count - 1, relay_turn, jnp.zeros_like(last_state))
    carried = jnp.exp(cum_step[:, None, :] * rate[None, :, :])
    scanned = scanned_local + jnp.sum(c_proj[:, :, None] * carried * entering[None, :, :], axis=1)
    gated_out = (
        (scanned + d_skip[None, :] * inputs) * jax.nn.silu(gate_z.astype(jnp.float32))
    ).astype(jnp.bfloat16)
    partial_value = jnp.dot(
        gated_out,
        lax.all_gather(out_weight, "ctx", axis=1, tiled=True),
        preferred_element_type=jnp.float32,
    )
    mamba_out = lax.psum(partial_value, ("exp", "tp"))
    stream = (resid.astype(jnp.float32) + mamba_out).astype(jnp.bfloat16)
    stream_wide = stream.astype(jnp.float32)
    square_mean = jnp.mean(stream_wide * stream_wide, axis=1, keepdims=True)
    normed = (stream_wide * lax.rsqrt(square_mean + 1e-06) * norm_gain[None, :]).astype(
        jnp.bfloat16
    )
    half_feats = lax.dynamic_slice_in_dim(normed, tp_index * half_width, half_width, 1)
    slot_total = EXPERTS * CAP
    flat_ids = route_ids.reshape(-1)
    pair_count = flat_ids.shape[0]
    onehot = (flat_ids[:, None] == jnp.arange(EXPERTS, dtype=jnp.int32)[None, :]).astype(
        jnp.float32
    )
    pair_index = jnp.arange(pair_count, dtype=jnp.int32)
    earlier_mask = (pair_index[:, None] > pair_index[None, :]).astype(jnp.float32)
    before = jnp.dot(earlier_mask, onehot, precision=lax.Precision.HIGHEST)
    position = jnp.sum(before * onehot, axis=1).astype(jnp.int32)
    target = (flat_ids * CAP + position).reshape(tokens, 2)
    matches = jnp.arange(slot_total, dtype=jnp.int32)[None, :, None] == target[:, None, :]
    placement = jnp.any(matches, axis=2).astype(jnp.bfloat16)
    combine_weights = jnp.sum(jnp.where(matches, route_weight[:, None, :], 0.0), axis=2)
    members = ctx_count // EXPERTS
    outgoing = lax.dot_general(
        placement, half_feats, (((0,), (0,)), ((), ())), preferred_element_type=jnp.float32
    )
    outgoing = jnp.repeat(
        outgoing.astype(jnp.bfloat16).reshape(EXPERTS, CAP, half_width), members, axis=0
    )
    arrived = lax.all_to_all(outgoing, "ctx", split_axis=0, concat_axis=0, tiled=True)
    sources = arrived.shape[0]
    item_count = arrived.shape[1]
    flat_rows = arrived.reshape(sources * item_count, half_width)
    gate_value = jnp.dot(flat_rows, w_gate, preferred_element_type=jnp.float32)
    up_value = jnp.dot(flat_rows, w_up, preferred_element_type=jnp.float32)
    gate_value, up_value = (
        lax.psum(gate_value.astype(jnp.bfloat16), "tp").astype(jnp.float32),
        lax.psum(up_value.astype(jnp.bfloat16), "tp").astype(jnp.float32),
    )
    hidden = (jax.nn.silu(gate_value) * up_value).astype(jnp.bfloat16)
    answer = jnp.dot(hidden, w_down, preferred_element_type=jnp.float32).astype(jnp.bfloat16)
    answer = answer.reshape(sources, item_count, half_width)
    returned = lax.all_to_all(answer, "ctx", split_axis=0, concat_axis=0, tiled=True)
    reply_width = returned.shape[2]
    merged = jnp.sum(
        returned.astype(jnp.float32).reshape(EXPERTS, members, CAP, reply_width), axis=1
    )
    merged = merged.reshape(slot_total, reply_width)
    moe_rows = jnp.dot(combine_weights, merged, precision=lax.Precision.HIGHEST)
    moe_piece = lax.psum_scatter(
        moe_rows.astype(jnp.bfloat16), "exp", scatter_dimension=1, tiled=True
    ).astype(jnp.float32)
    own_stream = lax.dynamic_slice_in_dim(
        stream_wide, tp_index * half_width + exp_index * piece_width, piece_width, 1
    )
    return (own_stream + moe_piece).astype(jnp.bfloat16)


LOG2E = 1.4426950408889634
HOLD = 3.0
HOLD_B = 5.0
ORDER = 5.0
AXES = ("ctx", "exp", "tp")
f32 = jnp.float32
bf16 = jnp.bfloat16


def lanes_to_rows(store_ref, value):
    rows, width = value.shape
    count = width // 128
    for k in range(count):
        store_ref[pl.ds(k, rows, stride=count), :] = value[:, k * 128 : (k + 1) * 128]


def scan_kernel(
    b_ref, c_ref, dt_ref, conv_ref, z_ref, alog_ref, skip_ref,
    base_ref, cum_ref, silu_ref, rate_ref, pack_ref, step_s, in_s, z_s, alog_s,
):
    tokens, width = dt_ref.shape
    states = alog_ref.shape[0]
    g = width // 128
    lanes_to_rows(step_s, jax.nn.softplus(dt_ref[...]))
    lanes_to_rows(in_s, conv_ref[...].astype(f32))
    lanes_to_rows(z_s, z_ref[...].astype(f32))
    lanes_to_rows(alog_s, alog_ref[...])
    rate_ref[...] = -jnp.exp(alog_s[...]) * LOG2E
    skip = skip_ref[...]

    def advance(t, carry):
        state, cum = carry
        rows = pl.ds(pl.multiple_of(t * g, g), g)
        step = step_s[rows, :]
        inp = in_s[rows, :]
        drive = step * inp
        out = skip * inp
        after = []
        for n in range(states):
            now = jnp.exp2(step * rate_ref[n * g : (n + 1) * g, :]) * state[n] + b_ref[n, t] * drive
            out = out + c_ref[n, t] * now
            after.append(now)
        cum = cum + step
        base_ref[rows, :] = out
        cum_ref[rows, :] = cum
        return (tuple(after), cum)

    zero = jnp.zeros((g, 128), f32)
    state, cum = lax.fori_loop(0, tokens, advance, ((zero,) * states, zero), unroll=2)
    z = z_s[...]
    silu_ref[...] = z / (1.0 + jnp.exp(-z))
    pack_ref[...] = jnp.concatenate(list(state) + [cum, zero], axis=0).astype(bf16)


def spread_kernel(c_ref, base_ref, cum_ref, silu_ref, rate_ref, out_ref, weight_ref):
    states = c_ref.shape[0]
    g = rate_ref.shape[0] // states
    tokens = base_ref.shape[0] // g
    out_ref[...] = base_ref[...] * silu_ref[...]

    def one(t, _):
        rows = pl.ds(pl.multiple_of(t * g, g), g)
        cum, silu = cum_ref[rows, :], silu_ref[rows, :]
        for n in range(states):
            weight_ref[pl.ds(pl.multiple_of(t * (g * states) + n * g, g), g), :] = (
                jnp.exp2(cum * rate_ref[n * g : (n + 1) * g, :]) * (c_ref[n, t] * silu)
            )
        return 0

    lax.fori_loop(0, tokens, one, 0, unroll=2)


def correct_kernel(one_ref, two_ref, three_ref, base_ref, weight_ref, rate_ref, out_ref, gated_s):
    tokens, width = out_ref.shape
    g = width // 128
    states = rate_ref.shape[0] // g
    top = states * g

    def halves(ref):
        both = ref[...].astype(f32)
        return both[:top].reshape(states, g, 128), both[top : top + g]

    rate = rate_ref[...].reshape(states, g, 128)
    ctx = lax.axis_index("ctx")
    s1, c1 = halves(one_ref)
    s2, c2 = halves(two_ref)
    s3, c3 = halves(three_ref)
    near, near_sum = jnp.where(ctx == 2, s3, s1), jnp.where(ctx == 2, c3, c1)
    far = jnp.where(ctx == 3, s3, 0.0)
    middle = s2 + jnp.exp2(c2[None] * rate) * far
    entering = near + jnp.exp2(near_sum[None] * rate) * jnp.where(ctx >= 2, middle, 0.0)
    entering = jnp.where(ctx == 0, 0.0, entering)

    def one(t, _):
        rows = pl.ds(pl.multiple_of(t * g, g), g)
        out = base_ref[rows, :]
        for n in range(states):
            out = out + weight_ref[pl.ds(pl.multiple_of(t * (g * states) + n * g, g), g), :] * entering[n]
        gated_s[rows, :] = out
        return 0

    lax.fori_loop(0, tokens, one, 0, unroll=4)
    for k in range(g):
        out_ref[:, k * 128 : (k + 1) * 128] = gated_s[pl.ds(k, tokens, stride=g), :].astype(bf16)


def route_kernel(ids_ref, lanes_ref, cols_ref):
    count = cols_ref.shape[0]
    ids = ids_ref[...].astype(f32)
    first, second = ids[0:1, :], ids[1:2, :]
    expert = lax.broadcasted_iota(jnp.int32, (8, count), 0).astype(f32)
    member = (jnp.where(expert == first, 1.0, 0.0) + jnp.where(expert == second, 1.0, 0.0)).astype(bf16)
    before = lax.broadcasted_iota(jnp.int32, (count, count), 0)
    token = lax.broadcasted_iota(jnp.int32, (count, count), 1)
    rank = jnp.dot(member, jnp.where(before < token, 1.0, 0.0).astype(bf16), preferred_element_type=f32)
    slot = [
        which * CAP + jnp.sum(jnp.where(expert == which, rank, 0.0), axis=0, keepdims=True) for which in (first, second)
    ]
    both = jnp.where(expert == 0, slot[0], jnp.where(expert == 1, slot[1], 0.0))
    lanes_ref[...] = both
    same = lax.broadcasted_iota(jnp.int32, (8, 128), 0) == lax.broadcasted_iota(jnp.int32, (8, 128), 1)
    cols_ref[...] = lax.dot_general(
        both.astype(bf16), jnp.where(same, 1.0, 0.0).astype(bf16), (((0,), (0,)), ((), ())), preferred_element_type=f32
    ).astype(bf16)


def pack_kernel(own_ref, peer_ref, resid_ref, slots_ref, m0_ref, m1_ref, m2_ref, m3_ref):
    ctx, exp = lax.axis_index("ctx"), lax.axis_index("exp")
    width = own_ref.shape[1]
    part = m0_ref.shape[1] - 2 * width - 128
    for p, ref in enumerate((m0_ref, m1_ref, m2_ref, m3_ref)):
        ref[:, :width] = own_ref[...]
        ref[:, width : 2 * width] = peer_ref[...]
        begin = pl.multiple_of((ctx ^ p) * 2 * part + exp * part, 128)
        ref[:, 2 * width : 2 * width + part] = resid_ref[:, pl.ds(begin, part)]
        ref[:, 2 * width + part :] = slots_ref[...]


def hold_out_kernel(own_ref, peer_ref, after_ref, out_ref, sems):
    half = own_ref.shape[0]
    copies = [
        pltpu.make_async_copy(ref, out_ref.at[pl.ds(k * half, half)], sems.at[k]) for k, ref in enumerate((own_ref, peer_ref))
    ]
    for copy in copies:
        copy.start()
    for copy in copies:
        copy.wait()


def after_kernel(earlier_ref, token_ref):
    token_ref[...] = jnp.zeros_like(token_ref)


def place_pair(scratch, odd, first, second):
    rows = first.shape[0]
    scratch[pl.ds(pl.multiple_of(odd * rows, rows), rows), :] = first
    scratch[pl.ds(pl.multiple_of((1 - odd) * rows, rows), rows), :] = second


def project_kernel(first_ref, second_ref, w_ref, after_ref, out_ref, slots_ref, rows_s):
    place_pair(rows_s, lax.axis_index("ctx") % 2, first_ref[...], second_ref[...])
    exp = lax.axis_index("exp")
    depth = w_ref.shape[0]
    part = out_ref.shape[1] // 2
    resid = rows_s[:, depth : depth + part].astype(f32)
    feats = rows_s[:, :depth]
    for side in range(2):
        value = jnp.dot(feats, w_ref[:, side * part : (side + 1) * part], preferred_element_type=f32)
        out_ref[:, side * part : (side + 1) * part] = (value + jnp.where(exp == side, resid, 0.0)).astype(bf16)
    slots_ref[...] = rows_s[:, depth + part :]


def select_kernel(
    own_ref, peer_ref, slots_ref, after_ref, stream_first_ref, stream_second_ref, d0_ref, d1_ref, d2_ref, d3_ref, rows_s
):
    ctx = lax.axis_index("ctx")
    odd = ctx % 2
    block = stream_first_ref.shape[0]
    rows_s[...] = (own_ref[...].astype(f32) + peer_ref[...].astype(f32)).astype(bf16)
    stream_first_ref[...] = rows_s[pl.ds(pl.multiple_of(odd * block, block), block), :]
    stream_second_ref[...] = rows_s[pl.ds(pl.multiple_of((1 - odd) * block, block), block), :]
    feats = rows_s[...]
    slots = slots_ref[...].astype(f32).T
    count = d0_ref.shape[0]
    row = lax.broadcasted_iota(jnp.int32, (count, 2 * block), 0)
    lane = lax.broadcasted_iota(jnp.int32, (count, 2 * block), 1)
    late = row >= CAP
    mine = late == (lane >= block)
    want = jnp.where(late, row - CAP, row).astype(f32)
    for p, ref in enumerate((d0_ref, d1_ref, d2_ref, d3_ref)):
        base = ((ctx ^ p) * CAP).astype(f32)
        hit = mine & ((slots[0:1, :] == want + base) | (slots[1:2, :] == want + base))
        pick = jnp.where(hit, 1.0, 0.0).astype(bf16)
        ref[...] = jnp.dot(pick, feats, preferred_element_type=f32).astype(bf16)


def part_copy(source_ref, begin, held_ref, place, sem, rows=None):
    height, cols = source_ref.shape[0], held_ref.shape[1]
    first, count = rows or (0, height)
    return pltpu.make_async_copy(
        source_ref.at[pl.ds(first, count), pl.ds(begin, cols)], held_ref.at[pl.ds(place * height + first, count)], sem
    )


def wait_all(copies):
    for copy in copies:
        copy.start()
    for copy in copies:
        copy.wait()


def hold_early_kernel(gate_ref, up_ref, after_ref, token_ref, held_ref, sems):
    token_ref[...] = jnp.zeros_like(token_ref)
    rows = up_ref.shape[0] // 2
    wait_all([part_copy(gate_ref, 0, held_ref, 0, sems.at[0]), part_copy(up_ref, 0, held_ref, 1, sems.at[1], (0, rows))])


def hold_late_kernel(gate_ref, up_ref, after_ref, held_second_ref, held_ref, sems):
    rows = up_ref.shape[0] // 2
    wait_all([
        part_copy(up_ref, 0, held_ref, 1, sems.at[0], (rows, rows)),
        part_copy(gate_ref, held_ref.shape[1], held_second_ref, 0, sems.at[1]),
    ])


def gate_up(feats, held_ref, out_ref):
    depth = feats.shape[1]
    width = held_ref.shape[1]
    block = min(512, width)
    for k in range(2):
        for n in range(0, width, block):
            out_ref[:, k * width + n : k * width + n + block] = jnp.dot(
                feats, held_ref[k * depth : (k + 1) * depth, n : n + block], preferred_element_type=f32
            ).astype(bf16)


def first_half_kernel(
    a0_ref, a1_ref, a2_ref, a3_ref, b0_ref, b1_ref, b2_ref, b3_ref, gain_ref, wu_ref,
    out_ref, feats_ref, held_ref, held_second_ref, squares_s, sem,
):
    begin = held_ref.shape[1]
    copy = part_copy(wu_ref, begin, held_second_ref, 1, sem)
    copy.start()
    expert = lax.axis_index("ctx")
    tp = lax.axis_index("tp")
    here = expert // 2 == tp
    count, width = a0_ref.shape

    def put(group, near_ref, far_ref):
        rows = pl.ds(pl.multiple_of((tp ^ group) * count, count), count)
        squares = jnp.zeros((count, 1), f32)
        for side, ref in ((expert % 2, near_ref), (1 - expert % 2, far_ref)):
            cols = pl.ds(pl.multiple_of(side * width, width), width)
            wide = ref[...].astype(f32)
            squares = squares + jnp.sum(wide * wide, axis=1, keepdims=True)
            feats_ref[rows, cols] = (wide * gain_ref[:, pl.ds(pl.multiple_of(tp * 2 * width + side * width, width), width)]).astype(bf16)
        squares_s[rows, :] = jnp.broadcast_to(squares, (count, 128))

    @pl.when(here)
    def _():
        put(0, a0_ref, a1_ref)
        put(1, b0_ref, b1_ref)

    @pl.when(jnp.logical_not(here))
    def _():
        put(0, a2_ref, a3_ref)
        put(1, b2_ref, b3_ref)

    squares = squares_s[...]
    high = squares.astype(bf16).astype(f32)
    lane = lax.broadcasted_iota(jnp.int32, squares.shape, 1)
    out_ref[:, 2 * begin :] = jnp.where(lane == 0, high, jnp.where(lane == 1, squares - high, 0.0)).astype(bf16)
    gate_up(feats_ref[...], held_ref, out_ref)
    copy.wait()


def second_half_kernel(feats_ref, wd_ref, out_ref, down_ref, held_ref, sem):
    copy = pltpu.make_async_copy(wd_ref, down_ref, sem)
    copy.start()
    gate_up(feats_ref[...], held_ref, out_ref)
    copy.wait()


def scale_of(own_ref, peer_ref, features):
    width = own_ref.shape[1]
    total = own_ref[:, width - 128 :].astype(f32) + peer_ref[:, width - 128 :].astype(f32)
    scale = lax.rsqrt((total[:, 0:1] + total[:, 1:2]) * (1.0 / features) + 1e-06)
    return jnp.broadcast_to(scale, total.shape)


def hidden_of(own_ref, peer_ref, scale):
    width = own_ref.shape[1] // 256 * 128
    gate = (own_ref[:, :width].astype(f32) + peer_ref[:, :width].astype(f32)) * scale
    up = (own_ref[:, width : 2 * width].astype(f32) + peer_ref[:, width : 2 * width].astype(f32)) * scale
    return (gate / (1.0 + jnp.exp(-gate)) * up).astype(bf16)


def down_first_kernel(features, own_ref, peer_ref, held_ref, out_ref, scale_ref):
    scale_ref[...] = scale_of(own_ref, peer_ref, features)
    hidden = hidden_of(own_ref, peer_ref, scale_ref[:, 0:1])
    depth = hidden.shape[1]
    block = min(512, out_ref.shape[1])
    for n in range(0, out_ref.shape[1], block):
        out_ref[:, n : n + block] = jnp.dot(hidden, held_ref[:depth, n : n + block], preferred_element_type=f32)


def down_piece(hidden, held_ref, acc_ref, near_ref, far_ref, sum_s, piece):
    depth = hidden.shape[1]
    count, width = near_ref.shape
    cols = pl.ds(pl.multiple_of(piece * width, width), width)
    sum_s[...] = acc_ref[:, cols] + jnp.dot(hidden, held_ref[depth:, cols], preferred_element_type=f32)
    pair = lax.axis_index("ctx") // 2
    near_ref[...] = sum_s[pl.ds(pl.multiple_of(pair * count, count), count), :].astype(bf16)
    far_ref[...] = sum_s[pl.ds(pl.multiple_of((1 - pair) * count, count), count), :].astype(bf16)


def down_theirs_kernel(
    own_ref, peer_ref, scale_ref, held_ref, acc_ref, near_ref, far_ref, hidden_ref, sum_s
):
    hidden_ref[...] = hidden_of(own_ref, peer_ref, scale_ref[:, 0:1])
    down_piece(hidden_ref[...], held_ref, acc_ref, near_ref, far_ref, sum_s, 1 - lax.axis_index("exp"))


def down_mine_kernel(hidden_ref, held_ref, acc_ref, near_ref, far_ref, sum_s):
    down_piece(hidden_ref[...], held_ref, acc_ref, near_ref, far_ref, sum_s, lax.axis_index("exp"))


def reply_kernel(own_ref, peer_ref, first_ref, second_ref, sum_s):
    odd = lax.axis_index("ctx") % 2
    sum_s[...] = own_ref[...].astype(f32) + peer_ref[...].astype(f32)
    count = first_ref.shape[0]
    for place, ref in ((odd, first_ref), (1 - odd, second_ref)):
        ref[...] = sum_s[pl.ds(pl.multiple_of(place * count, 8), count), :].astype(bf16)


def finish_kernel(
    s0_ref, s1_ref, s2_ref, s3_ref, slots_ref, weights_ref, r0_ref, r1_ref, r2_ref, r3_ref, out_ref
):
    ctx = lax.axis_index("ctx")
    apart = ctx ^ (lax.axis_index("tp") * lax.axis_size("exp") + lax.axis_index("exp"))
    tokens = out_ref.shape[0]
    stream = s0_ref[...]
    for p, ref in ((1, s1_ref), (2, s2_ref), (3, s3_ref)):
        stream = jnp.where(apart == p, ref[...], stream)
    total = stream.astype(f32)
    over_rows = (((0,), (0,)), ((), ()))
    want = lax.broadcasted_iota(jnp.int32, (r0_ref.shape[0], tokens), 0).astype(f32)
    for p, ref in enumerate((r0_ref, r1_ref, r2_ref, r3_ref)):
        base = ((ctx ^ p) * CAP).astype(f32)
        weight = jnp.zeros(want.shape, f32)
        for k in range(2):
            weight = weight + jnp.where(slots_ref[k : k + 1, :] == want + base, weights_ref[k : k + 1, :], 0.0)
        high = weight.astype(bf16)
        low = (weight - high.astype(f32)).astype(bf16)
        rows = ref[...]
        total = total + lax.dot_general(high, rows, over_rows, preferred_element_type=f32)
        total = total + lax.dot_general(low, rows, over_rows, preferred_element_type=f32)
    out_ref[...] = total.astype(bf16)


VM = pl.BlockSpec(memory_space=pltpu.VMEM)
SM = pl.BlockSpec(memory_space=pltpu.SMEM)
HB = pl.BlockSpec(memory_space=pltpu.HBM)
AN = pl.BlockSpec(memory_space=pl.ANY)


def call(kernel, out, ins, scratch=(), args=(), limit=8, us=0.0, keep=(), show=False):
    single = not isinstance(out, tuple)
    outs = (out,) if single else out
    first, last = len(ins), len(ins) + len(keep)

    def body_kernel(*refs):
        results = refs[last : last + len(outs) + (len(keep) if show else 0)]
        kernel(*refs[:first], *results, *refs[last + len(outs) + len(keep) :])

    result = pl.pallas_call(
        body_kernel,
        out_shape=outs + tuple(pltpu.VMEM(x.shape, x.dtype) for x in keep),
        in_specs=[*ins, *[VM] * len(keep)],
        out_specs=(VM,) * (len(outs) + len(keep)),
        scratch_shapes=list(scratch),
        input_output_aliases={first + k: len(outs) + k for k in range(len(keep))},
        compiler_params=pltpu.CompilerParams(vmem_limit_bytes=limit * 1024 * 1024),
        cost_estimate=pl.CostEstimate(flops=int(us * 1.0e9), transcendentals=0, bytes_accessed=0),
    )(*args, *[in_vmem(x) for x in keep])
    return result[0] if single and not keep else result


def shape(rows, cols, kind):
    return jax.ShapeDtypeStruct((rows, cols), kind)


def in_hbm(x):
    return pltpu.with_memory_space_constraint(x, pltpu.HBM)


def in_vmem(x):
    return pltpu.with_memory_space_constraint(x, pltpu.VMEM)


def fast_body(
    resid, conv_out, gate_z, dt_raw, b_proj, c_proj, a_log, d_skip, out_weight, norm_gain,
    route_ids, route_weight, w_gate, w_up, w_down,
):
    tokens, model_width = resid.shape
    ctx_count, exp_count, tp_count = (lax.axis_size(a) for a in AXES)
    ctx = lax.axis_index("ctx")
    channels = conv_out.shape[1]
    states = a_log.shape[0]
    block_cols = out_weight.shape[1]
    half_width = model_width // tp_count
    piece_width = half_width // exp_count
    g = channels // 128

    def number(c, x, t):
        return (c * exp_count + x) * tp_count + t

    def owner(c):
        return c // (ctx_count // tp_count)

    chips = [(c, x) for c in range(ctx_count) for x in range(exp_count)]
    away = range(1, ctx_count)

    def permute(x, pairs):
        return lax.ppermute(x, AXES, pairs)

    def to_owner(x, p):
        return permute(x, [(number(c ^ p, e, owner(c)), number(c, e, owner(c))) for c, e in chips])

    def from_owner(x, p):
        return permute(x, [(number(c, e, owner(c)), number(c ^ p, e, owner(c))) for c, e in chips])

    def swap_tp(x):
        return lax.ppermute(x, "tp", [(i, tp_count - 1 - i) for i in range(tp_count)])

    peer_weight = swap_tp(out_weight)
    with jax.named_scope("scan"):
        flat = shape(tokens * g, 128, f32)
        b_rows, c_rows = b_proj.T, c_proj.T
        base, cum, silu_z, rate, pack = call(
            scan_kernel,
            (flat, flat, flat, shape(states * g, 128, f32), shape((states + 2) * g, 128, bf16)),
            [SM, SM] + [VM] * 5,
            [pltpu.VMEM((tokens * g, 128), f32)] * 3 + [pltpu.VMEM((states * g, 128), f32)],
            tuple(in_hbm(v) for v in (b_rows, c_rows, dt_raw, conv_out, gate_z, a_log, d_skip.reshape(g, 128))),
        )
    with jax.named_scope("relay"):
        entered = [
            permute(pack, [(number(c, x, t), number(c ^ p, x, t)) for c, x in chips for t in range(tp_count)])
            for p in away
        ]
    with jax.named_scope("spread"):
        base, spread = call(
            spread_kernel, (flat, shape(tokens * states * g, 128, f32)), [SM] + [VM] * 4, (),
            (in_hbm(c_rows), base, cum, silu_z, rate), us=2.0,
        )
    with jax.named_scope("correct"):
        gated = call(
            correct_kernel, shape(tokens, channels, bf16), [VM] * 6, [pltpu.VMEM((tokens * g, 128), f32)],
            (*entered, base, spread, rate),
        )
    gated, route_ids = lax.optimization_barrier((gated, route_ids))
    with jax.named_scope("gather_gated"):
        peer_gated = swap_tp(gated)
    gain = norm_gain[None, :]
    with jax.named_scope("route"):
        slot_lanes, slot_cols = call(
            route_kernel, (shape(8, tokens, f32), shape(tokens, 128, bf16)), [VM], (), (in_hbm(route_ids.T),)
        )
    with jax.named_scope("gather_gated"):
        message = shape(tokens, 2 * channels + block_cols // 2 + 128, bf16)
        messages = call(
            pack_kernel, (message,) * 4, [VM] * 4, (), (gated, peer_gated, in_hbm(resid), slot_cols)
        )
        blocks = [messages[0]] + [to_owner(messages[p], p) for p in away]

    token_kind = shape(8, 128, f32)
    with jax.named_scope("hold_out_weight"):
        held_out = call(
            hold_out_kernel, pltpu.VMEM((2 * out_weight.shape[0], block_cols), bf16), [HB, AN, AN],
            [pltpu.SemaphoreType.DMA((2,))], (in_hbm(out_weight), peer_weight, messages[0]),
        )
    slots_total = EXPERTS * CAP
    part_width = w_gate.shape[1] // 2
    wg, wu, wd = (in_hbm(v) for v in (w_gate, w_up, w_down))
    dma = pltpu.SemaphoreType.DMA
    held_kind = pltpu.VMEM((2 * half_width, part_width), bf16)

    def project(first, second, token, keep):
        with jax.named_scope("project"):
            return call(
                project_kernel, (shape(2 * tokens, block_cols, bf16), shape(2 * tokens, 128, bf16)), [VM] * 3 + [AN],
                [pltpu.VMEM((2 * tokens, message.shape[1]), bf16)], (first, second, in_vmem(held_out), token), keep=keep,
            )

    def sum_exp(own):
        with jax.named_scope("sum_exp"):
            return permute(own, [(number(c, x, owner(c)), number(c, 1 - x, owner(c))) for c, x in chips])

    def select(own, peer, slots, token, keep):
        with jax.named_scope("select"):
            block = shape(tokens, block_cols, bf16)
            routed = shape(2 * CAP, block_cols, bf16)
            return call(
                select_kernel, (block, block) + (routed,) * 4, [VM] * 3 + [AN], [pltpu.VMEM((2 * tokens, block_cols), bf16)],
                (own, peer, slots, token), keep=keep,
            )

    def dispatch(out):
        with jax.named_scope("dispatch"):
            return [out[0]] + [from_owner(out[p], p) for p in away]

    own, slots, held_out = project(blocks[0], blocks[1], slot_lanes, (held_out,))
    peer = sum_exp(own)
    with jax.named_scope("hold_weights"):
        token, held = call(
            hold_early_kernel, (token_kind, held_kind), [HB, HB, AN], [dma((2,))], (wg, wu, own), us=HOLD
        )
    first, second, *out, held_out, held = select(own, peer, slots, token, (held_out, held))
    streams = [first, second]
    sent = [dispatch(out)]
    token = call(after_kernel, token_kind, [AN], (), (out[0],), us=ORDER)
    own, slots, held = project(blocks[2], blocks[3], token, (held,))
    peer = sum_exp(own)
    token = call(after_kernel, token_kind, [AN], (), (own,), us=ORDER)
    first, second, *out, held = select(own, peer, slots, token, (held,))
    streams += [first, second]
    sent.append(dispatch(out))
    with jax.named_scope("hold_weights"):
        held_second, held = call(
            hold_late_kernel, (held_kind,), [HB, HB, AN], [dma((2,))], (wg, wu, out[0]), us=HOLD, keep=(held,), show=True
        )
    with jax.named_scope("gate_up"):
        first, feats, held, held_second = call(
            first_half_kernel,
            (shape(slots_total, 2 * part_width + 128, bf16), shape(slots_total, half_width, bf16)),
            [VM] * 9 + [HB], [pltpu.VMEM((slots_total, 128), f32), dma],
            (*sent[0], *sent[1], in_hbm(gain), wu), keep=(held, held_second), show=True,
        )
        peer_first = swap_tp(first)
        second, held, _ = call(
            second_half_kernel, (shape(slots_total, 2 * part_width, bf16),), [VM, HB], [dma],
            (feats, wd), keep=(held, held_second), show=True,
        )
        peer_second = swap_tp(second)
    with jax.named_scope("down"):
        held = in_vmem(held)
        acc, scale = call(
            functools.partial(down_first_kernel, model_width),
            (shape(slots_total, half_width, f32), shape(slots_total, 128, f32)), [VM] * 3, (),
            (first, peer_first, held),
        )
        piece = shape(slots_total // 2, piece_width, bf16)
        total = pltpu.VMEM((slots_total, piece_width), f32)
        theirs_near, theirs_far, hidden = call(
            down_theirs_kernel, (piece, piece, shape(slots_total, part_width, bf16)),
            [VM] * 5, [total], (second, peer_second, scale, held, acc),
        )
    with jax.named_scope("sum_experts"):
        swap = [(0, 1), (1, 0)]
        peer_far = lax.ppermute(theirs_far, "exp", swap)
        theirs_near, _ = lax.optimization_barrier((theirs_near, theirs_far))
        peer_near = lax.ppermute(theirs_near, "exp", swap)
        mine_near, mine_far = call(down_mine_kernel, (piece, piece), [VM] * 3, [total], (hidden, held, acc))
    def reply(own, peer):
        small = shape(CAP, piece_width, bf16)
        return call(
            reply_kernel, (small, small), [VM] * 2, [pltpu.VMEM((slots_total // 2, piece_width), f32)], (own, peer)
        )

    def send(x, p):
        return permute(x, [(number(c, x_at, t), number(c ^ p, x_at, t)) for c, x_at in chips for t in range(tp_count)])

    def send_home(p, after):
        stream, _ = lax.optimization_barrier((streams[p], after))
        with jax.named_scope("stream_home"):
            return permute(
                stream,
                [(number(c, c % exp_count, owner(c)), number(c ^ p, c % exp_count, owner(c))) for c in range(ctx_count)],
            )

    with jax.named_scope("reply"):
        far_home = [send_home(p, mine_far) for p in (2, 3)]
        r2, r3 = reply(mine_far, peer_far)
        far = [send(r2, 2), send(r3, 3)]
        mine_near, peer_near, _ = lax.optimization_barrier((mine_near, peer_near, r2))
        r0, r1 = reply(mine_near, peer_near)
        replies = [r0, send(r1, 1), *far]
        home = [send_home(1, r1), *far_home]
    with jax.named_scope("finish"):
        return call(
            finish_kernel, shape(tokens, piece_width, bf16), [VM] * 10, (),
            (streams[0], *home, slot_lanes, route_weight.T, *replies),
        )


def solution(mesh):
    in_specs = (
        P(("groups", "ctx"), None),
        P(("groups", "ctx"), ("exp", "tp")),
        P(("groups", "ctx"), ("exp", "tp")),
        P(("groups", "ctx"), ("exp", "tp")),
        P(("groups", "ctx"), None),
        P(("groups", "ctx"), None),
        P(None, ("exp", "tp")),
        P(("exp", "tp")),
        P(("exp", "tp"), "ctx"),
        P(),
        P(("groups", "ctx"), None),
        P(("groups", "ctx"), None),
        P("tp", ("ctx", "exp")),
        P("tp", ("ctx", "exp")),
        P(("ctx", "exp"), "tp"),
    )
    out_specs = P(("groups", "ctx"), ("tp", "exp"))
    sizes = dict(mesh.shape)
    small = (sizes["ctx"], sizes["exp"], sizes["tp"]) == (EXPERTS, 2, 2)
    chosen = fast_body if small else body
    return jax.shard_map(chosen, mesh=mesh, in_specs=in_specs, out_specs=out_specs, check_vma=False)
```

```python
import functools

import jax
import jax.numpy as jnp
from jax import lax
from jax.experimental import pallas as pl
from jax.experimental.pallas import tpu as pltpu
from jax.sharding import PartitionSpec as P

EXPERTS = 4
CAP = 40


def shifted(x, axis, by):
    peers = lax.axis_size(axis)
    pairs = [(i, i + by) for i in range(peers) if 0 <= i + by < peers]
    return lax.ppermute(x, axis, pairs)


def body(
    resid,
    conv_out,
    gate_z,
    dt_raw,
    b_proj,
    c_proj,
    a_log,
    d_skip,
    out_weight,
    norm_gain,
    route_ids,
    route_weight,
    w_gate,
    w_up,
    w_down,
):
    tokens = resid.shape[0]
    model_width = resid.shape[1]
    ctx_count = lax.axis_size("ctx")
    exp_count = lax.axis_size("exp")
    tp_count = lax.axis_size("tp")
    half_width = model_width // tp_count
    piece_width = half_width // exp_count
    tp_index = lax.axis_index("tp")
    exp_index = lax.axis_index("exp")
    stride_amount = jax.nn.softplus(dt_raw)
    rate = -jnp.exp(a_log)
    inputs = conv_out.astype(jnp.float32)

    def advance(carry_state, column):
        step_now, b_now, c_now, in_now = column
        carry_state = (
            jnp.exp(step_now[None, :] * rate) * carry_state
            + step_now[None, :] * b_now[:, None] * in_now[None, :]
        )
        return (carry_state, jnp.sum(c_now[:, None] * carry_state, axis=0))

    last_state, scanned_local = lax.scan(
        advance,
        jnp.zeros(rate.shape, jnp.float32),
        (stride_amount, b_proj, c_proj, inputs),
        unroll=8,
    )
    cum_step = jnp.cumsum(stride_amount, axis=0)
    last_decay = jnp.exp(cum_step[-1][None, :] * rate)

    def relay_turn(turn_index, carry_state):
        return shifted(last_decay * carry_state + last_state, "ctx", 1)

    entering = lax.fori_loop(0, ctx_count - 1, relay_turn, jnp.zeros_like(last_state))
    carried = jnp.exp(cum_step[:, None, :] * rate[None, :, :])
    scanned = scanned_local + jnp.sum(c_proj[:, :, None] * carried * entering[None, :, :], axis=1)
    gated_out = (
        (scanned + d_skip[None, :] * inputs) * jax.nn.silu(gate_z.astype(jnp.float32))
    ).astype(jnp.bfloat16)
    partial_value = jnp.dot(
        gated_out,
        lax.all_gather(out_weight, "ctx", axis=1, tiled=True),
        preferred_element_type=jnp.float32,
    )
    mamba_out = lax.psum(partial_value, ("exp", "tp"))
    stream = (resid.astype(jnp.float32) + mamba_out).astype(jnp.bfloat16)
    stream_wide = stream.astype(jnp.float32)
    square_mean = jnp.mean(stream_wide * stream_wide, axis=1, keepdims=True)
    normed = (stream_wide * lax.rsqrt(square_mean + 1e-06) * norm_gain[None, :]).astype(
        jnp.bfloat16
    )
    half_feats = lax.dynamic_slice_in_dim(normed, tp_index * half_width, half_width, 1)
    slot_total = EXPERTS * CAP
    flat_ids = route_ids.reshape(-1)
    pair_count = flat_ids.shape[0]
    onehot = (flat_ids[:, None] == jnp.arange(EXPERTS, dtype=jnp.int32)[None, :]).astype(
        jnp.float32
    )
    pair_index = jnp.arange(pair_count, dtype=jnp.int32)
    earlier_mask = (pair_index[:, None] > pair_index[None, :]).astype(jnp.float32)
    before = jnp.dot(earlier_mask, onehot, precision=lax.Precision.HIGHEST)
    position = jnp.sum(before * onehot, axis=1).astype(jnp.int32)
    target = (flat_ids * CAP + position).reshape(tokens, 2)
    matches = jnp.arange(slot_total, dtype=jnp.int32)[None, :, None] == target[:, None, :]
    placement = jnp.any(matches, axis=2).astype(jnp.bfloat16)
    combine_weights = jnp.sum(jnp.where(matches, route_weight[:, None, :], 0.0), axis=2)
    members = ctx_count // EXPERTS
    outgoing = lax.dot_general(
        placement, half_feats, (((0,), (0,)), ((), ())), preferred_element_type=jnp.float32
    )
    outgoing = jnp.repeat(
        outgoing.astype(jnp.bfloat16).reshape(EXPERTS, CAP, half_width), members, axis=0
    )
    arrived = lax.all_to_all(outgoing, "ctx", split_axis=0, concat_axis=0, tiled=True)
    sources = arrived.shape[0]
    item_count = arrived.shape[1]
    flat_rows = arrived.reshape(sources * item_count, half_width)
    gate_value = jnp.dot(flat_rows, w_gate, preferred_element_type=jnp.float32)
    up_value = jnp.dot(flat_rows, w_up, preferred_element_type=jnp.float32)
    gate_value, up_value = (
        lax.psum(gate_value.astype(jnp.bfloat16), "tp").astype(jnp.float32),
        lax.psum(up_value.astype(jnp.bfloat16), "tp").astype(jnp.float32),
    )
    hidden = (jax.nn.silu(gate_value) * up_value).astype(jnp.bfloat16)
    answer = jnp.dot(hidden, w_down, preferred_element_type=jnp.float32).astype(jnp.bfloat16)
    answer = answer.reshape(sources, item_count, half_width)
    returned = lax.all_to_all(answer, "ctx", split_axis=0, concat_axis=0, tiled=True)
    reply_width = returned.shape[2]
    merged = jnp.sum(
        returned.astype(jnp.float32).reshape(EXPERTS, members, CAP, reply_width), axis=1
    )
    merged = merged.reshape(slot_total, reply_width)
    moe_rows = jnp.dot(combine_weights, merged, precision=lax.Precision.HIGHEST)
    moe_piece = lax.psum_scatter(
        moe_rows.astype(jnp.bfloat16), "exp", scatter_dimension=1, tiled=True
    ).astype(jnp.float32)
    own_stream = lax.dynamic_slice_in_dim(
        stream_wide, tp_index * half_width + exp_index * piece_width, piece_width, 1
    )
    return (own_stream + moe_piece).astype(jnp.bfloat16)


LOG2E = 1.4426950408889634
HOLD = 3.0
HOLD_B = 5.0
ORDER = 5.0
AXES = ("ctx", "exp", "tp")
f32 = jnp.float32
bf16 = jnp.bfloat16


def lanes_to_rows(store_ref, value):
    rows, width = value.shape
    count = width // 128
    for k in range(count):
        store_ref[pl.ds(k, rows, stride=count), :] = value[:, k * 128 : (k + 1) * 128]


def slots_of(ids, lanes):
    count = ids.shape[1]
    ids = ids.astype(f32)
    first, second = ids[0:1, :], ids[1:2, :]
    expert = lax.broadcasted_iota(jnp.int32, (8, count), 0).astype(f32)
    member = (jnp.where(expert == first, 1.0, 0.0) + jnp.where(expert == second, 1.0, 0.0)).astype(bf16)
    before = lax.broadcasted_iota(jnp.int32, (count, count), 0)
    token = lax.broadcasted_iota(jnp.int32, (count, count), 1)
    rank = jnp.dot(member, jnp.where(before < token, 1.0, 0.0).astype(bf16), preferred_element_type=f32)
    slot = [
        which * CAP + jnp.sum(jnp.where(expert == which, rank, 0.0), axis=0, keepdims=True) for which in (first, second)
    ]
    both = jnp.where(expert == 0, slot[0], jnp.where(expert == 1, slot[1], 0.0))
    row = lax.broadcasted_iota(jnp.int32, (count, lanes), 0)
    lane = lax.broadcasted_iota(jnp.int32, (count, lanes), 1)
    repeat = (row == lane) | (row + count == lane)
    return jnp.dot(both.astype(bf16), jnp.where(repeat, 1.0, 0.0).astype(bf16), preferred_element_type=f32)


def scan_kernel(
    b_ref, c_ref, dt_ref, conv_ref, z_ref, alog_ref, skip_ref, ids_ref,
    base_ref, cum_ref, silu_ref, rate_ref, pack_ref, step_s, in_s, z_s, alog_s,
):
    tokens, width = dt_ref.shape
    states = alog_ref.shape[0]
    g = width // 128
    lanes_to_rows(step_s, jax.nn.softplus(dt_ref[...]))
    lanes_to_rows(in_s, conv_ref[...].astype(f32))
    lanes_to_rows(z_s, z_ref[...].astype(f32))
    lanes_to_rows(alog_s, alog_ref[...])
    rate_ref[...] = -jnp.exp(alog_s[...]) * LOG2E
    skip = skip_ref[...]

    def advance(t, carry):
        state, cum = carry
        rows = pl.ds(pl.multiple_of(t * g, g), g)
        step = step_s[rows, :]
        inp = in_s[rows, :]
        drive = step * inp
        out = skip * inp
        after = []
        for n in range(states):
            now = jnp.exp2(step * rate_ref[n * g : (n + 1) * g, :]) * state[n] + b_ref[n, t] * drive
            out = out + c_ref[n, t] * now
            after.append(now)
        cum = cum + step
        base_ref[rows, :] = out
        cum_ref[rows, :] = cum
        return (tuple(after), cum)

    zero = jnp.zeros((g, 128), f32)
    state, cum = lax.fori_loop(0, tokens, advance, ((zero,) * states, zero), unroll=2)
    z = z_s[...]
    silu_ref[...] = z / (1.0 + jnp.exp(-z))
    pack_ref[...] = jnp.concatenate(list(state) + [cum, slots_of(ids_ref[...], 128)], axis=0).astype(bf16)


def spread_kernel(c_ref, base_ref, cum_ref, silu_ref, rate_ref, resid_ref, out_ref, weight_ref, near_ref, sem):
    states = c_ref.shape[0]
    g = rate_ref.shape[0] // states
    tokens = base_ref.shape[0] // g
    copy = pltpu.make_async_copy(resid_ref, near_ref, sem)
    copy.start()
    out_ref[...] = base_ref[...] * silu_ref[...]

    def one(t, _):
        rows = pl.ds(pl.multiple_of(t * g, g), g)
        cum, silu = cum_ref[rows, :], silu_ref[rows, :]
        for n in range(states):
            weight_ref[pl.ds(pl.multiple_of(t * (g * states) + n * g, g), g), :] = (
                jnp.exp2(cum * rate_ref[n * g : (n + 1) * g, :]) * (c_ref[n, t] * silu)
            )
        return 0

    lax.fori_loop(0, tokens, one, 0, unroll=2)
    copy.wait()


def correct_kernel(one_ref, two_ref, three_ref, base_ref, weight_ref, rate_ref, out_ref, gated_s):
    tokens, width = out_ref.shape
    g = width // 128
    states = rate_ref.shape[0] // g
    top = states * g

    def halves(ref):
        both = ref[...].astype(f32)
        return both[:top].reshape(states, g, 128), both[top : top + g]

    rate = rate_ref[...].reshape(states, g, 128)
    ctx = lax.axis_index("ctx")
    s1, c1 = halves(one_ref)
    s2, c2 = halves(two_ref)
    s3, c3 = halves(three_ref)
    near, near_sum = jnp.where(ctx == 2, s3, s1), jnp.where(ctx == 2, c3, c1)
    far = jnp.where(ctx == 3, s3, 0.0)
    middle = s2 + jnp.exp2(c2[None] * rate) * far
    entering = near + jnp.exp2(near_sum[None] * rate) * jnp.where(ctx >= 2, middle, 0.0)
    entering = jnp.where(ctx == 0, 0.0, entering)

    def one(t, _):
        rows = pl.ds(pl.multiple_of(t * g, g), g)
        out = base_ref[rows, :]
        for n in range(states):
            out = out + weight_ref[pl.ds(pl.multiple_of(t * (g * states) + n * g, g), g), :] * entering[n]
        gated_s[rows, :] = out
        return 0

    lax.fori_loop(0, tokens, one, 0, unroll=4)
    for k in range(g):
        out_ref[:, k * 128 : (k + 1) * 128] = gated_s[pl.ds(k, tokens, stride=g), :].astype(bf16)


def pack_kernel(own_ref, peer_ref, resid_ref, m0_ref, m1_ref, m2_ref, m3_ref):
    ctx, exp = lax.axis_index("ctx"), lax.axis_index("exp")
    width = own_ref.shape[1]
    part = m0_ref.shape[1] - 2 * width
    for p, ref in enumerate((m0_ref, m1_ref, m2_ref, m3_ref)):
        ref[:, :width] = own_ref[...]
        ref[:, width : 2 * width] = peer_ref[...]
        begin = pl.multiple_of((ctx ^ p) * 2 * part + exp * part, 128)
        ref[:, 2 * width :] = resid_ref[:, pl.ds(begin, part)]


def part_copy(source_ref, begin, held_ref, place, sem, rows=None):
    height, cols = source_ref.shape[0], held_ref.shape[1]
    first, count = rows or (0, height)
    return pltpu.make_async_copy(
        source_ref.at[pl.ds(first, count), pl.ds(begin, cols)], held_ref.at[pl.ds(place * height + first, count)], sem
    )


def wait_all(copies):
    for copy in copies:
        copy.start()
    for copy in copies:
        copy.wait()


def hold_out_kernel(own_ref, peer_ref, gate_ref, after_ref, out_ref, held_ref, sems):
    half = own_ref.shape[0]
    wait_all([
        *(
            pltpu.make_async_copy(ref, out_ref.at[pl.ds(k * half, half)], sems.at[k])
            for k, ref in enumerate((own_ref, peer_ref))
        ),
        part_copy(gate_ref, 0, held_ref, 0, sems.at[2], (0, gate_ref.shape[0] // 2)),
    ])


def after_kernel(earlier_ref, token_ref):
    token_ref[...] = jnp.zeros_like(token_ref)


def place_pair(scratch, odd, first, second):
    rows = first.shape[0]
    scratch[pl.ds(pl.multiple_of(odd * rows, rows), rows), :] = first
    scratch[pl.ds(pl.multiple_of((1 - odd) * rows, rows), rows), :] = second


def project_kernel(first_ref, second_ref, after_ref, out_ref, w_ref, held_ref, rows_s):
    place_pair(rows_s, lax.axis_index("ctx") % 2, first_ref[...], second_ref[...])
    exp = lax.axis_index("exp")
    depth = w_ref.shape[0]
    part = out_ref.shape[1] // 2
    resid = rows_s[:, depth : depth + part].astype(f32)
    feats = rows_s[:, :depth]
    for side in range(2):
        value = jnp.dot(feats, w_ref[:, side * part : (side + 1) * part], preferred_element_type=f32)
        out_ref[:, side * part : (side + 1) * part] = (value + jnp.where(exp == side, resid, 0.0)).astype(bf16)


def select_kernel(
    own_ref, peer_ref, first_ref, second_ref, after_ref, stream_first_ref, stream_second_ref, d0_ref, d1_ref, d2_ref, d3_ref, rows_s
):
    ctx = lax.axis_index("ctx")
    odd = ctx % 2
    block = stream_first_ref.shape[0]
    rows_s[...] = (own_ref[...].astype(f32) + peer_ref[...].astype(f32)).astype(bf16)
    stream_first_ref[...] = rows_s[pl.ds(pl.multiple_of(odd * block, block), block), :]
    stream_second_ref[...] = rows_s[pl.ds(pl.multiple_of((1 - odd) * block, block), block), :]
    feats = rows_s[...]
    top = first_ref.shape[0] - 16
    first, second = first_ref[top:, :].astype(f32), second_ref[top:, :].astype(f32)
    lane = lax.broadcasted_iota(jnp.int32, first.shape, 1)
    slots = jnp.where((lane >= block) == (odd == 0), second, first)
    count = d0_ref.shape[0]
    row = lax.broadcasted_iota(jnp.int32, (count, 2 * block), 0)
    lane = lax.broadcasted_iota(jnp.int32, (count, 2 * block), 1)
    late = row >= CAP
    mine = late == (lane >= block)
    want = jnp.where(late, row - CAP, row).astype(f32)
    for p, ref in enumerate((d0_ref, d1_ref, d2_ref, d3_ref)):
        base = ((ctx ^ p) * CAP).astype(f32)
        hit = mine & ((slots[8:9, :] == want + base) | (slots[9:10, :] == want + base))
        pick = jnp.where(hit, 1.0, 0.0).astype(bf16)
        ref[...] = jnp.dot(pick, feats, preferred_element_type=f32).astype(bf16)


def hold_early_kernel(gate_ref, up_ref, after_ref, token_ref, held_ref, sems):
    token_ref[...] = jnp.zeros_like(token_ref)
    rows = gate_ref.shape[0] // 2
    wait_all([part_copy(gate_ref, 0, held_ref, 0, sems.at[0], (rows, rows)), part_copy(up_ref, 0, held_ref, 1, sems.at[1])])


def hold_late_kernel(gate_ref, after_ref, held_second_ref, sem):
    wait_all([part_copy(gate_ref, held_second_ref.shape[1], held_second_ref, 0, sem)])


def gate_up(feats, held_ref, out_ref):
    depth = feats.shape[1]
    width = held_ref.shape[1]
    block = min(512, width)
    for k in range(2):
        for n in range(0, width, block):
            out_ref[:, k * width + n : k * width + n + block] = jnp.dot(
                feats, held_ref[k * depth : (k + 1) * depth, n : n + block], preferred_element_type=f32
            ).astype(bf16)


def first_half_kernel(
    a0_ref, a1_ref, a2_ref, a3_ref, b0_ref, b1_ref, b2_ref, b3_ref, gain_ref, wu_ref,
    out_ref, feats_ref, held_ref, held_second_ref, squares_s, sem,
):
    begin = held_ref.shape[1]
    copy = part_copy(wu_ref, begin, held_second_ref, 1, sem)
    copy.start()
    expert = lax.axis_index("ctx")
    tp = lax.axis_index("tp")
    here = expert // 2 == tp
    count, width = a0_ref.shape

    def put(group, near_ref, far_ref):
        rows = pl.ds(pl.multiple_of((tp ^ group) * count, count), count)
        squares = jnp.zeros((count, 1), f32)
        for side, ref in ((expert % 2, near_ref), (1 - expert % 2, far_ref)):
            cols = pl.ds(pl.multiple_of(side * width, width), width)
            wide = ref[...].astype(f32)
            squares = squares + jnp.sum(wide * wide, axis=1, keepdims=True)
            feats_ref[rows, cols] = (wide * gain_ref[:, pl.ds(pl.multiple_of(tp * 2 * width + side * width, width), width)]).astype(bf16)
        squares_s[rows, :] = jnp.broadcast_to(squares, (count, 128))

    @pl.when(here)
    def _():
        put(0, a0_ref, a1_ref)
        put(1, b0_ref, b1_ref)

    @pl.when(jnp.logical_not(here))
    def _():
        put(0, a2_ref, a3_ref)
        put(1, b2_ref, b3_ref)

    squares = squares_s[...]
    high = squares.astype(bf16).astype(f32)
    lane = lax.broadcasted_iota(jnp.int32, squares.shape, 1)
    out_ref[:, 2 * begin :] = jnp.where(lane == 0, high, jnp.where(lane == 1, squares - high, 0.0)).astype(bf16)
    gate_up(feats_ref[...], held_ref, out_ref)
    copy.wait()


def second_half_kernel(feats_ref, wd_ref, out_ref, down_ref, held_ref, sem):
    rows = wd_ref.shape[0] // 2
    copy = pltpu.make_async_copy(wd_ref.at[pl.ds(0, rows)], down_ref.at[pl.ds(0, rows)], sem)
    copy.start()
    gate_up(feats_ref[...], held_ref, out_ref)
    copy.wait()


def scale_of(own_ref, peer_ref, features):
    width = own_ref.shape[1]
    total = own_ref[:, width - 128 :].astype(f32) + peer_ref[:, width - 128 :].astype(f32)
    scale = lax.rsqrt((total[:, 0:1] + total[:, 1:2]) * (1.0 / features) + 1e-06)
    return jnp.broadcast_to(scale, total.shape)


def hidden_of(own_ref, peer_ref, scale):
    width = own_ref.shape[1] // 256 * 128
    gate = (own_ref[:, :width].astype(f32) + peer_ref[:, :width].astype(f32)) * scale
    up = (own_ref[:, width : 2 * width].astype(f32) + peer_ref[:, width : 2 * width].astype(f32)) * scale
    return (gate / (1.0 + jnp.exp(-gate)) * up).astype(bf16)


def down_first_kernel(features, own_ref, peer_ref, wd_ref, out_ref, scale_ref, held_ref, sem):
    rows = wd_ref.shape[0] // 2
    copy = pltpu.make_async_copy(wd_ref.at[pl.ds(rows, rows)], held_ref.at[pl.ds(rows, rows)], sem)
    copy.start()
    scale_ref[...] = scale_of(own_ref, peer_ref, features)
    hidden = hidden_of(own_ref, peer_ref, scale_ref[:, 0:1])
    depth = hidden.shape[1]
    block = min(512, out_ref.shape[1])
    for n in range(0, out_ref.shape[1], block):
        out_ref[:, n : n + block] = jnp.dot(hidden, held_ref[:depth, n : n + block], preferred_element_type=f32)
    copy.wait()


def down_piece(hidden, held_ref, acc_ref, near_ref, far_ref, sum_s, piece):
    depth = hidden.shape[1]
    count, width = near_ref.shape
    cols = pl.ds(pl.multiple_of(piece * width, width), width)
    sum_s[...] = acc_ref[:, cols] + jnp.dot(hidden, held_ref[depth:, cols], preferred_element_type=f32)
    pair = lax.axis_index("ctx") // 2
    near_ref[...] = sum_s[pl.ds(pl.multiple_of(pair * count, count), count), :].astype(bf16)
    far_ref[...] = sum_s[pl.ds(pl.multiple_of((1 - pair) * count, count), count), :].astype(bf16)


def down_theirs_kernel(own_ref, peer_ref, scale_ref, acc_ref, near_ref, far_ref, hidden_ref, held_ref, sum_s):
    hidden_ref[...] = hidden_of(own_ref, peer_ref, scale_ref[:, 0:1])
    down_piece(hidden_ref[...], held_ref, acc_ref, near_ref, far_ref, sum_s, 1 - lax.axis_index("exp"))


def down_mine_kernel(hidden_ref, acc_ref, near_ref, far_ref, held_ref, sum_s):
    down_piece(hidden_ref[...], held_ref, acc_ref, near_ref, far_ref, sum_s, lax.axis_index("exp"))


def reply_kernel(own_ref, peer_ref, first_ref, second_ref, sum_s):
    odd = lax.axis_index("ctx") % 2
    sum_s[...] = own_ref[...].astype(f32) + peer_ref[...].astype(f32)
    count = first_ref.shape[0]
    for place, ref in ((odd, first_ref), (1 - odd, second_ref)):
        ref[...] = sum_s[pl.ds(pl.multiple_of(place * count, 8), count), :].astype(bf16)


def finish_kernel(
    s0_ref, s1_ref, s2_ref, s3_ref, pack_ref, weights_ref, r0_ref, r1_ref, r2_ref, r3_ref, out_ref
):
    ctx = lax.axis_index("ctx")
    apart = ctx ^ (lax.axis_index("tp") * lax.axis_size("exp") + lax.axis_index("exp"))
    tokens = out_ref.shape[0]
    stream = s0_ref[...]
    for p, ref in ((1, s1_ref), (2, s2_ref), (3, s3_ref)):
        stream = jnp.where(apart == p, ref[...], stream)
    slots = pack_ref[pack_ref.shape[0] - 16 :, :].astype(f32)[8:10, :tokens]
    total = stream.astype(f32)
    over_rows = (((0,), (0,)), ((), ()))
    want = lax.broadcasted_iota(jnp.int32, (r0_ref.shape[0], tokens), 0).astype(f32)
    for p, ref in enumerate((r0_ref, r1_ref, r2_ref, r3_ref)):
        base = ((ctx ^ p) * CAP).astype(f32)
        weight = jnp.zeros(want.shape, f32)
        for k in range(2):
            weight = weight + jnp.where(slots[k : k + 1, :] == want + base, weights_ref[k : k + 1, :], 0.0)
        high = weight.astype(bf16)
        low = (weight - high.astype(f32)).astype(bf16)
        rows = ref[...]
        total = total + lax.dot_general(high, rows, over_rows, preferred_element_type=f32)
        total = total + lax.dot_general(low, rows, over_rows, preferred_element_type=f32)
    out_ref[...] = total.astype(bf16)


VM = pl.BlockSpec(memory_space=pltpu.VMEM)
SM = pl.BlockSpec(memory_space=pltpu.SMEM)
HB = pl.BlockSpec(memory_space=pltpu.HBM)
AN = pl.BlockSpec(memory_space=pl.ANY)


def call(kernel, out, ins, scratch=(), args=(), limit=8, us=0.0, keep=(), show=False):
    single = not isinstance(out, tuple)
    outs = (out,) if single else out
    first, last = len(ins), len(ins) + len(keep)

    def body_kernel(*refs):
        results = refs[last : last + len(outs) + (len(keep) if show else 0)]
        kernel(*refs[:first], *results, *refs[last + len(outs) + len(keep) :])

    result = pl.pallas_call(
        body_kernel,
        out_shape=outs + tuple(pltpu.VMEM(x.shape, x.dtype) for x in keep),
        in_specs=[*ins, *[VM] * len(keep)],
        out_specs=(VM,) * (len(outs) + len(keep)),
        scratch_shapes=list(scratch),
        input_output_aliases={first + k: len(outs) + k for k in range(len(keep))},
        compiler_params=pltpu.CompilerParams(vmem_limit_bytes=limit * 1024 * 1024),
        cost_estimate=pl.CostEstimate(flops=int(us * 1.0e9), transcendentals=0, bytes_accessed=0),
    )(*args, *[in_vmem(x) for x in keep])
    return result[0] if single and not keep else result


def shape(rows, cols, kind):
    return jax.ShapeDtypeStruct((rows, cols), kind)


def in_hbm(x):
    return pltpu.with_memory_space_constraint(x, pltpu.HBM)


def in_vmem(x):
    return pltpu.with_memory_space_constraint(x, pltpu.VMEM)


def fast_body(
    resid, conv_out, gate_z, dt_raw, b_proj, c_proj, a_log, d_skip, out_weight, norm_gain,
    route_ids, route_weight, w_gate, w_up, w_down,
):
    tokens, model_width = resid.shape
    ctx_count, exp_count, tp_count = (lax.axis_size(a) for a in AXES)
    ctx = lax.axis_index("ctx")
    channels = conv_out.shape[1]
    states = a_log.shape[0]
    block_cols = out_weight.shape[1]
    half_width = model_width // tp_count
    piece_width = half_width // exp_count
    g = channels // 128

    def number(c, x, t):
        return (c * exp_count + x) * tp_count + t

    def owner(c):
        return c // (ctx_count // tp_count)

    chips = [(c, x) for c in range(ctx_count) for x in range(exp_count)]
    away = range(1, ctx_count)

    def permute(x, pairs):
        return lax.ppermute(x, AXES, pairs)

    def to_owner(x, p):
        return permute(x, [(number(c ^ p, e, owner(c)), number(c, e, owner(c))) for c, e in chips])

    def from_owner(x, p):
        return permute(x, [(number(c, e, owner(c)), number(c ^ p, e, owner(c))) for c, e in chips])

    def swap_tp(x):
        return lax.ppermute(x, "tp", [(i, tp_count - 1 - i) for i in range(tp_count)])

    with jax.named_scope("scan"):
        flat = shape(tokens * g, 128, f32)
        b_rows, c_rows = b_proj.T, c_proj.T
        base, cum, silu_z, rate, pack = call(
            scan_kernel,
            (flat, flat, flat, shape(states * g, 128, f32), shape((states + 2) * g, 128, bf16)),
            [SM, SM] + [VM] * 6,
            [pltpu.VMEM((tokens * g, 128), f32)] * 3 + [pltpu.VMEM((states * g, 128), f32)],
            tuple(in_hbm(v) for v in (b_rows, c_rows, dt_raw, conv_out, gate_z, a_log, d_skip.reshape(g, 128), route_ids.T)),
        )
    peer_weight, _ = lax.optimization_barrier((out_weight, pack))
    peer_weight = swap_tp(peer_weight)
    with jax.named_scope("relay"):
        entered = [
            permute(pack, [(number(c, x, t), number(c ^ p, x, t)) for c, x in chips for t in range(tp_count)])
            for p in away
        ]
    with jax.named_scope("spread"):
        base, spread, resid = call(
            spread_kernel, (flat, shape(tokens * states * g, 128, f32), pltpu.VMEM(resid.shape, bf16)), [SM] + [VM] * 4 + [HB],
            [pltpu.SemaphoreType.DMA], (in_hbm(c_rows), base, cum, silu_z, rate, in_hbm(resid)), us=2.0,
        )
    with jax.named_scope("correct"):
        gated = call(
            correct_kernel, shape(tokens, channels, bf16), [VM] * 6, [pltpu.VMEM((tokens * g, 128), f32)],
            (*entered, base, spread, rate),
        )
    with jax.named_scope("gather_gated"):
        peer_gated = swap_tp(gated)
    gain = norm_gain[None, :]
    with jax.named_scope("gather_gated"):
        message = shape(tokens, 2 * channels + block_cols // 2, bf16)
        messages = call(
            pack_kernel, (message,) * 4, [VM] * 3, (), (gated, peer_gated, in_vmem(resid))
        )
        blocks = [messages[0]] + [to_owner(messages[p], p) for p in away]

    token_kind = shape(8, 128, f32)
    slots_total = EXPERTS * CAP
    part_width = w_gate.shape[1] // 2
    wg, wu, wd = (in_hbm(v) for v in (w_gate, w_up, w_down))
    dma = pltpu.SemaphoreType.DMA
    held_kind = pltpu.VMEM((2 * half_width, part_width), bf16)
    with jax.named_scope("hold_out_weight"):
        held_out, held = call(
            hold_out_kernel, (pltpu.VMEM((2 * out_weight.shape[0], block_cols), bf16), held_kind), [HB, AN, HB, AN],
            [dma((3,))], (in_hbm(out_weight), peer_weight, wg, messages[0]),
        )

    def project(first, second, token, keep):
        with jax.named_scope("project"):
            return call(
                project_kernel, (shape(2 * tokens, block_cols, bf16),), [VM] * 2 + [AN],
                [pltpu.VMEM((2 * tokens, message.shape[1]), bf16)], (first, second, token), keep=keep, show=True,
            )

    def sum_exp(own):
        with jax.named_scope("sum_exp"):
            return permute(own, [(number(c, x, owner(c)), number(c, 1 - x, owner(c))) for c, x in chips])

    def select(own, peer, first, second, token, keep):
        with jax.named_scope("select"):
            block = shape(tokens, block_cols, bf16)
            routed = shape(2 * CAP, block_cols, bf16)
            return call(
                select_kernel, (block, block) + (routed,) * 4, [VM] * 4 + [AN], [pltpu.VMEM((2 * tokens, block_cols), bf16)],
                (own, peer, first, second, token), keep=keep,
            )

    def dispatch(out):
        with jax.named_scope("dispatch"):
            return [out[0]] + [from_owner(out[p], p) for p in away]

    own, held_out, held = project(blocks[0], blocks[1], pack, (held_out, held))
    peer = sum_exp(own)
    with jax.named_scope("hold_weights"):
        token, held = call(
            hold_early_kernel, (token_kind,), [HB, HB, AN], [dma((2,))], (wg, wu, own), us=HOLD, keep=(held,), show=True
        )
    first, second, *out, held_out, held = select(own, peer, pack, entered[0], token, (held_out, held))
    streams = [first, second]
    sent = [dispatch(out)]
    token = call(after_kernel, token_kind, [AN], (), (out[0],), us=ORDER)
    own, _, held = project(blocks[2], blocks[3], token, (held_out, held))
    peer = sum_exp(own)
    token = call(after_kernel, token_kind, [AN], (), (own,), us=ORDER)
    first, second, *out, held = select(own, peer, entered[1], entered[2], token, (held,))
    streams += [first, second]
    sent.append(dispatch(out))
    with jax.named_scope("hold_weights"):
        held_second, held = call(
            hold_late_kernel, (held_kind,), [HB, AN], [dma], (wg, out[0]), us=HOLD, keep=(held,)
        )
    with jax.named_scope("gate_up"):
        first, feats, held, held_second = call(
            first_half_kernel,
            (shape(slots_total, 2 * part_width + 128, bf16), shape(slots_total, half_width, bf16)),
            [VM] * 9 + [HB], [pltpu.VMEM((slots_total, 128), f32), dma],
            (*sent[0], *sent[1], in_hbm(gain), wu), keep=(held, held_second), show=True,
        )
        peer_first = swap_tp(first)
        second, held, _ = call(
            second_half_kernel, (shape(slots_total, 2 * part_width, bf16),), [VM, HB], [dma],
            (feats, wd), keep=(held, held_second), show=True,
        )
        peer_second = swap_tp(second)
    with jax.named_scope("down"):
        acc, scale, held = call(
            functools.partial(down_first_kernel, model_width),
            (shape(slots_total, half_width, f32), shape(slots_total, 128, f32)), [VM] * 2 + [HB], [dma],
            (first, peer_first, wd), keep=(held,), show=True,
        )
        piece = shape(slots_total // 2, piece_width, bf16)
        total = pltpu.VMEM((slots_total, piece_width), f32)
        theirs_near, theirs_far, hidden, held = call(
            down_theirs_kernel, (piece, piece, shape(slots_total, part_width, bf16)),
            [VM] * 4, [total], (second, peer_second, scale, acc), keep=(held,), show=True,
        )
    with jax.named_scope("sum_experts"):
        swap = [(0, 1), (1, 0)]
        peer_far = lax.ppermute(theirs_far, "exp", swap)
        theirs_near, _ = lax.optimization_barrier((theirs_near, theirs_far))
        peer_near = lax.ppermute(theirs_near, "exp", swap)
        mine_near, mine_far, _ = call(
            down_mine_kernel, (piece, piece), [VM] * 2, [total], (hidden, acc), keep=(held,), show=True
        )
    def reply(own, peer):
        small = shape(CAP, piece_width, bf16)
        return call(
            reply_kernel, (small, small), [VM] * 2, [pltpu.VMEM((slots_total // 2, piece_width), f32)], (own, peer)
        )

    def send(x, p):
        return permute(x, [(number(c, x_at, t), number(c ^ p, x_at, t)) for c, x_at in chips for t in range(tp_count)])

    def send_home(p, after):
        stream, _ = lax.optimization_barrier((streams[p], after))
        with jax.named_scope("stream_home"):
            return permute(
                stream,
                [(number(c, c % exp_count, owner(c)), number(c ^ p, c % exp_count, owner(c))) for c in range(ctx_count)],
            )

    with jax.named_scope("reply"):
        far_home = [send_home(p, mine_far) for p in (2, 3)]
        r2, r3 = reply(mine_far, peer_far)
        far = [send(r2, 2), send(r3, 3)]
        mine_near, peer_near, _ = lax.optimization_barrier((mine_near, peer_near, r2))
        r0, r1 = reply(mine_near, peer_near)
        replies = [r0, send(r1, 1), *far]
        home = [send_home(1, r1), *far_home]
    with jax.named_scope("finish"):
        return call(
            finish_kernel, shape(tokens, piece_width, bf16), [VM] * 10, (),
            (streams[0], *home, pack, route_weight.T, *replies),
        )


def solution(mesh):
    in_specs = (
        P(("groups", "ctx"), None),
        P(("groups", "ctx"), ("exp", "tp")),
        P(("groups", "ctx"), ("exp", "tp")),
        P(("groups", "ctx"), ("exp", "tp")),
        P(("groups", "ctx"), None),
        P(("groups", "ctx"), None),
        P(None, ("exp", "tp")),
        P(("exp", "tp")),
        P(("exp", "tp"), "ctx"),
        P(),
        P(("groups", "ctx"), None),
        P(("groups", "ctx"), None),
        P("tp", ("ctx", "exp")),
        P("tp", ("ctx", "exp")),
        P(("ctx", "exp"), "tp"),
    )
    out_specs = P(("groups", "ctx"), ("tp", "exp"))
    sizes = dict(mesh.shape)
    small = (sizes["ctx"], sizes["exp"], sizes["tp"]) == (EXPERTS, 2, 2)
    chosen = fast_body if small else body
    return jax.shard_map(chosen, mesh=mesh, in_specs=in_specs, out_specs=out_specs, check_vma=False)
```

```python
import functools

import jax
import jax.numpy as jnp
from jax import lax
from jax.experimental import pallas as pl
from jax.experimental.pallas import tpu as pltpu
from jax.sharding import PartitionSpec as P

EXPERTS = 4
CAP = 40


def shifted(x, axis, by):
    peers = lax.axis_size(axis)
    pairs = [(i, i + by) for i in range(peers) if 0 <= i + by < peers]
    return lax.ppermute(x, axis, pairs)


def body(
    resid,
    conv_out,
    gate_z,
    dt_raw,
    b_proj,
    c_proj,
    a_log,
    d_skip,
    out_weight,
    norm_gain,
    route_ids,
    route_weight,
    w_gate,
    w_up,
    w_down,
):
    tokens = resid.shape[0]
    model_width = resid.shape[1]
    ctx_count = lax.axis_size("ctx")
    exp_count = lax.axis_size("exp")
    tp_count = lax.axis_size("tp")
    half_width = model_width // tp_count
    piece_width = half_width // exp_count
    tp_index = lax.axis_index("tp")
    exp_index = lax.axis_index("exp")
    stride_amount = jax.nn.softplus(dt_raw)
    rate = -jnp.exp(a_log)
    inputs = conv_out.astype(jnp.float32)

    def advance(carry_state, column):
        step_now, b_now, c_now, in_now = column
        carry_state = (
            jnp.exp(step_now[None, :] * rate) * carry_state
            + step_now[None, :] * b_now[:, None] * in_now[None, :]
        )
        return (carry_state, jnp.sum(c_now[:, None] * carry_state, axis=0))

    last_state, scanned_local = lax.scan(
        advance,
        jnp.zeros(rate.shape, jnp.float32),
        (stride_amount, b_proj, c_proj, inputs),
        unroll=8,
    )
    cum_step = jnp.cumsum(stride_amount, axis=0)
    last_decay = jnp.exp(cum_step[-1][None, :] * rate)

    def relay_turn(turn_index, carry_state):
        return shifted(last_decay * carry_state + last_state, "ctx", 1)

    entering = lax.fori_loop(0, ctx_count - 1, relay_turn, jnp.zeros_like(last_state))
    carried = jnp.exp(cum_step[:, None, :] * rate[None, :, :])
    scanned = scanned_local + jnp.sum(c_proj[:, :, None] * carried * entering[None, :, :], axis=1)
    gated_out = (
        (scanned + d_skip[None, :] * inputs) * jax.nn.silu(gate_z.astype(jnp.float32))
    ).astype(jnp.bfloat16)
    partial_value = jnp.dot(
        gated_out,
        lax.all_gather(out_weight, "ctx", axis=1, tiled=True),
        preferred_element_type=jnp.float32,
    )
    mamba_out = lax.psum(partial_value, ("exp", "tp"))
    stream = (resid.astype(jnp.float32) + mamba_out).astype(jnp.bfloat16)
    stream_wide = stream.astype(jnp.float32)
    square_mean = jnp.mean(stream_wide * stream_wide, axis=1, keepdims=True)
    normed = (stream_wide * lax.rsqrt(square_mean + 1e-06) * norm_gain[None, :]).astype(
        jnp.bfloat16
    )
    half_feats = lax.dynamic_slice_in_dim(normed, tp_index * half_width, half_width, 1)
    slot_total = EXPERTS * CAP
    flat_ids = route_ids.reshape(-1)
    pair_count = flat_ids.shape[0]
    onehot = (flat_ids[:, None] == jnp.arange(EXPERTS, dtype=jnp.int32)[None, :]).astype(
        jnp.float32
    )
    pair_index = jnp.arange(pair_count, dtype=jnp.int32)
    earlier_mask = (pair_index[:, None] > pair_index[None, :]).astype(jnp.float32)
    before = jnp.dot(earlier_mask, onehot, precision=lax.Precision.HIGHEST)
    position = jnp.sum(before * onehot, axis=1).astype(jnp.int32)
    target = (flat_ids * CAP + position).reshape(tokens, 2)
    matches = jnp.arange(slot_total, dtype=jnp.int32)[None, :, None] == target[:, None, :]
    placement = jnp.any(matches, axis=2).astype(jnp.bfloat16)
    combine_weights = jnp.sum(jnp.where(matches, route_weight[:, None, :], 0.0), axis=2)
    members = ctx_count // EXPERTS
    outgoing = lax.dot_general(
        placement, half_feats, (((0,), (0,)), ((), ())), preferred_element_type=jnp.float32
    )
    outgoing = jnp.repeat(
        outgoing.astype(jnp.bfloat16).reshape(EXPERTS, CAP, half_width), members, axis=0
    )
    arrived = lax.all_to_all(outgoing, "ctx", split_axis=0, concat_axis=0, tiled=True)
    sources = arrived.shape[0]
    item_count = arrived.shape[1]
    flat_rows = arrived.reshape(sources * item_count, half_width)
    gate_value = jnp.dot(flat_rows, w_gate, preferred_element_type=jnp.float32)
    up_value = jnp.dot(flat_rows, w_up, preferred_element_type=jnp.float32)
    gate_value, up_value = (
        lax.psum(gate_value.astype(jnp.bfloat16), "tp").astype(jnp.float32),
        lax.psum(up_value.astype(jnp.bfloat16), "tp").astype(jnp.float32),
    )
    hidden = (jax.nn.silu(gate_value) * up_value).astype(jnp.bfloat16)
    answer = jnp.dot(hidden, w_down, preferred_element_type=jnp.float32).astype(jnp.bfloat16)
    answer = answer.reshape(sources, item_count, half_width)
    returned = lax.all_to_all(answer, "ctx", split_axis=0, concat_axis=0, tiled=True)
    reply_width = returned.shape[2]
    merged = jnp.sum(
        returned.astype(jnp.float32).reshape(EXPERTS, members, CAP, reply_width), axis=1
    )
    merged = merged.reshape(slot_total, reply_width)
    moe_rows = jnp.dot(combine_weights, merged, precision=lax.Precision.HIGHEST)
    moe_piece = lax.psum_scatter(
        moe_rows.astype(jnp.bfloat16), "exp", scatter_dimension=1, tiled=True
    ).astype(jnp.float32)
    own_stream = lax.dynamic_slice_in_dim(
        stream_wide, tp_index * half_width + exp_index * piece_width, piece_width, 1
    )
    return (own_stream + moe_piece).astype(jnp.bfloat16)


LOG2E = 1.4426950408889634
HOLD = 3.0
HOLD_B = 5.0
ORDER = 5.0
AXES = ("ctx", "exp", "tp")
f32 = jnp.float32
bf16 = jnp.bfloat16


def lanes_to_rows(store_ref, value):
    rows, width = value.shape
    count = width // 128
    for k in range(count):
        store_ref[pl.ds(k, rows, stride=count), :] = value[:, k * 128 : (k + 1) * 128]


def slots_of(ids, lanes):
    count = ids.shape[1]
    ids = ids.astype(f32)
    first, second = ids[0:1, :], ids[1:2, :]
    expert = lax.broadcasted_iota(jnp.int32, (8, count), 0).astype(f32)
    member = (jnp.where(expert == first, 1.0, 0.0) + jnp.where(expert == second, 1.0, 0.0)).astype(bf16)
    before = lax.broadcasted_iota(jnp.int32, (count, count), 0)
    token = lax.broadcasted_iota(jnp.int32, (count, count), 1)
    rank = jnp.dot(member, jnp.where(before < token, 1.0, 0.0).astype(bf16), preferred_element_type=f32)
    slot = [
        which * CAP + jnp.sum(jnp.where(expert == which, rank, 0.0), axis=0, keepdims=True) for which in (first, second)
    ]
    both = jnp.where(expert == 0, slot[0], jnp.where(expert == 1, slot[1], 0.0))
    row = lax.broadcasted_iota(jnp.int32, (count, lanes), 0)
    lane = lax.broadcasted_iota(jnp.int32, (count, lanes), 1)
    repeat = (row == lane) | (row + count == lane)
    return jnp.dot(both.astype(bf16), jnp.where(repeat, 1.0, 0.0).astype(bf16), preferred_element_type=f32)


def scan_kernel(
    b_ref, c_ref, dt_ref, conv_ref, z_ref, alog_ref, skip_ref, ids_ref,
    base_ref, cum_ref, silu_ref, rate_ref, pack_ref, step_s, in_s, z_s, alog_s,
):
    tokens, width = dt_ref.shape
    states = alog_ref.shape[0]
    g = width // 128
    lanes_to_rows(step_s, jax.nn.softplus(dt_ref[...]))
    lanes_to_rows(in_s, conv_ref[...].astype(f32))
    lanes_to_rows(z_s, z_ref[...].astype(f32))
    lanes_to_rows(alog_s, alog_ref[...])
    rate_ref[...] = -jnp.exp(alog_s[...]) * LOG2E
    skip = skip_ref[...]

    def advance(t, carry):
        state, cum = carry
        rows = pl.ds(pl.multiple_of(t * g, g), g)
        step = step_s[rows, :]
        inp = in_s[rows, :]
        drive = step * inp
        out = skip * inp
        after = []
        for n in range(states):
            now = jnp.exp2(step * rate_ref[n * g : (n + 1) * g, :]) * state[n] + b_ref[n, t] * drive
            out = out + c_ref[n, t] * now
            after.append(now)
        cum = cum + step
        base_ref[rows, :] = out
        cum_ref[rows, :] = cum
        return (tuple(after), cum)

    zero = jnp.zeros((g, 128), f32)
    state, cum = lax.fori_loop(0, tokens, advance, ((zero,) * states, zero), unroll=2)
    z = z_s[...]
    silu_ref[...] = z / (1.0 + jnp.exp(-z))
    pack_ref[...] = jnp.concatenate(list(state) + [cum, slots_of(ids_ref[...], 128)], axis=0).astype(bf16)


def spread_kernel(c_ref, base_ref, cum_ref, silu_ref, rate_ref, resid_ref, out_ref, weight_ref, near_ref, sem):
    states = c_ref.shape[0]
    g = rate_ref.shape[0] // states
    tokens = base_ref.shape[0] // g
    copy = pltpu.make_async_copy(resid_ref, near_ref, sem)
    copy.start()
    out_ref[...] = base_ref[...] * silu_ref[...]

    def one(t, _):
        rows = pl.ds(pl.multiple_of(t * g, g), g)
        cum, silu = cum_ref[rows, :], silu_ref[rows, :]
        for n in range(states):
            weight_ref[pl.ds(pl.multiple_of(t * (g * states) + n * g, g), g), :] = (
                jnp.exp2(cum * rate_ref[n * g : (n + 1) * g, :]) * (c_ref[n, t] * silu)
            )
        return 0

    lax.fori_loop(0, tokens, one, 0, unroll=2)
    copy.wait()


def correct_kernel(one_ref, two_ref, three_ref, base_ref, weight_ref, rate_ref, out_ref, gated_s):
    tokens, width = out_ref.shape
    g = width // 128
    states = rate_ref.shape[0] // g
    top = states * g

    def halves(ref):
        both = ref[...].astype(f32)
        return both[:top].reshape(states, g, 128), both[top : top + g]

    rate = rate_ref[...].reshape(states, g, 128)
    ctx = lax.axis_index("ctx")
    s1, c1 = halves(one_ref)
    s2, c2 = halves(two_ref)
    s3, c3 = halves(three_ref)
    near, near_sum = jnp.where(ctx == 2, s3, s1), jnp.where(ctx == 2, c3, c1)
    far = jnp.where(ctx == 3, s3, 0.0)
    middle = s2 + jnp.exp2(c2[None] * rate) * far
    entering = near + jnp.exp2(near_sum[None] * rate) * jnp.where(ctx >= 2, middle, 0.0)
    entering = jnp.where(ctx == 0, 0.0, entering)

    def one(t, _):
        rows = pl.ds(pl.multiple_of(t * g, g), g)
        out = base_ref[rows, :]
        for n in range(states):
            out = out + weight_ref[pl.ds(pl.multiple_of(t * (g * states) + n * g, g), g), :] * entering[n]
        gated_s[rows, :] = out
        return 0

    lax.fori_loop(0, tokens, one, 0, unroll=4)
    for k in range(g):
        out_ref[:, k * 128 : (k + 1) * 128] = gated_s[pl.ds(k, tokens, stride=g), :].astype(bf16)


def pack_kernel(own_ref, peer_ref, resid_ref, m0_ref, m1_ref, m2_ref, m3_ref):
    ctx, exp = lax.axis_index("ctx"), lax.axis_index("exp")
    width = own_ref.shape[1]
    part = m0_ref.shape[1] - 2 * width
    for p, ref in enumerate((m0_ref, m1_ref, m2_ref, m3_ref)):
        ref[:, :width] = own_ref[...]
        ref[:, width : 2 * width] = peer_ref[...]
        begin = pl.multiple_of((ctx ^ p) * 2 * part + exp * part, 128)
        ref[:, 2 * width :] = resid_ref[:, pl.ds(begin, part)]


def part_copy(source_ref, begin, held_ref, place, sem, rows=None):
    height, cols = source_ref.shape[0], held_ref.shape[1]
    first, count = rows or (0, height)
    return pltpu.make_async_copy(
        source_ref.at[pl.ds(first, count), pl.ds(begin, cols)], held_ref.at[pl.ds(place * height + first, count)], sem
    )


def wait_all(copies):
    for copy in copies:
        copy.start()
    for copy in copies:
        copy.wait()


def hold_out_kernel(own_ref, peer_ref, gate_ref, after_ref, out_ref, held_ref, sems):
    half = own_ref.shape[0]
    wait_all([
        *(
            pltpu.make_async_copy(ref, out_ref.at[pl.ds(k * half, half)], sems.at[k])
            for k, ref in enumerate((own_ref, peer_ref))
        ),
        part_copy(gate_ref, 0, held_ref, 0, sems.at[2], (0, gate_ref.shape[0] // 2)),
    ])


def after_kernel(earlier_ref, token_ref):
    token_ref[...] = jnp.zeros_like(token_ref)


def place_pair(scratch, odd, first, second):
    rows = first.shape[0]
    scratch[pl.ds(pl.multiple_of(odd * rows, rows), rows), :] = first
    scratch[pl.ds(pl.multiple_of((1 - odd) * rows, rows), rows), :] = second


def project_kernel(first_ref, second_ref, after_ref, out_ref, w_ref, held_ref, rows_s):
    place_pair(rows_s, lax.axis_index("ctx") % 2, first_ref[...], second_ref[...])
    exp = lax.axis_index("exp")
    depth = w_ref.shape[0]
    part = out_ref.shape[1] // 2
    resid = rows_s[:, depth : depth + part].astype(f32)
    feats = rows_s[:, :depth]
    for side in range(2):
        value = jnp.dot(feats, w_ref[:, side * part : (side + 1) * part], preferred_element_type=f32)
        out_ref[:, side * part : (side + 1) * part] = (value + jnp.where(exp == side, resid, 0.0)).astype(bf16)


def select_kernel(
    own_ref, peer_ref, first_ref, second_ref, after_ref, stream_first_ref, stream_second_ref, d0_ref, d1_ref, d2_ref, d3_ref, rows_s
):
    ctx = lax.axis_index("ctx")
    odd = ctx % 2
    block = stream_first_ref.shape[0]
    rows_s[...] = (own_ref[...].astype(f32) + peer_ref[...].astype(f32)).astype(bf16)
    stream_first_ref[...] = rows_s[pl.ds(pl.multiple_of(odd * block, block), block), :]
    stream_second_ref[...] = rows_s[pl.ds(pl.multiple_of((1 - odd) * block, block), block), :]
    feats = rows_s[...]
    top = first_ref.shape[0] - 16
    first, second = first_ref[top:, :].astype(f32), second_ref[top:, :].astype(f32)
    lane = lax.broadcasted_iota(jnp.int32, first.shape, 1)
    slots = jnp.where((lane >= block) == (odd == 0), second, first)
    count = d0_ref.shape[0]
    row = lax.broadcasted_iota(jnp.int32, (count, 2 * block), 0)
    lane = lax.broadcasted_iota(jnp.int32, (count, 2 * block), 1)
    late = row >= CAP
    mine = late == (lane >= block)
    want = jnp.where(late, row - CAP, row).astype(f32)
    for p, ref in enumerate((d0_ref, d1_ref, d2_ref, d3_ref)):
        base = ((ctx ^ p) * CAP).astype(f32)
        hit = mine & ((slots[8:9, :] == want + base) | (slots[9:10, :] == want + base))
        pick = jnp.where(hit, 1.0, 0.0).astype(bf16)
        ref[...] = jnp.dot(pick, feats, preferred_element_type=f32).astype(bf16)


def hold_early_kernel(gate_ref, up_ref, after_ref, token_ref, held_ref, sems):
    token_ref[...] = jnp.zeros_like(token_ref)
    rows = gate_ref.shape[0] // 2
    wait_all([part_copy(gate_ref, 0, held_ref, 0, sems.at[0], (rows, rows)), part_copy(up_ref, 0, held_ref, 1, sems.at[1])])


def hold_late_kernel(gate_ref, after_ref, held_second_ref, sem):
    wait_all([part_copy(gate_ref, held_second_ref.shape[1], held_second_ref, 0, sem)])


def gate_up(feats, held_ref, out_ref):
    depth = feats.shape[1]
    width = held_ref.shape[1]
    block = min(512, width)
    for k in range(2):
        for n in range(0, width, block):
            out_ref[:, k * width + n : k * width + n + block] = jnp.dot(
                feats, held_ref[k * depth : (k + 1) * depth, n : n + block], preferred_element_type=f32
            ).astype(bf16)


def first_half_kernel(
    a0_ref, a2_ref, a3_ref, a1_ref, b0_ref, b2_ref, b3_ref, b1_ref, gain_ref, wu_ref,
    out_ref, feats_ref, held_ref, held_second_ref, squares_s, sem,
):
    begin = held_ref.shape[1]
    copy = part_copy(wu_ref, begin, held_second_ref, 1, sem)
    copy.start()
    expert = lax.axis_index("ctx")
    tp = lax.axis_index("tp")
    here = expert // 2 == tp
    count, width = a0_ref.shape

    def put(group, near_ref, far_ref):
        rows = pl.ds(pl.multiple_of((tp ^ group) * count, count), count)
        squares = jnp.zeros((count, 1), f32)
        for side, ref in ((expert % 2, near_ref), (1 - expert % 2, far_ref)):
            cols = pl.ds(pl.multiple_of(side * width, width), width)
            wide = ref[...].astype(f32)
            squares = squares + jnp.sum(wide * wide, axis=1, keepdims=True)
            feats_ref[rows, cols] = (wide * gain_ref[:, pl.ds(pl.multiple_of(tp * 2 * width + side * width, width), width)]).astype(bf16)
        squares_s[rows, :] = jnp.broadcast_to(squares, (count, 128))

    @pl.when(here)
    def _():
        put(0, a0_ref, a1_ref)
        put(1, b0_ref, b1_ref)

    @pl.when(jnp.logical_not(here))
    def _():
        put(0, a2_ref, a3_ref)
        put(1, b2_ref, b3_ref)

    squares = squares_s[...]
    high = squares.astype(bf16).astype(f32)
    lane = lax.broadcasted_iota(jnp.int32, squares.shape, 1)
    out_ref[:, 2 * begin :] = jnp.where(lane == 0, high, jnp.where(lane == 1, squares - high, 0.0)).astype(bf16)
    gate_up(feats_ref[...], held_ref, out_ref)
    copy.wait()


def second_half_kernel(feats_ref, wd_ref, out_ref, down_ref, held_ref, sem):
    rows = wd_ref.shape[0] // 2
    copy = pltpu.make_async_copy(wd_ref.at[pl.ds(0, rows)], down_ref.at[pl.ds(0, rows)], sem)
    copy.start()
    gate_up(feats_ref[...], held_ref, out_ref)
    copy.wait()


def scale_of(own_ref, peer_ref, features):
    width = own_ref.shape[1]
    total = own_ref[:, width - 128 :].astype(f32) + peer_ref[:, width - 128 :].astype(f32)
    scale = lax.rsqrt((total[:, 0:1] + total[:, 1:2]) * (1.0 / features) + 1e-06)
    return jnp.broadcast_to(scale, total.shape)


def hidden_of(own_ref, peer_ref, scale):
    width = own_ref.shape[1] // 256 * 128
    gate = (own_ref[:, :width].astype(f32) + peer_ref[:, :width].astype(f32)) * scale
    up = (own_ref[:, width : 2 * width].astype(f32) + peer_ref[:, width : 2 * width].astype(f32)) * scale
    return (gate / (1.0 + jnp.exp(-gate)) * up).astype(bf16)


def down_first_kernel(features, own_ref, peer_ref, wd_ref, out_ref, scale_ref, held_ref, sem):
    rows = wd_ref.shape[0] // 2
    copy = pltpu.make_async_copy(wd_ref.at[pl.ds(rows, rows)], held_ref.at[pl.ds(rows, rows)], sem)
    copy.start()
    scale_ref[...] = scale_of(own_ref, peer_ref, features)
    hidden = hidden_of(own_ref, peer_ref, scale_ref[:, 0:1])
    depth = hidden.shape[1]
    block = min(512, out_ref.shape[1])
    for n in range(0, out_ref.shape[1], block):
        out_ref[:, n : n + block] = jnp.dot(hidden, held_ref[:depth, n : n + block], preferred_element_type=f32)
    copy.wait()


def down_piece(hidden, held_ref, acc_ref, out_ref, piece):
    depth = hidden.shape[1]
    width = out_ref.shape[1]
    cols = pl.ds(pl.multiple_of(piece * width, width), width)
    out_ref[...] = (acc_ref[:, cols] + jnp.dot(hidden, held_ref[depth:, cols], preferred_element_type=f32)).astype(bf16)


def down_theirs_kernel(own_ref, peer_ref, scale_ref, acc_ref, out_ref, hidden_ref, held_ref):
    hidden_ref[...] = hidden_of(own_ref, peer_ref, scale_ref[:, 0:1])
    down_piece(hidden_ref[...], held_ref, acc_ref, out_ref, 1 - lax.axis_index("exp"))


def down_mine_kernel(hidden_ref, acc_ref, out_ref, held_ref):
    down_piece(hidden_ref[...], held_ref, acc_ref, out_ref, lax.axis_index("exp"))


def reply_kernel(own_ref, peer_ref, r0_ref, r1_ref, r2_ref, r3_ref, sum_s):
    ctx = lax.axis_index("ctx")
    sum_s[...] = own_ref[...].astype(f32) + peer_ref[...].astype(f32)
    count = r0_ref.shape[0]
    for p, ref in enumerate((r0_ref, r1_ref, r2_ref, r3_ref)):
        ref[...] = sum_s[pl.ds(pl.multiple_of((ctx ^ p) * count, 8), count), :].astype(bf16)


def finish_kernel(
    s0_ref, s1_ref, s2_ref, s3_ref, pack_ref, weights_ref, r0_ref, r1_ref, r2_ref, r3_ref, out_ref
):
    ctx = lax.axis_index("ctx")
    apart = ctx ^ (lax.axis_index("tp") * lax.axis_size("exp") + lax.axis_index("exp"))
    tokens = out_ref.shape[0]
    stream = s0_ref[...]
    for p, ref in ((1, s1_ref), (2, s2_ref), (3, s3_ref)):
        stream = jnp.where(apart == p, ref[...], stream)
    slots = pack_ref[pack_ref.shape[0] - 16 :, :].astype(f32)[8:10, :tokens]
    total = stream.astype(f32)
    over_rows = (((0,), (0,)), ((), ()))
    want = lax.broadcasted_iota(jnp.int32, (r0_ref.shape[0], tokens), 0).astype(f32)
    for p, ref in enumerate((r0_ref, r1_ref, r2_ref, r3_ref)):
        base = ((ctx ^ p) * CAP).astype(f32)
        weight = jnp.zeros(want.shape, f32)
        for k in range(2):
            weight = weight + jnp.where(slots[k : k + 1, :] == want + base, weights_ref[k : k + 1, :], 0.0)
        high = weight.astype(bf16)
        low = (weight - high.astype(f32)).astype(bf16)
        rows = ref[...]
        total = total + lax.dot_general(high, rows, over_rows, preferred_element_type=f32)
        total = total + lax.dot_general(low, rows, over_rows, preferred_element_type=f32)
    out_ref[...] = total.astype(bf16)


VM = pl.BlockSpec(memory_space=pltpu.VMEM)
SM = pl.BlockSpec(memory_space=pltpu.SMEM)
HB = pl.BlockSpec(memory_space=pltpu.HBM)
AN = pl.BlockSpec(memory_space=pl.ANY)


def call(kernel, out, ins, scratch=(), args=(), limit=8, us=0.0, keep=(), show=False):
    single = not isinstance(out, tuple)
    outs = (out,) if single else out
    first, last = len(ins), len(ins) + len(keep)

    def body_kernel(*refs):
        results = refs[last : last + len(outs) + (len(keep) if show else 0)]
        kernel(*refs[:first], *results, *refs[last + len(outs) + len(keep) :])

    result = pl.pallas_call(
        body_kernel,
        out_shape=outs + tuple(pltpu.VMEM(x.shape, x.dtype) for x in keep),
        in_specs=[*ins, *[VM] * len(keep)],
        out_specs=(VM,) * (len(outs) + len(keep)),
        scratch_shapes=list(scratch),
        input_output_aliases={first + k: len(outs) + k for k in range(len(keep))},
        compiler_params=pltpu.CompilerParams(vmem_limit_bytes=limit * 1024 * 1024),
        cost_estimate=pl.CostEstimate(flops=int(us * 1.0e9), transcendentals=0, bytes_accessed=0),
    )(*args, *[in_vmem(x) for x in keep])
    return result[0] if single and not keep else result


def shape(rows, cols, kind):
    return jax.ShapeDtypeStruct((rows, cols), kind)


def in_hbm(x):
    return pltpu.with_memory_space_constraint(x, pltpu.HBM)


def in_vmem(x):
    return pltpu.with_memory_space_constraint(x, pltpu.VMEM)


def fast_body(
    resid, conv_out, gate_z, dt_raw, b_proj, c_proj, a_log, d_skip, out_weight, norm_gain,
    route_ids, route_weight, w_gate, w_up, w_down,
):
    tokens, model_width = resid.shape
    ctx_count, exp_count, tp_count = (lax.axis_size(a) for a in AXES)
    ctx = lax.axis_index("ctx")
    channels = conv_out.shape[1]
    states = a_log.shape[0]
    block_cols = out_weight.shape[1]
    half_width = model_width // tp_count
    piece_width = half_width // exp_count
    g = channels // 128

    def number(c, x, t):
        return (c * exp_count + x) * tp_count + t

    def owner(c):
        return c // (ctx_count // tp_count)

    chips = [(c, x) for c in range(ctx_count) for x in range(exp_count)]
    away = range(1, ctx_count)

    def permute(x, pairs):
        return lax.ppermute(x, AXES, pairs)

    def to_owner(x, p):
        return permute(x, [(number(c ^ p, e, owner(c)), number(c, e, owner(c))) for c, e in chips])

    def from_owner(x, p):
        return permute(x, [(number(c, e, owner(c)), number(c ^ p, e, owner(c))) for c, e in chips])

    def swap_tp(x):
        return lax.ppermute(x, "tp", [(i, tp_count - 1 - i) for i in range(tp_count)])

    with jax.named_scope("scan"):
        flat = shape(tokens * g, 128, f32)
        b_rows, c_rows = b_proj.T, c_proj.T
        base, cum, silu_z, rate, pack = call(
            scan_kernel,
            (flat, flat, flat, shape(states * g, 128, f32), shape((states + 2) * g, 128, bf16)),
            [SM, SM] + [VM] * 6,
            [pltpu.VMEM((tokens * g, 128), f32)] * 3 + [pltpu.VMEM((states * g, 128), f32)],
            tuple(in_hbm(v) for v in (b_rows, c_rows, dt_raw, conv_out, gate_z, a_log, d_skip.reshape(g, 128), route_ids.T)),
        )
    peer_weight, _ = lax.optimization_barrier((out_weight, pack))
    peer_weight = swap_tp(peer_weight)
    with jax.named_scope("relay"):
        entered = [
            permute(pack, [(number(c, x, t), number(c ^ p, x, t)) for c, x in chips for t in range(tp_count)])
            for p in away
        ]
    with jax.named_scope("spread"):
        base, spread, resid = call(
            spread_kernel, (flat, shape(tokens * states * g, 128, f32), pltpu.VMEM(resid.shape, bf16)), [SM] + [VM] * 4 + [HB],
            [pltpu.SemaphoreType.DMA], (in_hbm(c_rows), base, cum, silu_z, rate, in_hbm(resid)), us=2.0,
        )
    with jax.named_scope("correct"):
        gated = call(
            correct_kernel, shape(tokens, channels, bf16), [VM] * 6, [pltpu.VMEM((tokens * g, 128), f32)],
            (*entered, base, spread, rate),
        )
    with jax.named_scope("gather_gated"):
        peer_gated = swap_tp(gated)
    gain = norm_gain[None, :]
    with jax.named_scope("gather_gated"):
        message = shape(tokens, 2 * channels + block_cols // 2, bf16)
        messages = call(
            pack_kernel, (message,) * 4, [VM] * 3, (), (gated, peer_gated, in_vmem(resid))
        )
        blocks = [messages[0]] + [to_owner(messages[p], p) for p in away]

    token_kind = shape(8, 128, f32)
    slots_total = EXPERTS * CAP
    part_width = w_gate.shape[1] // 2
    wg, wu, wd = (in_hbm(v) for v in (w_gate, w_up, w_down))
    dma = pltpu.SemaphoreType.DMA
    held_kind = pltpu.VMEM((2 * half_width, part_width), bf16)
    with jax.named_scope("hold_out_weight"):
        held_out, held = call(
            hold_out_kernel, (pltpu.VMEM((2 * out_weight.shape[0], block_cols), bf16), held_kind), [HB, AN, HB, AN],
            [dma((3,))], (in_hbm(out_weight), peer_weight, wg, messages[0]),
        )

    def project(first, second, token, keep):
        with jax.named_scope("project"):
            return call(
                project_kernel, (shape(2 * tokens, block_cols, bf16),), [VM] * 2 + [AN],
                [pltpu.VMEM((2 * tokens, message.shape[1]), bf16)], (first, second, token), keep=keep, show=True,
            )

    def sum_exp(own):
        with jax.named_scope("sum_exp"):
            return permute(own, [(number(c, x, owner(c)), number(c, 1 - x, owner(c))) for c, x in chips])

    def select(own, peer, first, second, token, keep):
        with jax.named_scope("select"):
            block = shape(tokens, block_cols, bf16)
            routed = shape(2 * CAP, block_cols, bf16)
            return call(
                select_kernel, (block, block) + (routed,) * 4, [VM] * 4 + [AN], [pltpu.VMEM((2 * tokens, block_cols), bf16)],
                (own, peer, first, second, token), keep=keep,
            )

    def dispatch(out, order):
        with jax.named_scope("dispatch"):
            arrived = {p: from_owner(out[p], p) for p in order}
            return [out[0]] + [arrived[p] for p in away]

    own, held_out, held = project(blocks[0], blocks[1], pack, (held_out, held))
    peer = sum_exp(own)
    with jax.named_scope("hold_weights"):
        token, held = call(
            hold_early_kernel, (token_kind,), [HB, HB, AN], [dma((2,))], (wg, wu, own), us=HOLD, keep=(held,), show=True
        )
    first, second, *out, held_out, held = select(own, peer, pack, entered[0], token, (held_out, held))
    streams = [first, second]
    sent = [dispatch(out, (1,2,3))]
    token = call(after_kernel, token_kind, [AN], (), (out[0],), us=5.0)
    own, _, held = project(blocks[2], blocks[3], token, (held_out, held))
    peer = sum_exp(own)
    token = call(after_kernel, token_kind, [AN], (), (own,), us=5.0)
    first, second, *out, held = select(own, peer, entered[1], entered[2], token, (held,))
    streams += [first, second]
    sent.append(dispatch(out, (2, 3, 1)))
    with jax.named_scope("hold_weights"):
        held_second, held = call(
            hold_late_kernel, (held_kind,), [HB, AN], [dma], (wg, out[0]), us=HOLD, keep=(held,)
        )
    with jax.named_scope("gate_up"):
        first, feats, held, held_second = call(
            first_half_kernel,
            (shape(slots_total, 2 * part_width + 128, bf16), shape(slots_total, half_width, bf16)),
            [VM] * 9 + [HB], [pltpu.VMEM((slots_total, 128), f32), dma],
            (*(sent[k][p] for k in range(2) for p in (0, 2, 3, 1)), in_hbm(gain), wu), keep=(held, held_second), show=True,
        )
        peer_first = swap_tp(first)
        second, held, _ = call(
            second_half_kernel, (shape(slots_total, 2 * part_width, bf16),), [VM, HB], [dma],
            (feats, wd), keep=(held, held_second), show=True,
        )
        peer_second = swap_tp(second)
    with jax.named_scope("down"):
        acc, scale, held = call(
            functools.partial(down_first_kernel, model_width),
            (shape(slots_total, half_width, f32), shape(slots_total, 128, f32)), [VM] * 2 + [HB], [dma],
            (first, peer_first, wd), keep=(held,), show=True,
        )
        piece = shape(slots_total, piece_width, bf16)
        theirs, hidden, held = call(
            down_theirs_kernel, (piece, shape(slots_total, part_width, bf16)), [VM] * 4, (),
            (second, peer_second, scale, acc), keep=(held,), show=True,
        )
    with jax.named_scope("sum_experts"):
        peer = lax.ppermute(theirs, "exp", [(0, 1), (1, 0)])
        mine, _ = call(down_mine_kernel, (piece,), [VM] * 2, (), (hidden, acc), keep=(held,), show=True)

    def send_home(p, after):
        stream, _ = lax.optimization_barrier((streams[p], after))
        with jax.named_scope("stream_home"):
            return permute(
                stream,
                [(number(c, c % exp_count, owner(c)), number(c ^ p, c % exp_count, owner(c))) for c in range(ctx_count)],
            )

    def send(x, p):
        with jax.named_scope("reply"):
            return permute(x, [(number(c, x_at, t), number(c ^ p, x_at, t)) for c, x_at in chips for t in range(tp_count)])

    home = [send_home(p, mine) for p in away]
    with jax.named_scope("reply"):
        small = shape(CAP, piece_width, bf16)
        replies = call(
            reply_kernel, (small,) * 4, [VM] * 2, [pltpu.VMEM((slots_total, piece_width), f32)], (mine, peer)
        )
    replies = [replies[0]] + [send(replies[p], p) for p in away]
    with jax.named_scope("finish"):
        return call(
            finish_kernel, shape(tokens, piece_width, bf16), [VM] * 10, (),
            (streams[0], *home, pack, route_weight.T, *replies),
        )


def solution(mesh):
    in_specs = (
        P(("groups", "ctx"), None),
        P(("groups", "ctx"), ("exp", "tp")),
        P(("groups", "ctx"), ("exp", "tp")),
        P(("groups", "ctx"), ("exp", "tp")),
        P(("groups", "ctx"), None),
        P(("groups", "ctx"), None),
        P(None, ("exp", "tp")),
        P(("exp", "tp")),
        P(("exp", "tp"), "ctx"),
        P(),
        P(("groups", "ctx"), None),
        P(("groups", "ctx"), None),
        P("tp", ("ctx", "exp")),
        P("tp", ("ctx", "exp")),
        P(("ctx", "exp"), "tp"),
    )
    out_specs = P(("groups", "ctx"), ("tp", "exp"))
    sizes = dict(mesh.shape)
    small = (sizes["ctx"], sizes["exp"], sizes["tp"]) == (EXPERTS, 2, 2)
    chosen = fast_body if small else body
    return jax.shard_map(chosen, mesh=mesh, in_specs=in_specs, out_specs=out_specs, check_vma=False)
```

```python
import functools

import jax
import jax.numpy as jnp
from jax import lax
from jax.experimental import pallas as pl
from jax.experimental.pallas import tpu as pltpu
from jax.sharding import PartitionSpec as P

EXPERTS = 4
CAP = 40


def shifted(x, axis, by):
    peers = lax.axis_size(axis)
    pairs = [(i, i + by) for i in range(peers) if 0 <= i + by < peers]
    return lax.ppermute(x, axis, pairs)


def body(
    resid,
    conv_out,
    gate_z,
    dt_raw,
    b_proj,
    c_proj,
    a_log,
    d_skip,
    out_weight,
    norm_gain,
    route_ids,
    route_weight,
    w_gate,
    w_up,
    w_down,
):
    tokens = resid.shape[0]
    model_width = resid.shape[1]
    ctx_count = lax.axis_size("ctx")
    exp_count = lax.axis_size("exp")
    tp_count = lax.axis_size("tp")
    half_width = model_width // tp_count
    piece_width = half_width // exp_count
    tp_index = lax.axis_index("tp")
    exp_index = lax.axis_index("exp")
    stride_amount = jax.nn.softplus(dt_raw)
    rate = -jnp.exp(a_log)
    inputs = conv_out.astype(jnp.float32)

    def advance(carry_state, column):
        step_now, b_now, c_now, in_now = column
        carry_state = (
            jnp.exp(step_now[None, :] * rate) * carry_state
            + step_now[None, :] * b_now[:, None] * in_now[None, :]
        )
        return (carry_state, jnp.sum(c_now[:, None] * carry_state, axis=0))

    last_state, scanned_local = lax.scan(
        advance,
        jnp.zeros(rate.shape, jnp.float32),
        (stride_amount, b_proj, c_proj, inputs),
        unroll=8,
    )
    cum_step = jnp.cumsum(stride_amount, axis=0)
    last_decay = jnp.exp(cum_step[-1][None, :] * rate)

    def relay_turn(turn_index, carry_state):
        return shifted(last_decay * carry_state + last_state, "ctx", 1)

    entering = lax.fori_loop(0, ctx_count - 1, relay_turn, jnp.zeros_like(last_state))
    carried = jnp.exp(cum_step[:, None, :] * rate[None, :, :])
    scanned = scanned_local + jnp.sum(c_proj[:, :, None] * carried * entering[None, :, :], axis=1)
    gated_out = (
        (scanned + d_skip[None, :] * inputs) * jax.nn.silu(gate_z.astype(jnp.float32))
    ).astype(jnp.bfloat16)
    partial_value = jnp.dot(
        gated_out,
        lax.all_gather(out_weight, "ctx", axis=1, tiled=True),
        preferred_element_type=jnp.float32,
    )
    mamba_out = lax.psum(partial_value, ("exp", "tp"))
    stream = (resid.astype(jnp.float32) + mamba_out).astype(jnp.bfloat16)
    stream_wide = stream.astype(jnp.float32)
    square_mean = jnp.mean(stream_wide * stream_wide, axis=1, keepdims=True)
    normed = (stream_wide * lax.rsqrt(square_mean + 1e-06) * norm_gain[None, :]).astype(
        jnp.bfloat16
    )
    half_feats = lax.dynamic_slice_in_dim(normed, tp_index * half_width, half_width, 1)
    slot_total = EXPERTS * CAP
    flat_ids = route_ids.reshape(-1)
    pair_count = flat_ids.shape[0]
    onehot = (flat_ids[:, None] == jnp.arange(EXPERTS, dtype=jnp.int32)[None, :]).astype(
        jnp.float32
    )
    pair_index = jnp.arange(pair_count, dtype=jnp.int32)
    earlier_mask = (pair_index[:, None] > pair_index[None, :]).astype(jnp.float32)
    before = jnp.dot(earlier_mask, onehot, precision=lax.Precision.HIGHEST)
    position = jnp.sum(before * onehot, axis=1).astype(jnp.int32)
    target = (flat_ids * CAP + position).reshape(tokens, 2)
    matches = jnp.arange(slot_total, dtype=jnp.int32)[None, :, None] == target[:, None, :]
    placement = jnp.any(matches, axis=2).astype(jnp.bfloat16)
    combine_weights = jnp.sum(jnp.where(matches, route_weight[:, None, :], 0.0), axis=2)
    members = ctx_count // EXPERTS
    outgoing = lax.dot_general(
        placement, half_feats, (((0,), (0,)), ((), ())), preferred_element_type=jnp.float32
    )
    outgoing = jnp.repeat(
        outgoing.astype(jnp.bfloat16).reshape(EXPERTS, CAP, half_width), members, axis=0
    )
    arrived = lax.all_to_all(outgoing, "ctx", split_axis=0, concat_axis=0, tiled=True)
    sources = arrived.shape[0]
    item_count = arrived.shape[1]
    flat_rows = arrived.reshape(sources * item_count, half_width)
    gate_value = jnp.dot(flat_rows, w_gate, preferred_element_type=jnp.float32)
    up_value = jnp.dot(flat_rows, w_up, preferred_element_type=jnp.float32)
    gate_value, up_value = (
        lax.psum(gate_value.astype(jnp.bfloat16), "tp").astype(jnp.float32),
        lax.psum(up_value.astype(jnp.bfloat16), "tp").astype(jnp.float32),
    )
    hidden = (jax.nn.silu(gate_value) * up_value).astype(jnp.bfloat16)
    answer = jnp.dot(hidden, w_down, preferred_element_type=jnp.float32).astype(jnp.bfloat16)
    answer = answer.reshape(sources, item_count, half_width)
    returned = lax.all_to_all(answer, "ctx", split_axis=0, concat_axis=0, tiled=True)
    reply_width = returned.shape[2]
    merged = jnp.sum(
        returned.astype(jnp.float32).reshape(EXPERTS, members, CAP, reply_width), axis=1
    )
    merged = merged.reshape(slot_total, reply_width)
    moe_rows = jnp.dot(combine_weights, merged, precision=lax.Precision.HIGHEST)
    moe_piece = lax.psum_scatter(
        moe_rows.astype(jnp.bfloat16), "exp", scatter_dimension=1, tiled=True
    ).astype(jnp.float32)
    own_stream = lax.dynamic_slice_in_dim(
        stream_wide, tp_index * half_width + exp_index * piece_width, piece_width, 1
    )
    return (own_stream + moe_piece).astype(jnp.bfloat16)


LOG2E = 1.4426950408889634
HOLD = 3.0
HOLD_B = 5.0
ORDER = 5.0
AXES = ("ctx", "exp", "tp")
f32 = jnp.float32
bf16 = jnp.bfloat16


def lanes_to_rows(store_ref, value):
    rows, width = value.shape
    count = width // 128
    for k in range(count):
        store_ref[pl.ds(k, rows, stride=count), :] = value[:, k * 128 : (k + 1) * 128]


def slots_of(ids, lanes):
    count = ids.shape[1]
    ids = ids.astype(f32)
    first, second = ids[0:1, :], ids[1:2, :]
    expert = lax.broadcasted_iota(jnp.int32, (8, count), 0).astype(f32)
    member = (jnp.where(expert == first, 1.0, 0.0) + jnp.where(expert == second, 1.0, 0.0)).astype(bf16)
    before = lax.broadcasted_iota(jnp.int32, (count, count), 0)
    token = lax.broadcasted_iota(jnp.int32, (count, count), 1)
    rank = jnp.dot(member, jnp.where(before < token, 1.0, 0.0).astype(bf16), preferred_element_type=f32)
    slot = [
        which * CAP + jnp.sum(jnp.where(expert == which, rank, 0.0), axis=0, keepdims=True) for which in (first, second)
    ]
    both = jnp.where(expert == 0, slot[0], jnp.where(expert == 1, slot[1], 0.0))
    row = lax.broadcasted_iota(jnp.int32, (count, lanes), 0)
    lane = lax.broadcasted_iota(jnp.int32, (count, lanes), 1)
    repeat = (row == lane) | (row + count == lane)
    return jnp.dot(both.astype(bf16), jnp.where(repeat, 1.0, 0.0).astype(bf16), preferred_element_type=f32)


def scan_kernel(
    b_ref, c_ref, dt_ref, conv_ref, z_ref, alog_ref, skip_ref, ids_ref,
    base_ref, cum_ref, silu_ref, rate_ref, pack_ref, step_s, in_s, z_s, alog_s,
):
    tokens, width = dt_ref.shape
    states = alog_ref.shape[0]
    g = width // 128
    lanes_to_rows(step_s, jax.nn.softplus(dt_ref[...]))
    lanes_to_rows(in_s, conv_ref[...].astype(f32))
    lanes_to_rows(z_s, z_ref[...].astype(f32))
    lanes_to_rows(alog_s, alog_ref[...])
    rate_ref[...] = -jnp.exp(alog_s[...]) * LOG2E
    skip = skip_ref[...]

    def advance(t, carry):
        state, cum = carry
        rows = pl.ds(pl.multiple_of(t * g, g), g)
        step = step_s[rows, :]
        inp = in_s[rows, :]
        drive = step * inp
        out = skip * inp
        after = []
        for n in range(states):
            now = jnp.exp2(step * rate_ref[n * g : (n + 1) * g, :]) * state[n] + b_ref[n, t] * drive
            out = out + c_ref[n, t] * now
            after.append(now)
        cum = cum + step
        base_ref[rows, :] = out
        cum_ref[rows, :] = cum
        return (tuple(after), cum)

    zero = jnp.zeros((g, 128), f32)
    state, cum = lax.fori_loop(0, tokens, advance, ((zero,) * states, zero), unroll=2)
    z = z_s[...]
    silu_ref[...] = z / (1.0 + jnp.exp(-z))
    pack_ref[...] = jnp.concatenate(list(state) + [cum, slots_of(ids_ref[...], 128)], axis=0).astype(bf16)


def spread_kernel(c_ref, base_ref, cum_ref, silu_ref, rate_ref, resid_ref, out_ref, weight_ref, near_ref, sem):
    states = c_ref.shape[0]
    g = rate_ref.shape[0] // states
    tokens = base_ref.shape[0] // g
    copy = pltpu.make_async_copy(resid_ref, near_ref, sem)
    copy.start()
    out_ref[...] = base_ref[...] * silu_ref[...]

    def one(t, _):
        rows = pl.ds(pl.multiple_of(t * g, g), g)
        cum, silu = cum_ref[rows, :], silu_ref[rows, :]
        for n in range(states):
            weight_ref[pl.ds(pl.multiple_of(t * (g * states) + n * g, g), g), :] = (
                jnp.exp2(cum * rate_ref[n * g : (n + 1) * g, :]) * (c_ref[n, t] * silu)
            )
        return 0

    lax.fori_loop(0, tokens, one, 0, unroll=2)
    copy.wait()


def correct_kernel(one_ref, three_ref, two_ref, base_ref, weight_ref, rate_ref, out_ref, gated_s):
    tokens, width = out_ref.shape
    g = width // 128
    states = rate_ref.shape[0] // g
    top = states * g

    def halves(ref):
        both = ref[...].astype(f32)
        return both[:top].reshape(states, g, 128), both[top : top + g]

    rate = rate_ref[...].reshape(states, g, 128)
    ctx = lax.axis_index("ctx")
    s1, c1 = halves(one_ref)
    s2, c2 = halves(two_ref)
    s3, c3 = halves(three_ref)
    near, near_sum = jnp.where(ctx == 2, s3, s1), jnp.where(ctx == 2, c3, c1)
    far = jnp.where(ctx == 3, s3, 0.0)
    middle = s2 + jnp.exp2(c2[None] * rate) * far
    entering = near + jnp.exp2(near_sum[None] * rate) * jnp.where(ctx >= 2, middle, 0.0)
    entering = jnp.where(ctx == 0, 0.0, entering)

    def one(t, _):
        rows = pl.ds(pl.multiple_of(t * g, g), g)
        out = base_ref[rows, :]
        for n in range(states):
            out = out + weight_ref[pl.ds(pl.multiple_of(t * (g * states) + n * g, g), g), :] * entering[n]
        gated_s[rows, :] = out
        return 0

    lax.fori_loop(0, tokens, one, 0, unroll=4)
    for k in range(g):
        out_ref[:, k * 128 : (k + 1) * 128] = gated_s[pl.ds(k, tokens, stride=g), :].astype(bf16)


def pack_kernel(own_ref, peer_ref, resid_ref, m0_ref, m1_ref, m2_ref, m3_ref):
    ctx, exp = lax.axis_index("ctx"), lax.axis_index("exp")
    width = own_ref.shape[1]
    part = m0_ref.shape[1] - 2 * width
    for p, ref in enumerate((m0_ref, m1_ref, m2_ref, m3_ref)):
        ref[:, :width] = own_ref[...]
        ref[:, width : 2 * width] = peer_ref[...]
        begin = pl.multiple_of((ctx ^ p) * 2 * part + exp * part, 128)
        ref[:, 2 * width :] = resid_ref[:, pl.ds(begin, part)]


def part_copy(source_ref, begin, held_ref, place, sem, rows=None):
    height, cols = source_ref.shape[0], held_ref.shape[1]
    first, count = rows or (0, height)
    return pltpu.make_async_copy(
        source_ref.at[pl.ds(first, count), pl.ds(begin, cols)], held_ref.at[pl.ds(place * height + first, count)], sem
    )


def wait_all(copies):
    for copy in copies:
        copy.start()
    for copy in copies:
        copy.wait()


def hold_out_kernel(own_ref, peer_ref, gate_ref, after_ref, out_ref, held_ref, sems):
    half = own_ref.shape[0]
    wait_all([
        *(
            pltpu.make_async_copy(ref, out_ref.at[pl.ds(k * half, half)], sems.at[k])
            for k, ref in enumerate((own_ref, peer_ref))
        ),
        part_copy(gate_ref, 0, held_ref, 0, sems.at[2], (0, gate_ref.shape[0] // 2)),
    ])


def after_kernel(earlier_ref, token_ref):
    token_ref[...] = jnp.zeros_like(token_ref)


def place_pair(scratch, odd, first, second):
    rows = first.shape[0]
    scratch[pl.ds(pl.multiple_of(odd * rows, rows), rows), :] = first
    scratch[pl.ds(pl.multiple_of((1 - odd) * rows, rows), rows), :] = second


def project_kernel(first_ref, second_ref, after_ref, out_ref, w_ref, held_ref, rows_s):
    place_pair(rows_s, lax.axis_index("ctx") % 2, first_ref[...], second_ref[...])
    exp = lax.axis_index("exp")
    depth = w_ref.shape[0]
    part = out_ref.shape[1] // 2
    resid = rows_s[:, depth : depth + part].astype(f32)
    feats = rows_s[:, :depth]
    for side in range(2):
        value = jnp.dot(feats, w_ref[:, side * part : (side + 1) * part], preferred_element_type=f32)
        out_ref[:, side * part : (side + 1) * part] = (value + jnp.where(exp == side, resid, 0.0)).astype(bf16)


def select_kernel(
    own_ref, peer_ref, first_ref, second_ref, after_ref, stream_first_ref, stream_second_ref, d0_ref, d1_ref, d2_ref, d3_ref, rows_s
):
    ctx = lax.axis_index("ctx")
    odd = ctx % 2
    block = stream_first_ref.shape[0]
    rows_s[...] = (own_ref[...].astype(f32) + peer_ref[...].astype(f32)).astype(bf16)
    stream_first_ref[...] = rows_s[pl.ds(pl.multiple_of(odd * block, block), block), :]
    stream_second_ref[...] = rows_s[pl.ds(pl.multiple_of((1 - odd) * block, block), block), :]
    feats = rows_s[...]
    top = first_ref.shape[0] - 16
    first, second = first_ref[top:, :].astype(f32), second_ref[top:, :].astype(f32)
    lane = lax.broadcasted_iota(jnp.int32, first.shape, 1)
    slots = jnp.where((lane >= block) == (odd == 0), second, first)
    count = d0_ref.shape[0]
    row = lax.broadcasted_iota(jnp.int32, (count, 2 * block), 0)
    lane = lax.broadcasted_iota(jnp.int32, (count, 2 * block), 1)
    late = row >= CAP
    mine = late == (lane >= block)
    want = jnp.where(late, row - CAP, row).astype(f32)
    for p, ref in enumerate((d0_ref, d1_ref, d2_ref, d3_ref)):
        base = ((ctx ^ p) * CAP).astype(f32)
        hit = mine & ((slots[8:9, :] == want + base) | (slots[9:10, :] == want + base))
        pick = jnp.where(hit, 1.0, 0.0).astype(bf16)
        ref[...] = jnp.dot(pick, feats, preferred_element_type=f32).astype(bf16)


def hold_early_kernel(gate_ref, up_ref, after_ref, token_ref, held_ref, sems):
    token_ref[...] = jnp.zeros_like(token_ref)
    rows = gate_ref.shape[0] // 2
    wait_all([part_copy(gate_ref, 0, held_ref, 0, sems.at[0], (rows, rows)), part_copy(up_ref, 0, held_ref, 1, sems.at[1])])


def hold_late_kernel(gate_ref, after_ref, held_second_ref, sem):
    wait_all([part_copy(gate_ref, held_second_ref.shape[1], held_second_ref, 0, sem)])


def gate_up(feats, held_ref, out_ref):
    depth = feats.shape[1]
    width = held_ref.shape[1]
    block = min(512, width)
    for k in range(2):
        for n in range(0, width, block):
            out_ref[:, k * width + n : k * width + n + block] = jnp.dot(
                feats, held_ref[k * depth : (k + 1) * depth, n : n + block], preferred_element_type=f32
            ).astype(bf16)


def first_half_kernel(
    a0_ref, a2_ref, a3_ref, a1_ref, b0_ref, b2_ref, b3_ref, b1_ref, gain_ref, wu_ref,
    out_ref, feats_ref, held_ref, held_second_ref, squares_s, sem,
):
    begin = held_ref.shape[1]
    copy = part_copy(wu_ref, begin, held_second_ref, 1, sem)
    copy.start()
    expert = lax.axis_index("ctx")
    tp = lax.axis_index("tp")
    here = expert // 2 == tp
    count, width = a0_ref.shape

    def put(group, near_ref, far_ref):
        rows = pl.ds(pl.multiple_of((tp ^ group) * count, count), count)
        squares = jnp.zeros((count, 1), f32)
        for side, ref in ((expert % 2, near_ref), (1 - expert % 2, far_ref)):
            cols = pl.ds(pl.multiple_of(side * width, width), width)
            wide = ref[...].astype(f32)
            squares = squares + jnp.sum(wide * wide, axis=1, keepdims=True)
            feats_ref[rows, cols] = (wide * gain_ref[:, pl.ds(pl.multiple_of(tp * 2 * width + side * width, width), width)]).astype(bf16)
        squares_s[rows, :] = jnp.broadcast_to(squares, (count, 128))

    @pl.when(here)
    def _():
        put(0, a0_ref, a1_ref)
        put(1, b0_ref, b1_ref)

    @pl.when(jnp.logical_not(here))
    def _():
        put(0, a2_ref, a3_ref)
        put(1, b2_ref, b3_ref)

    squares = squares_s[...]
    high = squares.astype(bf16).astype(f32)
    lane = lax.broadcasted_iota(jnp.int32, squares.shape, 1)
    out_ref[:, 2 * begin :] = jnp.where(lane == 0, high, jnp.where(lane == 1, squares - high, 0.0)).astype(bf16)
    gate_up(feats_ref[...], held_ref, out_ref)
    copy.wait()


def second_half_kernel(feats_ref, wd_ref, out_ref, down_ref, held_ref, sem):
    rows = wd_ref.shape[0] // 2
    copy = pltpu.make_async_copy(wd_ref.at[pl.ds(0, rows)], down_ref.at[pl.ds(0, rows)], sem)
    copy.start()
    gate_up(feats_ref[...], held_ref, out_ref)
    copy.wait()


def scale_of(own_ref, peer_ref, features):
    width = own_ref.shape[1]
    total = own_ref[:, width - 128 :].astype(f32) + peer_ref[:, width - 128 :].astype(f32)
    scale = lax.rsqrt((total[:, 0:1] + total[:, 1:2]) * (1.0 / features) + 1e-06)
    return jnp.broadcast_to(scale, total.shape)


def hidden_of(own_ref, peer_ref, scale):
    width = own_ref.shape[1] // 256 * 128
    gate = (own_ref[:, :width].astype(f32) + peer_ref[:, :width].astype(f32)) * scale
    up = (own_ref[:, width : 2 * width].astype(f32) + peer_ref[:, width : 2 * width].astype(f32)) * scale
    return (gate / (1.0 + jnp.exp(-gate)) * up).astype(bf16)


def down_first_kernel(features, own_ref, peer_ref, wd_ref, out_ref, scale_ref, held_ref, sem):
    rows = wd_ref.shape[0] // 2
    copy = pltpu.make_async_copy(wd_ref.at[pl.ds(rows, rows)], held_ref.at[pl.ds(rows, rows)], sem)
    copy.start()
    scale_ref[...] = scale_of(own_ref, peer_ref, features)
    hidden = hidden_of(own_ref, peer_ref, scale_ref[:, 0:1])
    depth = hidden.shape[1]
    block = min(512, out_ref.shape[1])
    for n in range(0, out_ref.shape[1], block):
        out_ref[:, n : n + block] = jnp.dot(hidden, held_ref[:depth, n : n + block], preferred_element_type=f32)
    copy.wait()


def down_piece(hidden, held_ref, acc_ref, out_ref, piece):
    depth = hidden.shape[1]
    width = out_ref.shape[1]
    cols = pl.ds(pl.multiple_of(piece * width, width), width)
    out_ref[...] = (acc_ref[:, cols] + jnp.dot(hidden, held_ref[depth:, cols], preferred_element_type=f32)).astype(bf16)


def down_theirs_kernel(own_ref, peer_ref, scale_ref, acc_ref, out_ref, hidden_ref, held_ref):
    hidden_ref[...] = hidden_of(own_ref, peer_ref, scale_ref[:, 0:1])
    down_piece(hidden_ref[...], held_ref, acc_ref, out_ref, 1 - lax.axis_index("exp"))


def down_mine_kernel(hidden_ref, acc_ref, out_ref, held_ref):
    down_piece(hidden_ref[...], held_ref, acc_ref, out_ref, lax.axis_index("exp"))


def reply_kernel(own_ref, peer_ref, r0_ref, r1_ref, r2_ref, r3_ref, sum_s):
    ctx = lax.axis_index("ctx")
    sum_s[...] = own_ref[...].astype(f32) + peer_ref[...].astype(f32)
    count = r0_ref.shape[0]
    for p, ref in enumerate((r0_ref, r1_ref, r2_ref, r3_ref)):
        ref[...] = sum_s[pl.ds(pl.multiple_of((ctx ^ p) * count, 8), count), :].astype(bf16)


def finish_kernel(
    s0_ref, s2_ref, s3_ref, s1_ref, pack_ref, weights_ref, r0_ref, r2_ref, r3_ref, r1_ref, out_ref
):
    ctx = lax.axis_index("ctx")
    apart = ctx ^ (lax.axis_index("tp") * lax.axis_size("exp") + lax.axis_index("exp"))
    tokens = out_ref.shape[0]
    stream = s0_ref[...]
    for p, ref in ((1, s1_ref), (2, s2_ref), (3, s3_ref)):
        stream = jnp.where(apart == p, ref[...], stream)
    slots = pack_ref[pack_ref.shape[0] - 16 :, :].astype(f32)[8:10, :tokens]
    total = stream.astype(f32)
    over_rows = (((0,), (0,)), ((), ()))
    want = lax.broadcasted_iota(jnp.int32, (r0_ref.shape[0], tokens), 0).astype(f32)
    for p, ref in enumerate((r0_ref, r1_ref, r2_ref, r3_ref)):
        base = ((ctx ^ p) * CAP).astype(f32)
        weight = jnp.zeros(want.shape, f32)
        for k in range(2):
            weight = weight + jnp.where(slots[k : k + 1, :] == want + base, weights_ref[k : k + 1, :], 0.0)
        high = weight.astype(bf16)
        low = (weight - high.astype(f32)).astype(bf16)
        rows = ref[...]
        total = total + lax.dot_general(high, rows, over_rows, preferred_element_type=f32)
        total = total + lax.dot_general(low, rows, over_rows, preferred_element_type=f32)
    out_ref[...] = total.astype(bf16)


VM = pl.BlockSpec(memory_space=pltpu.VMEM)
SM = pl.BlockSpec(memory_space=pltpu.SMEM)
HB = pl.BlockSpec(memory_space=pltpu.HBM)
AN = pl.BlockSpec(memory_space=pl.ANY)


def call(kernel, out, ins, scratch=(), args=(), limit=8, us=0.0, keep=(), show=False):
    single = not isinstance(out, tuple)
    outs = (out,) if single else out
    first, last = len(ins), len(ins) + len(keep)

    def body_kernel(*refs):
        results = refs[last : last + len(outs) + (len(keep) if show else 0)]
        kernel(*refs[:first], *results, *refs[last + len(outs) + len(keep) :])

    result = pl.pallas_call(
        body_kernel,
        out_shape=outs + tuple(pltpu.VMEM(x.shape, x.dtype) for x in keep),
        in_specs=[*ins, *[VM] * len(keep)],
        out_specs=(VM,) * (len(outs) + len(keep)),
        scratch_shapes=list(scratch),
        input_output_aliases={first + k: len(outs) + k for k in range(len(keep))},
        compiler_params=pltpu.CompilerParams(vmem_limit_bytes=limit * 1024 * 1024),
        cost_estimate=pl.CostEstimate(flops=int(us * 1.0e9), transcendentals=0, bytes_accessed=0),
    )(*args, *[in_vmem(x) for x in keep])
    return result[0] if single and not keep else result


def shape(rows, cols, kind):
    return jax.ShapeDtypeStruct((rows, cols), kind)


def in_hbm(x):
    return pltpu.with_memory_space_constraint(x, pltpu.HBM)


def in_vmem(x):
    return pltpu.with_memory_space_constraint(x, pltpu.VMEM)


def fast_body(
    resid, conv_out, gate_z, dt_raw, b_proj, c_proj, a_log, d_skip, out_weight, norm_gain,
    route_ids, route_weight, w_gate, w_up, w_down,
):
    tokens, model_width = resid.shape
    ctx_count, exp_count, tp_count = (lax.axis_size(a) for a in AXES)
    ctx = lax.axis_index("ctx")
    channels = conv_out.shape[1]
    states = a_log.shape[0]
    block_cols = out_weight.shape[1]
    half_width = model_width // tp_count
    piece_width = half_width // exp_count
    g = channels // 128

    def number(c, x, t):
        return (c * exp_count + x) * tp_count + t

    def owner(c):
        return c // (ctx_count // tp_count)

    chips = [(c, x) for c in range(ctx_count) for x in range(exp_count)]
    away = range(1, ctx_count)

    def permute(x, pairs):
        return lax.ppermute(x, AXES, pairs)

    def to_owner(x, p):
        return permute(x, [(number(c ^ p, e, owner(c)), number(c, e, owner(c))) for c, e in chips])

    def from_owner(x, p):
        return permute(x, [(number(c, e, owner(c)), number(c ^ p, e, owner(c))) for c, e in chips])

    def swap_tp(x):
        return lax.ppermute(x, "tp", [(i, tp_count - 1 - i) for i in range(tp_count)])

    with jax.named_scope("scan"):
        flat = shape(tokens * g, 128, f32)
        b_rows, c_rows = b_proj.T, c_proj.T
        base, cum, silu_z, rate, pack = call(
            scan_kernel,
            (flat, flat, flat, shape(states * g, 128, f32), shape((states + 2) * g, 128, bf16)),
            [SM, SM] + [VM] * 6,
            [pltpu.VMEM((tokens * g, 128), f32)] * 3 + [pltpu.VMEM((states * g, 128), f32)],
            tuple(in_hbm(v) for v in (b_rows, c_rows, dt_raw, conv_out, gate_z, a_log, d_skip.reshape(g, 128), route_ids.T)),
        )
    peer_weight, _ = lax.optimization_barrier((out_weight, pack))
    peer_weight = swap_tp(peer_weight)
    with jax.named_scope("relay"):
        entered = [
            permute(pack, [(number(c, x, t), number(c ^ p, x, t)) for c, x in chips for t in range(tp_count)])
            for p in away
        ]
    with jax.named_scope("spread"):
        base, spread, resid = call(
            spread_kernel, (flat, shape(tokens * states * g, 128, f32), pltpu.VMEM(resid.shape, bf16)), [SM] + [VM] * 4 + [HB],
            [pltpu.SemaphoreType.DMA], (in_hbm(c_rows), base, cum, silu_z, rate, in_hbm(resid)), us=2.0,
        )
    with jax.named_scope("correct"):
        gated = call(
            correct_kernel, shape(tokens, channels, bf16), [VM] * 6, [pltpu.VMEM((tokens * g, 128), f32)],
            (entered[0], entered[2], entered[1], base, spread, rate),
        )
    with jax.named_scope("gather_gated"):
        peer_gated = swap_tp(gated)
    gain = norm_gain[None, :]
    with jax.named_scope("gather_gated"):
        message = shape(tokens, 2 * channels + block_cols // 2, bf16)
        messages = call(
            pack_kernel, (message,) * 4, [VM] * 3, (), (gated, peer_gated, in_vmem(resid))
        )
        blocks = [messages[0]] + [to_owner(messages[p], p) for p in away]

    token_kind = shape(8, 128, f32)
    slots_total = EXPERTS * CAP
    part_width = w_gate.shape[1] // 2
    wg, wu, wd = (in_hbm(v) for v in (w_gate, w_up, w_down))
    dma = pltpu.SemaphoreType.DMA
    held_kind = pltpu.VMEM((2 * half_width, part_width), bf16)
    with jax.named_scope("hold_out_weight"):
        held_out, held = call(
            hold_out_kernel, (pltpu.VMEM((2 * out_weight.shape[0], block_cols), bf16), held_kind), [HB, AN, HB, AN],
            [dma((3,))], (in_hbm(out_weight), peer_weight, wg, messages[0]),
        )

    def project(first, second, token, keep):
        with jax.named_scope("project"):
            return call(
                project_kernel, (shape(2 * tokens, block_cols, bf16),), [VM] * 2 + [AN],
                [pltpu.VMEM((2 * tokens, message.shape[1]), bf16)], (first, second, token), keep=keep, show=True,
            )

    def sum_exp(own):
        with jax.named_scope("sum_exp"):
            return permute(own, [(number(c, x, owner(c)), number(c, 1 - x, owner(c))) for c, x in chips])

    def select(own, peer, first, second, token, keep):
        with jax.named_scope("select"):
            block = shape(tokens, block_cols, bf16)
            routed = shape(2 * CAP, block_cols, bf16)
            return call(
                select_kernel, (block, block) + (routed,) * 4, [VM] * 4 + [AN], [pltpu.VMEM((2 * tokens, block_cols), bf16)],
                (own, peer, first, second, token), keep=keep,
            )

    def dispatch(out, order):
        with jax.named_scope("dispatch"):
            arrived = {p: from_owner(out[p], p) for p in order}
            return [out[0]] + [arrived[p] for p in away]

    own, held_out, held = project(blocks[0], blocks[1], pack, (held_out, held))
    peer = sum_exp(own)
    with jax.named_scope("hold_weights"):
        token, held = call(
            hold_early_kernel, (token_kind,), [HB, HB, AN], [dma((2,))], (wg, wu, own), us=HOLD, keep=(held,), show=True
        )
    first, second, *out, held_out, held = select(own, peer, pack, entered[0], token, (held_out, held))
    streams = [first, second]
    sent = [dispatch(out, (1,2,3))]
    token = call(after_kernel, token_kind, [AN], (), (out[0],), us=5.0)
    own, _, held = project(blocks[2], blocks[3], token, (held_out, held))
    peer = sum_exp(own)
    token = call(after_kernel, token_kind, [AN], (), (own,), us=5.0)
    first, second, *out, held = select(own, peer, entered[1], entered[2], token, (held,))
    streams += [first, second]
    sent.append(dispatch(out, (2, 3, 1)))
    with jax.named_scope("hold_weights"):
        held_second, held = call(
            hold_late_kernel, (held_kind,), [HB, AN], [dma], (wg, out[0]), us=HOLD, keep=(held,)
        )
    with jax.named_scope("gate_up"):
        first, feats, held, held_second = call(
            first_half_kernel,
            (shape(slots_total, 2 * part_width + 128, bf16), shape(slots_total, half_width, bf16)),
            [VM] * 9 + [HB], [pltpu.VMEM((slots_total, 128), f32), dma],
            (*(sent[k][p] for k in range(2) for p in (0, 2, 3, 1)), in_hbm(gain), wu), keep=(held, held_second), show=True,
        )
        peer_first = swap_tp(first)
        second, held, _ = call(
            second_half_kernel, (shape(slots_total, 2 * part_width, bf16),), [VM, HB], [dma],
            (feats, wd), keep=(held, held_second), show=True,
        )
        peer_second = swap_tp(second)
    with jax.named_scope("down"):
        acc, scale, held = call(
            functools.partial(down_first_kernel, model_width),
            (shape(slots_total, half_width, f32), shape(slots_total, 128, f32)), [VM] * 2 + [HB], [dma],
            (first, peer_first, wd), keep=(held,), show=True,
        )
        piece = shape(slots_total, piece_width, bf16)
        theirs, hidden, held = call(
            down_theirs_kernel, (piece, shape(slots_total, part_width, bf16)), [VM] * 4, (),
            (second, peer_second, scale, acc), keep=(held,), show=True,
        )
    with jax.named_scope("sum_experts"):
        peer = lax.ppermute(theirs, "exp", [(0, 1), (1, 0)])
        mine, _ = call(down_mine_kernel, (piece,), [VM] * 2, (), (hidden, acc), keep=(held,), show=True)

    def send_home(p, after):
        stream, _ = lax.optimization_barrier((streams[p], after))
        with jax.named_scope("stream_home"):
            return permute(
                stream,
                [(number(c, c % exp_count, owner(c)), number(c ^ p, c % exp_count, owner(c))) for c in range(ctx_count)],
            )

    def send(x, p):
        with jax.named_scope("reply"):
            return permute(x, [(number(c, x_at, t), number(c ^ p, x_at, t)) for c, x_at in chips for t in range(tp_count)])

    home = [send_home(p, mine) for p in away]
    with jax.named_scope("reply"):
        small = shape(CAP, piece_width, bf16)
        replies = call(
            reply_kernel, (small,) * 4, [VM] * 2, [pltpu.VMEM((slots_total, piece_width), f32)], (mine, peer)
        )
    replies = [replies[0]] + [send(replies[p], p) for p in away]
    with jax.named_scope("finish"):
        return call(
            finish_kernel, shape(tokens, piece_width, bf16), [VM] * 10, (),
            (streams[0], home[1], home[2], home[0], pack, route_weight.T, *(replies[p] for p in (0, 2, 3, 1))),
        )


def solution(mesh):
    in_specs = (
        P(("groups", "ctx"), None),
        P(("groups", "ctx"), ("exp", "tp")),
        P(("groups", "ctx"), ("exp", "tp")),
        P(("groups", "ctx"), ("exp", "tp")),
        P(("groups", "ctx"), None),
        P(("groups", "ctx"), None),
        P(None, ("exp", "tp")),
        P(("exp", "tp")),
        P(("exp", "tp"), "ctx"),
        P(),
        P(("groups", "ctx"), None),
        P(("groups", "ctx"), None),
        P("tp", ("ctx", "exp")),
        P("tp", ("ctx", "exp")),
        P(("ctx", "exp"), "tp"),
    )
    out_specs = P(("groups", "ctx"), ("tp", "exp"))
    sizes = dict(mesh.shape)
    small = (sizes["ctx"], sizes["exp"], sizes["tp"]) == (EXPERTS, 2, 2)
    chosen = fast_body if small else body
    return jax.shard_map(chosen, mesh=mesh, in_specs=in_specs, out_specs=out_specs, check_vma=False)
```
